32 devices in a mesh: seq: 8 (over z, y), head: 4 (over x, core).
Axes of the slice: x: 2, y: 2, z: 4, core: 2. Of those that a mesh axis runs over, the one named last changes fastest.
Arguments:
- tokens: bfloat16 [16384, 1024], P('seq', 'head'), may hold values from -6 to 6
- row_starts: int32 [4], replicated, may hold values from 0 to 16320, as said below
- attn_gain: bfloat16 [1, 1024], replicated, may hold values from 0.5 to 1.5
- query_weight: bfloat16 [1, 1024, 512], P(None, None, 'head'), may hold values from -0.1875 to 0.1875
- key_weight: bfloat16 [1, 1024, 512], P(None, None, 'head'), may hold values from -0.1875 to 0.1875
- value_weight: bfloat16 [1, 1024, 1024], P(None, None, 'head'), may hold values from -0.1875 to 0.1875
- gate_weight: bfloat16 [1, 1024, 1024], P(None, None, 'head'), may hold values from -0.1875 to 0.1875
- rank_down: bfloat16 [1, 1024, 16], replicated, may hold values from -0.1875 to 0.1875
- rank_up: bfloat16 [1, 16, 512], P(None, None, 'head'), may hold values from -1.5 to 1.5
- rank_bias: bfloat16 [1, 512], P(None, 'head'), may hold values from -1 to 11
- group_gain: bfloat16 [1, 256], replicated, may hold values from 0.5 to 1.5
- out_weight: bfloat16 [1, 1024, 1024], P(None, 'head'), may hold values from -0.1875 to 0.1875
- feed_gain: bfloat16 [1, 1024], replicated, may hold values from 0.5 to 1.5
- feed_gate: bfloat16 [1, 1024, 2816], P(None, None, 'head'), may hold values from -0.1875 to 0.1875
- feed_up: bfloat16 [1, 1024, 2816], P(None, None, 'head'), may hold values from -0.1875 to 0.1875
- feed_down: bfloat16 [1, 2816, 1024], P(None, 'head'), may hold values from -0.109375 to 0.109375
- cotangent: bfloat16 [16384, 1024], P('seq', 'head'), may hold values from -6 to 6
Outputs:
- layer_out: bfloat16 [16384, 1024], P('seq', 'head')
- grad_tokens: float32 [16384, 1024], P('seq', 'head')
- grad_attn_gain: float32 [1, 1024], P(None, 'head')
- grad_query: float32 [1, 1024, 512], P(None, None, 'head')
- grad_key: float32 [1, 1024, 512], P(None, None, 'head')
- grad_value: float32 [1, 1024, 1024], P(None, None, 'head')
- grad_gate: float32 [1, 1024, 1024], P(None, None, 'head')
- grad_rank_down: float32 [1, 1024, 16], replicated
- grad_rank_up: float32 [1, 16, 512], P(None, None, 'head')
- grad_rank_bias: float32 [1, 512], P(None, 'head')
- grad_group_gain: float32 [1, 256], replicated
- grad_out: float32 [1, 1024, 1024], P(None, 'head')
- grad_feed_gain: float32 [1, 1024], P(None, 'head')
- grad_feed_gate: float32 [1, 1024, 2816], P(None, None, 'head')
- grad_feed_up: float32 [1, 1024, 2816], P(None, None, 'head')
- grad_feed_down: float32 [1, 2816, 1024], P(None, 'head')
The draws below stay inside these ranges and needn't reach their ends.
Inputs may be any that keep to these rules, and one draw needn't show every extreme that they name: `row_starts`: increasing multiples of 64; the first is 0, the second lies within the first 2048 tokens and the third within the last 2048.
All inputs are finite; a program needn't handle non-finite values.
Results may differ from the reference program's by a relative error of at most 0.03.
Values may be sent and summed in bfloat16 or wider, within the bound.
A program may use at most 192 MiB of HBM per device.

```python
from functools import partial
import jax
import jax.numpy as jnp
from jax import lax

MODEL_WIDTH = 1024
HEADS = 4
HK = 128
HV = 256
FF = 2816
RANK = 16
SPAN = 64
LAYERS = 1
TOK_DEV = 2048
TOKENS = 16384
KD = 512
VD = 1024
N_SEQ = 8
N_HEAD = 4


def draw_row_starts(key, part):
    key = jax.random.fold_in(key, 11)
    subkeys = jax.random.split(key, 3)
    per_device = TOK_DEV // SPAN
    span_total = TOKENS // SPAN
    first_start = jax.random.randint(subkeys[0], (), 1, per_device)
    second_start = jax.random.randint(subkeys[1], (), span_total - per_device + 1, span_total - 1)
    third_start = jax.random.randint(subkeys[2], (), second_start + 1, span_total)
    starts = jnp.stack([jnp.zeros((), jnp.int32), first_start, second_start, third_start])
    return (starts * SPAN).astype(jnp.int32)


def draw_rank_bias(key, part):
    key = jax.random.fold_in(key, 23)
    subkeys = jax.random.split(key, 3)
    slow_share = 0.5
    chooser = jax.random.uniform(subkeys[0], (LAYERS, KD), jnp.float32)
    slow_level = jax.random.uniform(subkeys[1], (LAYERS, KD), jnp.float32, 8.0, 11.0)
    fast_level = jax.random.uniform(subkeys[2], (LAYERS, KD), jnp.float32, -1.0, 2.0)
    return jnp.where(chooser < slow_share, slow_level, fast_level).astype(jnp.bfloat16)


def levels(stream_key, extent, cuts, smallest, top_value):
    def one(position, shards_of):
        draws = jax.random.uniform(jax.random.fold_in(jax.random.fold_in(stream_key, 6), position), (shards_of,), jnp.float32, smallest / len(cuts), top_value / len(cuts))
        return jnp.repeat(jnp.exp(draws), extent[position] // shards_of).reshape((-1,) + (1,) * (len(extent) - position - 1))

    loudness = one(*cuts[0])
    for cut in cuts[1:]:
        loudness = loudness * one(*cut)
    return loudness


def centred(stream_key, dims, width, most, cuts=(), kind=jnp.bfloat16):
    level = levels(stream_key, dims, cuts, -0.22, 0.18) if cuts else 1.0
    values = jax.random.normal(stream_key, dims, jnp.float32) * width * level
    return jnp.minimum(jnp.maximum(values, -most), most).astype(kind)


def setup_inputs(seed: int = 0) -> dict:
    key_list = jax.random.split(jax.random.key(seed), 18)
    return {
        "tokens": centred(key_list[0], (TOKENS, MODEL_WIDTH), 1.0, 6.0, ((0, 8), (1, 4))),
        "row_starts": draw_row_starts(jax.random.fold_in(key_list[17], 71), 0),
        "attn_gain": jnp.clip(1.0 + 0.1 * jax.random.normal(key_list[2], (LAYERS, MODEL_WIDTH), jnp.float32), 0.5, 1.5).astype(jnp.bfloat16),
        "query_weight": centred(key_list[3], (LAYERS, MODEL_WIDTH, KD), MODEL_WIDTH ** -0.5, 0.1875, ((2, 4),)),
        "key_weight": centred(key_list[4], (LAYERS, MODEL_WIDTH, KD), MODEL_WIDTH ** -0.5, 0.1875, ((2, 4),)),
        "value_weight": centred(key_list[5], (LAYERS, MODEL_WIDTH, VD), MODEL_WIDTH ** -0.5, 0.1875, ((2, 4),)),
        "gate_weight": centred(key_list[6], (LAYERS, MODEL_WIDTH, VD), MODEL_WIDTH ** -0.5, 0.1875, ((2, 4),)),
        "rank_down": centred(key_list[7], (LAYERS, MODEL_WIDTH, RANK), MODEL_WIDTH ** -0.5, 0.1875),
        "rank_up": centred(key_list[8], (LAYERS, RANK, KD), RANK ** -0.5, 1.5, ((2, 4),)),
        "rank_bias": draw_rank_bias(jax.random.fold_in(key_list[17], 71), 0),
        "group_gain": jnp.clip(1.0 + 0.1 * jax.random.normal(key_list[10], (LAYERS, HV), jnp.float32), 0.5, 1.5).astype(jnp.bfloat16),
        "out_weight": centred(key_list[11], (LAYERS, VD, MODEL_WIDTH), VD ** -0.5, 0.1875, ((1, 4),)),
        "feed_gain": jnp.clip(1.0 + 0.1 * jax.random.normal(key_list[12], (LAYERS, MODEL_WIDTH), jnp.float32), 0.5, 1.5).astype(jnp.bfloat16),
        "feed_gate": centred(key_list[13], (LAYERS, MODEL_WIDTH, FF), MODEL_WIDTH ** -0.5, 0.1875, ((2, 4),)),
        "feed_up": centred(key_list[14], (LAYERS, MODEL_WIDTH, FF), MODEL_WIDTH ** -0.5, 0.1875, ((2, 4),)),
        "feed_down": centred(key_list[15], (LAYERS, FF, MODEL_WIDTH), FF ** -0.5, 0.109375, ((1, 4),)),
        "cotangent": centred(key_list[16], (TOKENS, MODEL_WIDTH), 1.0, 6.0, ((0, 8), (1, 4))),
    }


@jax.custom_vjp
def low(v):
    return lax.optimization_barrier(v.astype(jnp.bfloat16)).astype(jnp.float32)

@jax.custom_vjp
def low_back(v):
    return v

def low_keep(v):
    return (low(v), None)

def low_pass(kept, grad):
    return (grad,)

def back_keep(v):
    return (v, None)

def back_low(kept, grad):
    return (low(grad),)
low.defvjp(low_keep, low_pass)
low_back.defvjp(back_keep, back_low)
EPS = 1e-06
GATE_NORM = 16.0
EXACT_MATH = lax.Precision.HIGHEST

def product(left, right):
    return jnp.dot(left, right, precision=EXACT_MATH)

def rms_scale(values):
    return lax.rsqrt(lax.optimization_barrier(jnp.mean(values * values, axis=-1, keepdims=True)) + EPS)

def split_sum(left, right):
    feature_width = left.shape[1] // N_HEAD
    grouped = left.reshape(left.shape[0], N_HEAD, feature_width)
    pieces = right.reshape(N_HEAD, feature_width, right.shape[1])
    terms = jnp.einsum('tgk,gkd->tgd', grouped, pieces, precision=EXACT_MATH)
    return lax.optimization_barrier(jnp.sum(low(terms), axis=1))

def attend_input(params, block):
    attn_gain, query_weight, key_weight, value_weight, gate_weight, rank_down, rank_up, rank_bias = params[:8]
    rounded = low(block)
    normed = low(rounded * rms_scale(rounded) * attn_gain)
    query_raw = low_back(product(normed, query_weight))
    key_raw = low_back(product(normed, key_weight))
    reduced_value = low(low_back(product(normed, value_weight)))
    gate_raw = low_back(product(normed, gate_weight))
    low_rank = low(product(normed, rank_down))
    log_decay = jax.nn.log_sigmoid(product(low_rank, rank_up) + rank_bias) / GATE_NORM
    return (query_raw, key_raw, reduced_value, gate_raw, log_decay)

def span_step(carried, pieces):
    query_raw, key_raw, reduced_value, log_decay, reset_now = pieces
    cumul = jnp.cumsum(log_decay, axis=0)
    ending = cumul[-1]
    decayed_query = low(query_raw * HK ** (-0.5) * jnp.exp(cumul - ending))
    decayed_key = low(key_raw * jnp.exp(ending - cumul))
    causal = jnp.arange(SPAN)[None, :, None] >= jnp.arange(SPAN)[None, None, :]
    scores = jnp.einsum('thk,shk->hts', decayed_query, decayed_key, precision=EXACT_MATH)
    attn_weights = low(low_back(jnp.where(causal, scores, 0.0)))
    state_in = (1.0 - reset_now) * carried
    scaled_rows = jnp.exp(ending)[:, :, None] * state_in
    across_output = jnp.einsum('nsx,sxe->nse', decayed_query, low(scaled_rows), precision=EXACT_MATH)
    intra_out = jnp.einsum('hts,shv->thv', attn_weights, reduced_value, precision=EXACT_MATH)
    state_update = low_back(jnp.einsum('djn,djr->jnr', decayed_key, reduced_value, precision=EXACT_MATH))
    return (scaled_rows + state_update, intra_out + across_output)

def finish_layer(params, pieces):
    group_gain, out_weight, feed_gain, feed_gate, feed_up, feed_down = params[8:]
    block, core_output, gate_raw = pieces
    row_count = block.shape[0]
    core_output = low_back(core_output)
    gated = low(core_output * rms_scale(core_output) * group_gain * jax.nn.silu(gate_raw.reshape(row_count, HEADS, HV)))
    middle = block + low_back(split_sum(gated.reshape(row_count, HEADS * HV), out_weight))
    rounded = low(middle)
    normed = low(rounded * rms_scale(rounded) * feed_gain)
    gate_feed = low_back(product(normed, feed_gate))
    up_feed = low_back(product(normed, feed_up))
    hidden = low(jax.nn.silu(gate_feed) * up_feed)
    return middle + low_back(split_sum(hidden, feed_down))

def apply_layer(stream, params, resets):
    blocks = stream.reshape(N_SEQ, TOK_DEV, MODEL_WIDTH)
    query_raw, key_raw, reduced_value, gate_raw, log_decay = lax.map(jax.checkpoint(partial(attend_input, params)), blocks)
    shaped = (TOKENS // SPAN, SPAN, HEADS, HK)
    last_state, core_output = lax.scan(jax.checkpoint(span_step), jnp.zeros((HEADS, HK, HV), jnp.float32), (query_raw.reshape(shaped), key_raw.reshape(shaped), reduced_value.reshape(TOKENS // SPAN, SPAN, HEADS, HV), log_decay.reshape(shaped), resets))
    core_output = core_output.reshape(N_SEQ, TOK_DEV, HEADS, HV)
    output = lax.map(jax.checkpoint(partial(finish_layer, params)), (blocks, core_output, gate_raw))
    return output.reshape(TOKENS, MODEL_WIDTH)

def forward_pass(stream, weights, resets):
    for layer_number in range(LAYERS):
        params = tuple((member[layer_number] for member in weights))
        stream = apply_layer(stream, params, resets)
    return stream

def reference(tokens, row_starts, attn_gain, query_weight, key_weight, value_weight, gate_weight, rank_down, rank_up, rank_bias, group_gain, out_weight, feed_gain, feed_gate, feed_up, feed_down, cotangent):
    weights = tuple((member.astype(jnp.float32) for member in (attn_gain, query_weight, key_weight, value_weight, gate_weight, rank_down, rank_up, rank_bias, group_gain, out_weight, feed_gain, feed_gate, feed_up, feed_down)))
    span_ids = jnp.arange(TOKENS // SPAN, dtype=jnp.int32)
    resets = jnp.any((row_starts // SPAN).astype(jnp.int32)[None, :] == span_ids[:, None], axis=1).astype(jnp.float32)
    output, pullback = jax.vjp(partial(forward_pass, resets=resets), tokens.astype(jnp.float32), weights)
    input_gradient, grad_weights = pullback(cotangent.astype(jnp.float32))
    return (output.astype(jnp.bfloat16), input_gradient, grad_weights[0], grad_weights[1], grad_weights[2], grad_weights[3], grad_weights[4], grad_weights[5], grad_weights[6], grad_weights[7], grad_weights[8], grad_weights[9], grad_weights[10], grad_weights[11], grad_weights[12], grad_weights[13])
```

```python
import functools

import jax
import jax.numpy as jnp
from jax import lax
from jax.experimental import pallas as pl
from jax.experimental.pallas import tpu as pltpu
from jax.sharding import PartitionSpec as P

MODEL_WIDTH = 1024
HK = 128
HV = 256
SPAN = 64
RANK = 16
EPS = 1e-06
GATE_NORM = 16.0
TILE = 256
PER = TILE // SPAN
BLOCK = 256
AHEAD = 3
F32 = jnp.float32
BF16 = jnp.bfloat16
MESH = pl.DeviceIdType.MESH
VMEM_LIMIT = 60 * 1024 * 1024


def dot_nn(a, b):
    return jnp.dot(a, b, preferred_element_type=F32)


def dot_nt(a, b):
    return lax.dot_general(a, b, (((1,), (1,)), ((), ())), preferred_element_type=F32)


def dot_tn(a, b):
    return lax.dot_general(a, b, (((0,), (0,)), ((), ())), preferred_element_type=F32)


def peers():
    me = lax.axis_index("head")
    mate = me + 1 - 2 * lax.rem(me, 2)
    cross = lax.rem(me + 2, 4)
    far = cross + 1 - 2 * lax.rem(cross, 2)
    return me, mate, cross, far


def greet_head():
    _, mate, cross, far = peers()
    barrier = pltpu.get_barrier_semaphore()
    for other in (mate, cross, far):
        pl.semaphore_signal(barrier, inc=1, device_id={"head": other}, device_id_type=MESH)


def greet_seq(count):
    place = lax.axis_index("seq")
    barrier = pltpu.get_barrier_semaphore()

    def one(step, carry):
        other = lax.rem(place + step, count)
        pl.semaphore_signal(barrier, inc=1, device_id={"seq": other}, device_id_type=MESH)
        return carry

    lax.fori_loop(1, count, one, 0)


def to_head(src, dst, send, recv, other):
    return pltpu.make_async_remote_copy(
        src_ref=src, dst_ref=dst, send_sem=send, recv_sem=recv,
        device_id={"head": other}, device_id_type=MESH,
    )


def to_seq(src, dst, send, recv, other):
    return pltpu.make_async_remote_copy(
        src_ref=src, dst_ref=dst, send_sem=send, recv_sem=recv,
        device_id={"seq": other}, device_id_type=MESH,
    )


def span_masks(rows, cols):
    r = lax.broadcasted_iota(jnp.int32, (rows, cols), 0)
    c = lax.broadcasted_iota(jnp.int32, (rows, cols), 1)
    same = (r >> 6) == (c >> 6)
    return same & (r >= c), same


def three(x):
    a = x.astype(BF16)
    rest = x - a.astype(F32)
    b = rest.astype(BF16)
    c = (rest - b.astype(F32)).astype(BF16)
    return jnp.concatenate([a, b, c], axis=1)


def fold(x):
    w = x.shape[1] // 3
    return x[:, :w] + x[:, w : 2 * w] + x[:, 2 * w :]


def front_kernel(
    tiles, count,
    x_ref, c_ref, keep_ref, gain_ref, wq, wk, wv, wg, wr, rup, bias_ref,
    na_o, cg_o, inv_o, f_o, b_o, o_o, u_o, e_o, in_o, d_o,
    grid_buf, wcat, tri, state, decay, sbuf, rbuf, sems, esend, erecv,
):
    i = pl.program_id(0)
    me, mate, cross, far = peers()
    place = lax.axis_index("seq")
    total = 2 * tiles

    def own_mate(m):
        return to_head(grid_buf.at[m, me], grid_buf.at[m, me], sems.at[0, m], sems.at[1, m], mate)

    def own_cross(m):
        return to_head(grid_buf.at[m, me], grid_buf.at[m, me], sems.at[2, m], sems.at[3, m], cross)

    def onward(m):
        return to_head(grid_buf.at[m, cross], grid_buf.at[m, cross], sems.at[4, m], sems.at[5, m], mate)

    @pl.when(i == 0)
    def _():
        greet_head()
        greet_seq(count)

        def own(m, carry):
            rows = pl.ds(pl.multiple_of(m * TILE, TILE), TILE)
            grid_buf[m, me] = x_ref[rows, :]
            grid_buf[m + tiles, me] = c_ref[rows, :]
            return carry

        lax.fori_loop(0, tiles, own, 0)
        pl.semaphore_wait(pltpu.get_barrier_semaphore(), 3 + count - 1)
        for m in range(AHEAD):
            own_cross(m).start()
            own_mate(m).start()
        wcat[:, 0:128] = wq[...]
        wcat[:, 128:256] = wk[...]
        wcat[:, 256:512] = wv[...]
        wcat[:, 512:768] = wg[...]
        wcat[:, 768:896] = wr[...]
        causal, same = span_masks(TILE, TILE)
        tri[0:TILE, :] = jnp.where(causal, 1.0, 0.0).astype(BF16)
        tri[TILE : 2 * TILE, :] = jnp.where(same, 1.0, 0.0).astype(BF16)
        state[...] = jnp.zeros_like(state)
        decay[...] = jnp.ones_like(decay)

    @pl.when(i < total)
    def _():
        own_cross(i).wait_recv()
        onward(i).start()

    @pl.when(i + AHEAD < total)
    def _():
        own_cross(i + AHEAD).start()
        own_mate(i + AHEAD).start()

    @pl.when(i >= 1)
    def _():
        own_mate(i - 1).wait_recv()
        onward(i - 1).wait_recv()

    @pl.when((i >= 1) & (i <= tiles))
    def _():
        m = i - 1
        squares = jnp.zeros((TILE, 1), F32)
        for j in range(4):
            xj = grid_buf[m, j].astype(F32)
            squares = squares + jnp.sum(xj * xj, axis=1, keepdims=True)
        inv = lax.rsqrt(squares / MODEL_WIDTH + EPS)
        inv_o[...] = jnp.broadcast_to(inv, (TILE, 128))
        for j in range(4):
            cols = slice(j * BLOCK, (j + 1) * BLOCK)
            xj = grid_buf[m, j].astype(F32)
            na_o[:, cols] = (xj * inv * gain_ref[:, cols]).astype(BF16)
        proj = dot_nn(na_o[...], wcat[...])
        q = proj[:, 0:128]
        k = proj[:, 128:256]
        v = proj[:, 256:512].astype(BF16)
        o_o[:, 0:256] = proj[:, 512:768]
        lr = proj[:, 768:896].astype(BF16)
        z = dot_nn(lr, rup[...]) + bias_ref[...]
        g = (jnp.minimum(z, 0.0) - jnp.log1p(jnp.exp(-jnp.abs(z)))) / GATE_NORM
        sums = fold(dot_nn(tri[...], three(g)))
        b = sums[0:TILE]
        e = sums[TILE : 2 * TILE]
        fq = (HK ** (-0.5)) * jnp.exp(b - e)
        fk = jnp.exp(e - b)
        qf = q * fq
        kf = k * fk
        f_o[:, 0:128] = qf
        f_o[:, 128:256] = kf
        f_o[:, 256:384] = fq
        f_o[:, 384:512] = fk
        f_o[:, 512:640] = jax.nn.sigmoid(-z) / GATE_NORM
        qd = qf.astype(BF16)
        kd = kf.astype(BF16)
        causal, _ = span_masks(TILE, TILE)
        scores = jnp.where(causal, dot_nt(qd, kd), 0.0).astype(BF16)
        b_o[:, 0:256] = v
        b_o[:, 256:512] = scores
        b_o[:, 512:640] = lr
        o_o[:, 256:512] = dot_nn(scores, v)
        for c in range(PER):
            rows = slice(c * SPAN, (c + 1) * SPAN)
            update = dot_tn(v[rows], kd[rows])
            u_o[c] = update
            ee = jnp.exp(e[c * SPAN : c * SPAN + 1])
            e_o[0, c : c + 1, :] = ee
            through = keep_ref[m, c : c + 1, :] * ee
            state[...] = through * state[...] + update
            decay[...] = through * decay[...]

    @pl.when(i == tiles)
    def _():
        d_o[...] = decay[...]
        sbuf[0:HV, :] = state[...].astype(BF16)
        d = decay[...]
        hi = d.astype(BF16).astype(F32)
        first = lax.broadcasted_iota(jnp.int32, (16, 128), 0) < 8
        both = jnp.where(first, jnp.concatenate([hi, hi], axis=0), jnp.concatenate([d - hi, d - hi], axis=0))
        sbuf[HV : HV + 16, :] = both.astype(BF16)

        def send(p, carry):
            to_seq(sbuf, rbuf.at[place], esend.at[p], erecv.at[place], p).start()
            return carry

        lax.fori_loop(place + 1, count, send, 0)

    @pl.when(i > tiles)
    def _():
        m = i - 1
        for j in range(4):
            cg_o[:, j * BLOCK : (j + 1) * BLOCK] = grid_buf[m, j]

    @pl.when(i == total)
    def _():
        in_o[...] = jnp.zeros_like(in_o)

        def join(p, carry):
            to_seq(sbuf, rbuf.at[p], esend.at[p], erecv.at[p], place).wait_recv()
            got = rbuf[p].astype(F32)
            d = got[HV : HV + 1] + got[HV + 8 : HV + 9]
            in_o[...] = got[0:HV] + d * in_o[...]
            return carry

        lax.fori_loop(0, place, join, 0)

        def sent(p, carry):
            to_seq(sbuf, rbuf.at[place], esend.at[p], erecv.at[place], p).wait_send()
            return carry

        lax.fori_loop(place + 1, count, sent, 0)

        def out(m, carry):
            own_cross(m).wait_send()
            own_mate(m).wait_send()
            onward(m).wait_send()
            return carry

        lax.fori_loop(0, total, out, 0)


def whole(shape):
    zeros = (0,) * len(shape)
    return pl.BlockSpec(shape, lambda i: zeros, pipeline_mode=pl.Buffered(1))


def front(x, cot, keep, gain, wq, wk, wv, wg, wr, rup, bias):
    rows = x.shape[0]
    tiles = rows // TILE
    count = lax.axis_size("seq")

    def tile(shape, lag, axis0=True):
        rest = (0,) * (len(shape) - 1)
        return pl.BlockSpec(shape, lambda i: (jnp.clip(i - lag, 0, tiles - 1),) + rest)

    ins = (x, cot, keep, gain, wq, wk, wv, wg, wr, rup, bias)
    outs = [
        ((rows, MODEL_WIDTH), BF16, tile((TILE, MODEL_WIDTH), 1)),
        ((rows, MODEL_WIDTH), BF16, tile((TILE, MODEL_WIDTH), 1 + tiles)),
        ((rows, 128), F32, tile((TILE, 128), 1)),
        ((rows, 640), F32, tile((TILE, 640), 1)),
        ((rows, 640), BF16, tile((TILE, 640), 1)),
        ((rows, 512), F32, tile((TILE, 512), 1)),
        ((rows // SPAN, HV, HK), F32, tile((PER, HV, HK), 1)),
        ((tiles, 8, 128), F32, tile((1, 8, 128), 1)),
        ((HV, HK), F32, whole((HV, HK))),
        ((8, 128), F32, whole((8, 128))),
    ]
    return pl.pallas_call(
        functools.partial(front_kernel, tiles, count),
        grid=(2 * tiles + 1,),
        out_shape=[jax.ShapeDtypeStruct(s, d) for s, d, _ in outs],
        in_specs=[whole(a.shape) for a in ins],
        out_specs=[s for _, _, s in outs],
        scratch_shapes=[
            pltpu.VMEM((2 * tiles, 4, TILE, BLOCK), BF16),
            pltpu.VMEM((MODEL_WIDTH, 896), BF16),
            pltpu.VMEM((2 * TILE, TILE), BF16),
            pltpu.VMEM((HV, HK), F32),
            pltpu.VMEM((8, 128), F32),
            pltpu.VMEM((HV + 16, HK), BF16),
            pltpu.VMEM((count, HV + 16, HK), BF16),
            pltpu.SemaphoreType.DMA((6, 2 * tiles)),
            pltpu.SemaphoreType.DMA((count,)),
            pltpu.SemaphoreType.DMA((count,)),
        ],
        compiler_params=pltpu.CompilerParams(
            collective_id=1, has_side_effects=True, vmem_limit_bytes=VMEM_LIMIT,
            dimension_semantics=("arbitrary",),
        ),
        name="front",
    )(*ins)


EXACT_MATH = lax.Precision.HIGHEST


def carried_in(x, axis, join, neutral, backward):
    count = lax.axis_size(axis)
    place = lax.axis_index(axis)
    ahead = count - 1 - place if backward else place
    gathered = jax.tree.map(
        lambda a, kind: lax.all_gather(a.astype(kind), axis), x, (jnp.bfloat16, jnp.bfloat16)
    )
    state = jax.tree.map(lambda a, e: jnp.zeros_like(a) + jnp.asarray(e, a.dtype), x, neutral)

    def one(step, state):
        source = count - 1 - step if backward else step
        return join(
            state,
            jax.tree.map(
                lambda a, own: lax.dynamic_index_in_dim(a, source, 0, False).astype(own.dtype),
                gathered,
                x,
            ),
        )

    return lax.fori_loop(0, ahead, one, state)


def as_sent(x):
    return jax.tree.map(lambda a: a.astype(jnp.bfloat16) if a.dtype == jnp.float32 else a, x)


def matmul(left, right):
    return jnp.dot(left, right, preferred_element_type=jnp.float32)


def rows_product(left, right):
    return lax.dot_general(
        left, right, (((0,), (0,)), ((), ())), preferred_element_type=jnp.float32
    )


def cols_product(left, right):
    return lax.dot_general(
        left, right, (((1,), (1,)), ((), ())), preferred_element_type=jnp.float32
    )


def exact_rows(left, right):
    return jnp.einsum(
        "tk,tj->kj", left, right, precision=EXACT_MATH, preferred_element_type=jnp.float32
    )


def exact_cols(left, right):
    return jnp.einsum(
        "tk,jk->tj", left, right, precision=EXACT_MATH, preferred_element_type=jnp.float32
    )


def chain_state(earlier, later):
    return (earlier[0] * later[0], later[1] + later[0][..., None] * earlier[1])


def gather_features(slice_value):
    return lax.all_gather(slice_value.astype(jnp.bfloat16), "head", axis=1, tiled=True)


def reduce_partial(partial_value):
    return lax.psum_scatter(
        partial_value.astype(jnp.bfloat16), "head", scatter_dimension=1, tiled=True
    ).astype(jnp.float32)


def gather_grads(slice_grad):
    return lax.all_gather(slice_grad.astype(jnp.bfloat16), "head", axis=1, tiled=True)


def normalize(collected_rows, gain):
    values = collected_rows.astype(jnp.float32)
    inverse_norm = lax.rsqrt(jnp.mean(values * values, axis=1, keepdims=True) + EPS)
    return ((values * inverse_norm * gain).astype(jnp.bfloat16), inverse_norm)


def norm_stat(grad_normed, collected_rows, inverse_norm, gain):
    return jnp.sum(
        grad_normed * gain * (collected_rows.astype(jnp.float32) * inverse_norm),
        axis=1,
        keepdims=True,
    )


def norm_back(gradient_portion, statistic_sum, collected_rows, inverse_norm, gain, feature_width):
    column_slot = lax.axis_index("head") * feature_width
    normalized_portion = (
        lax.dynamic_slice_in_dim(collected_rows, column_slot, feature_width, 1).astype(jnp.float32)
        * inverse_norm
    )
    gain_portion = lax.dynamic_slice_in_dim(gain, column_slot, feature_width, 0)
    gain_gradient = jnp.sum(gradient_portion * normalized_portion, axis=0)
    input_gradient = inverse_norm * (
        gain_portion * gradient_portion - normalized_portion * statistic_sum / MODEL_WIDTH
    )
    return (input_gradient, gain_gradient)


def core_forward(f, bb, o, u, ee, inc, decay, reduced_value, resets, keep_before, causal):
    spans = u.shape[0]
    shape = (spans, SPAN, 1, HK)
    qf = f[:, 0:128].reshape(shape)
    kf = f[:, 128:256].reshape(shape)
    fq = f[:, 256:384].reshape(shape)
    fk = f[:, 384:512].reshape(shape)
    blocks = bb[:, 256:512].reshape(spans // PER, PER, SPAN, PER, SPAN)
    attn_weights = jnp.stack([blocks[:, c, :, c, :] for c in range(PER)], axis=1).reshape(spans, 1, SPAN, SPAN)
    state_update = jnp.swapaxes(u, 1, 2)[:, None]
    decay_end = ee[:, 0:PER].reshape(spans, 1, HK)

    def forward_step(carried, pieces):
        reset_now, decay_now, update_now = pieces
        state_in = (1.0 - reset_now) * carried
        return (decay_now[..., None] * state_in + update_now, state_in)

    _, states_in = lax.scan(forward_step, inc.T[None], (resets, decay_end, state_update))
    scaled_rows = decay_end[..., None] * states_in
    state_low = scaled_rows.astype(jnp.bfloat16)
    decayed_query = qf.astype(jnp.bfloat16)
    decayed_key = kf.astype(jnp.bfloat16)
    across_output = jnp.einsum(
        "cthk,chkv->cthv", decayed_query, state_low, preferred_element_type=jnp.float32
    )
    intra_out = o[:, 256:512].reshape(spans, SPAN, 1, HV)
    kept = (qf, kf, fq, fk, decayed_query, decayed_key, attn_weights, reduced_value, decay_end, scaled_rows, state_low, decay)
    return (intra_out + across_output, kept)


def core_backward(grad_core, kept_core, resets, keep_after, causal):
    (
        qf,
        kf,
        fq,
        fk,
        decayed_query,
        decayed_key,
        attn_weights,
        reduced_value,
        decay_end,
        scaled_rows,
        state_low,
        device_decay,
    ) = kept_core
    ending = jnp.log(decay_end)
    grad_attn = jnp.einsum(
        "cthv,cshv->chts", grad_core, reduced_value, preferred_element_type=jnp.float32
    )
    grad_scores = jnp.where(causal, grad_attn, 0.0).astype(jnp.bfloat16)
    grad_value = jnp.einsum(
        "chts,cthv->cshv", attn_weights, grad_core, preferred_element_type=jnp.float32
    )
    grad_state_low = jnp.einsum(
        "cthk,cthv->chkv", decayed_query, grad_core, preferred_element_type=jnp.float32
    )
    grad_query_dec = jnp.einsum(
        "chts,cshk->cthk", grad_scores, decayed_key, preferred_element_type=jnp.float32
    )
    grad_query_dec = grad_query_dec + jnp.einsum(
        "cthv,chkv->cthk", grad_core, state_low, preferred_element_type=jnp.float32
    )
    grad_key_dec = jnp.einsum(
        "chts,cthk->cshk", grad_scores, decayed_query, preferred_element_type=jnp.float32
    )

    def backward_step(carried, pieces):
        reset_now, decay_now, grad_now = pieces
        grad_state_in = decay_now[..., None] * (grad_now + carried)
        return ((1.0 - reset_now) * grad_state_in, carried)

    first_local, grad_out_local = lax.scan(
        backward_step,
        jnp.zeros(grad_state_low.shape[1:], jnp.float32),
        (resets, decay_end, grad_state_low),
        reverse=True,
    )
    outgoing = carried_in(
        (device_decay, first_local),
        "seq",
        chain_state,
        (jnp.ones_like(device_decay), jnp.zeros_like(first_local)),
        True,
    )[1]
    following = keep_after[:, None, None] * jnp.exp(
        jnp.sum(ending, axis=0) - jnp.cumsum(ending, axis=0)
    )
    grad_state_out = grad_out_local + following[..., None] * outgoing[None]
    grad_scaled = grad_state_low + grad_state_out
    grad_update = grad_state_out.astype(jnp.bfloat16)
    grad_key_dec = grad_key_dec + jnp.einsum(
        "chkv,cshv->cshk", grad_update, reduced_value, preferred_element_type=jnp.float32
    )
    grad_value = grad_value + jnp.einsum(
        "cshk,chkv->cshv", decayed_key, grad_update, preferred_element_type=jnp.float32
    )
    query_term = grad_query_dec * qf
    key_term = grad_key_dec * kf
    extra_term = jnp.sum(key_term - query_term, axis=1) + jnp.sum(grad_scaled * scaled_rows, axis=3)
    local_term = query_term - key_term
    grad_log_decay = jnp.flip(jnp.cumsum(jnp.flip(local_term, 1), axis=1), 1) + extra_term[:, None]
    grad_query = grad_query_dec * fq
    grad_key = grad_key_dec * fk
    return (grad_query, grad_key, grad_value, grad_log_decay)


def shards(
    tokens,
    row_starts,
    attn_gain,
    query_weight,
    key_weight,
    value_weight,
    gate_weight,
    rank_down,
    rank_up,
    rank_bias,
    group_gain,
    out_weight,
    feed_gain,
    feed_gate,
    feed_up,
    feed_down,
    cotangent,
):
    rows_local = tokens.shape[0]
    slice_width = tokens.shape[1]
    heads_local = query_weight.shape[2] // HK
    head_count = lax.axis_size("head")
    spans = rows_local // SPAN
    span_ids = lax.axis_index("seq") * spans + jnp.arange(spans, dtype=jnp.int32)
    resets = jnp.any((row_starts // SPAN)[None, :] == span_ids[:, None], axis=1).astype(jnp.float32)
    keep_before = jnp.cumprod(1.0 - resets)
    keep_after = jnp.concatenate(
        [jnp.cumprod((1.0 - resets)[::-1])[::-1][1:], jnp.ones((1,), jnp.float32)]
    )
    causal = jnp.arange(SPAN)[:, None] >= jnp.arange(SPAN)[None, :]
    key_shape = (spans, SPAN, heads_local, HK)
    value_shape = (spans, SPAN, heads_local, HV)
    residual = tokens.astype(jnp.float32)
    layer_number = 0
    tiles = rows_local // TILE
    keep_tiles = jnp.zeros((tiles, 8, 128), jnp.float32).at[:, 0:PER].set(
        jnp.broadcast_to((1.0 - resets).reshape(tiles, PER, 1), (tiles, PER, 128))
    )
    rank_wide = jnp.pad(rank_down[0], ((0, 0), (0, 128 - RANK)))
    rank_tall = jnp.pad(rank_up[0], ((0, 128 - RANK), (0, 0)))
    normed_attn, grad_full, inverse_wide, f, bb, o, u, ee, inc, dec = front(
        tokens, cotangent, keep_tiles, attn_gain.astype(jnp.float32), query_weight[0], key_weight[0],
        value_weight[0], gate_weight[0], rank_wide, rank_tall, rank_bias.astype(jnp.float32),
    )
    inverse_attn = inverse_wide[:, 0:1]
    low_rank = bb[:, 512:512 + RANK]
    reduced_value = bb[:, 0:256]
    gate_raw = o[:, 0:256]
    gathered_attn = gather_features(residual)
    core_output, kept_core = core_forward(
        f, bb, o, u, ee, inc, dec[0:1], reduced_value.reshape(value_shape), resets, keep_before, causal
    )
    gate_logit = None
    core_output = core_output.reshape(rows_local, heads_local, HV)
    group_inverse_norm = lax.rsqrt(jnp.mean(core_output * core_output, axis=2, keepdims=True) + EPS)
    group_normalized = core_output * group_inverse_norm
    gate_activations = gate_raw.reshape(rows_local, heads_local, HV)
    common_gain = group_gain[layer_number].astype(jnp.float32)
    gated_low = (
        (group_normalized * common_gain * jax.nn.silu(gate_activations))
        .astype(jnp.bfloat16)
        .reshape(rows_local, heads_local * HV)
    )
    middle = residual + reduce_partial(matmul(gated_low, out_weight[layer_number]))
    gathered_feed = gather_features(middle)
    normed_feed, inverse_feed = normalize(
        gathered_feed, feed_gain[layer_number].astype(jnp.float32)
    )
    gate_feed = matmul(normed_feed, feed_gate[layer_number])
    up_feed = matmul(normed_feed, feed_up[layer_number])
    hidden_feed = (jax.nn.silu(gate_feed) * up_feed).astype(jnp.bfloat16)
    residual = middle + reduce_partial(matmul(hidden_feed, feed_down[layer_number]))
    memory = [
        (
            gathered_attn,
            normed_attn,
            inverse_attn,
            low_rank,
            gate_logit,
            kept_core,
            group_inverse_norm,
            group_normalized,
            gate_activations,
            gated_low,
            gathered_feed,
            normed_feed,
            inverse_feed,
            gate_feed,
            up_feed,
            hidden_feed,
        )
    ]
    layer_out = residual.astype(jnp.bfloat16)
    grad_stream = cotangent.astype(jnp.float32)
    layer_grads = []
    layer_number = 0
    (
        gathered_attn,
        normed_attn,
        inverse_attn,
        low_rank,
        gate_logit,
        kept_core,
        group_inverse_norm,
        group_normalized,
        gate_activations,
        gated_low,
        gathered_feed,
        normed_feed,
        inverse_feed,
        gate_feed,
        up_feed,
        hidden_feed,
    ) = memory[layer_number]
    grad_feed_down = rows_product(hidden_feed, grad_full)
    grad_hidden = cols_product(grad_full, feed_down[layer_number])
    sigma_feed = jax.nn.sigmoid(gate_feed)
    grad_up_feed = (grad_hidden * gate_feed * sigma_feed).astype(jnp.bfloat16)
    grad_gate_feed = (
        grad_hidden * up_feed * sigma_feed * (1.0 + gate_feed * (1.0 - sigma_feed))
    ).astype(jnp.bfloat16)
    grad_feed_gate = rows_product(normed_feed, grad_gate_feed)
    grad_feed_up = rows_product(normed_feed, grad_up_feed)
    grad_normed_feed = cols_product(grad_gate_feed, feed_gate[layer_number]) + cols_product(
        grad_up_feed, feed_up[layer_number]
    )
    gain_feed = feed_gain[layer_number].astype(jnp.float32)
    stat_feed = norm_stat(grad_normed_feed, gathered_feed, inverse_feed, gain_feed)
    slice_feed = lax.psum_scatter(
        grad_normed_feed.astype(jnp.bfloat16), "head", scatter_dimension=1, tiled=True
    ).astype(jnp.float32)
    total_feed = lax.psum_scatter(
        jnp.tile(stat_feed, (1, head_count)).astype(jnp.bfloat16),
        "head",
        scatter_dimension=1,
        tiled=True,
    ).astype(jnp.float32)
    grad_middle_norm, grad_feed_gain = norm_back(
        slice_feed, total_feed, gathered_feed, inverse_feed, gain_feed, slice_width
    )
    grad_middle = grad_stream + grad_middle_norm
    feed_grads = (grad_feed_gain, grad_feed_gate, grad_feed_up, grad_feed_down)
    grad_mid_full = gather_grads(grad_middle)
    grad_out = rows_product(gated_low, grad_mid_full)
    grad_gated = cols_product(grad_mid_full, out_weight[layer_number]).reshape(
        rows_local, heads_local, HV
    )
    common_gain = group_gain[layer_number].astype(jnp.float32)
    sigma_gate = jax.nn.sigmoid(gate_activations)
    normed_core_gradient = grad_gated * gate_activations * sigma_gate
    grad_gate_values = (
        (
            grad_gated
            * group_normalized
            * common_gain
            * sigma_gate
            * (1.0 + gate_activations * (1.0 - sigma_gate))
        )
        .astype(jnp.bfloat16)
        .reshape(rows_local, heads_local * HV)
    )
    shared_gradient = jnp.sum(normed_core_gradient * group_normalized, axis=(0, 1))
    inside_term = normed_core_gradient * common_gain
    grad_core = group_inverse_norm * (
        inside_term
        - group_normalized * jnp.mean(inside_term * group_normalized, axis=2, keepdims=True)
    )
    grad_query_raw, grad_key_raw, grad_value_raw, grad_log_decay = core_backward(
        grad_core.astype(jnp.bfloat16).reshape(value_shape), kept_core, resets, keep_after, causal
    )
    grad_query_low = grad_query_raw.reshape(rows_local, heads_local * HK).astype(jnp.bfloat16)
    grad_key_low = grad_key_raw.reshape(rows_local, heads_local * HK).astype(jnp.bfloat16)
    grad_value_low = grad_value_raw.reshape(rows_local, heads_local * HV).astype(jnp.bfloat16)
    grad_logit = (
        grad_log_decay.reshape(rows_local, heads_local * HK) * f[:, 512:640]
    )
    grad_rank_up = exact_rows(low_rank, grad_logit)
    grad_rank_bias = jnp.sum(grad_logit, axis=0)
    grad_low = exact_cols(grad_logit, rank_up[layer_number])
    grad_query = rows_product(normed_attn, grad_query_low)
    grad_key = rows_product(normed_attn, grad_key_low)
    grad_value = rows_product(normed_attn, grad_value_low)
    grad_gate = rows_product(normed_attn, grad_gate_values)
    grad_normed_attn = cols_product(grad_query_low, query_weight[layer_number]) + cols_product(
        grad_key_low, key_weight[layer_number]
    )
    grad_normed_attn = (
        grad_normed_attn
        + cols_product(grad_value_low, value_weight[layer_number])
        + cols_product(grad_gate_values, gate_weight[layer_number])
    )
    grad_normed_attn = grad_normed_attn + exact_cols(grad_low, rank_down[layer_number])
    gain_attn = attn_gain[layer_number].astype(jnp.float32)
    stat_attn = norm_stat(grad_normed_attn, gathered_attn, inverse_attn, gain_attn)
    slice_attn = lax.psum_scatter(
        grad_normed_attn.astype(jnp.bfloat16), "head", scatter_dimension=1, tiled=True
    ).astype(jnp.float32)
    total_attn = lax.psum_scatter(
        jnp.tile(stat_attn, (1, head_count)).astype(jnp.bfloat16),
        "head",
        scatter_dimension=1,
        tiled=True,
    ).astype(jnp.float32)
    low_total = lax.psum_scatter(
        jnp.tile(grad_low, (1, head_count)).astype(jnp.bfloat16),
        "head",
        scatter_dimension=1,
        tiled=True,
    ).astype(jnp.float32)
    shared_total = lax.psum_scatter(
        jnp.tile(shared_gradient[None, :], (1, head_count)).astype(jnp.bfloat16),
        "head",
        scatter_dimension=1,
        tiled=True,
    ).astype(jnp.float32)
    grad_rank_down = exact_rows(normed_attn, low_total)
    grad_input_norm, grad_attn_gain = norm_back(
        slice_attn, total_attn, gathered_attn, inverse_attn, gain_attn, slice_width
    )
    grad_stream = grad_middle + grad_input_norm
    attn_grads = (
        grad_attn_gain,
        grad_query,
        grad_key,
        grad_value,
        grad_gate,
        grad_rank_down,
        grad_rank_up,
        grad_rank_bias,
        shared_total[0],
        grad_out,
    )
    layer_grads.insert(0, tuple(attn_grads) + tuple(feed_grads))
    stacked = tuple((jnp.stack([layer_grads[0][member]]) for member in range(14)))
    stacked = jax.tree.map(lambda part: part.astype(jnp.float32), lax.psum(as_sent(stacked), "seq"))
    return (layer_out, grad_stream) + tuple(stacked)


def solution(mesh):
    placed = (
        P("seq", "head"),
        P(),
        P(),
        P(None, None, "head"),
        P(None, None, "head"),
        P(None, None, "head"),
        P(None, None, "head"),
        P(),
        P(None, None, "head"),
        P(None, "head"),
        P(),
        P(None, "head", None),
        P(),
        P(None, None, "head"),
        P(None, None, "head"),
        P(None, "head", None),
        P("seq", "head"),
    )
    return jax.shard_map(
        shards,
        mesh=mesh,
        in_specs=placed,
        out_specs=(
            P("seq", "head"),
            P("seq", "head"),
            P(None, "head"),
            P(None, None, "head"),
            P(None, None, "head"),
            P(None, None, "head"),
            P(None, None, "head"),
            P(),
            P(None, None, "head"),
            P(None, "head"),
            P(),
            P(None, "head", None),
            P(None, "head"),
            P(None, None, "head"),
            P(None, None, "head"),
            P(None, "head", None),
        ),
        check_vma=False,
    )
```

```python
import functools

import jax
import jax.numpy as jnp
from jax import lax
from jax.experimental import pallas as pl
from jax.experimental.pallas import tpu as pltpu
from jax.sharding import PartitionSpec as P

MODEL_WIDTH = 1024
HK = 128
HV = 256
SPAN = 64
RANK = 16
EPS = 1e-06
GATE_NORM = 16.0
TILE = 256
PER = TILE // SPAN
BLOCK = 256
AHEAD = 3
F32 = jnp.float32
BF16 = jnp.bfloat16
MESH = pl.DeviceIdType.MESH
VMEM_LIMIT = 60 * 1024 * 1024


def dot_nn(a, b):
    return jnp.dot(a, b, preferred_element_type=F32)


def dot_nt(a, b):
    return lax.dot_general(a, b, (((1,), (1,)), ((), ())), preferred_element_type=F32)


def dot_tn(a, b):
    return lax.dot_general(a, b, (((0,), (0,)), ((), ())), preferred_element_type=F32)


def peers():
    me = lax.axis_index("head")
    mate = me + 1 - 2 * lax.rem(me, 2)
    cross = lax.rem(me + 2, 4)
    far = cross + 1 - 2 * lax.rem(cross, 2)
    return me, mate, cross, far


def greet_head():
    _, mate, cross, far = peers()
    barrier = pltpu.get_barrier_semaphore()
    for other in (mate, cross, far):
        pl.semaphore_signal(barrier, inc=1, device_id={"head": other}, device_id_type=MESH)


def greet_seq(count):
    place = lax.axis_index("seq")
    barrier = pltpu.get_barrier_semaphore()

    def one(step, carry):
        other = lax.rem(place + step, count)
        pl.semaphore_signal(barrier, inc=1, device_id={"seq": other}, device_id_type=MESH)
        return carry

    lax.fori_loop(1, count, one, 0)


def to_head(src, dst, send, recv, other):
    return pltpu.make_async_remote_copy(
        src_ref=src, dst_ref=dst, send_sem=send, recv_sem=recv,
        device_id={"head": other}, device_id_type=MESH,
    )


def to_seq(src, dst, send, recv, other):
    return pltpu.make_async_remote_copy(
        src_ref=src, dst_ref=dst, send_sem=send, recv_sem=recv,
        device_id={"seq": other}, device_id_type=MESH,
    )


def span_masks(rows, cols):
    r = lax.broadcasted_iota(jnp.int32, (rows, cols), 0)
    c = lax.broadcasted_iota(jnp.int32, (rows, cols), 1)
    same = (r >> 6) == (c >> 6)
    return same & (r >= c), same


def three(x):
    a = x.astype(BF16)
    rest = x - a.astype(F32)
    b = rest.astype(BF16)
    c = (rest - b.astype(F32)).astype(BF16)
    return jnp.concatenate([a, b, c], axis=1)


def fold(x):
    w = x.shape[1] // 3
    return x[:, :w] + x[:, w : 2 * w] + x[:, 2 * w :]


def front_kernel(
    tiles, count,
    x_ref, c_ref, keep_ref, gain_ref, wq, wk, wv, wg, wr, rup, bias_ref,
    na_o, cg_o, inv_o, f_o, b_o, o_o, u_o, e_o, in_o, d_o,
    grid_buf, wcat, tri, state, decay, sbuf, rbuf, sems, esend, erecv,
):
    i = pl.program_id(0)
    me, mate, cross, far = peers()
    place = lax.axis_index("seq")
    total = 2 * tiles

    def own_mate(m):
        return to_head(grid_buf.at[m, me], grid_buf.at[m, me], sems.at[0, m], sems.at[1, m], mate)

    def own_cross(m):
        return to_head(grid_buf.at[m, me], grid_buf.at[m, me], sems.at[2, m], sems.at[3, m], cross)

    def onward(m):
        return to_head(grid_buf.at[m, cross], grid_buf.at[m, cross], sems.at[4, m], sems.at[5, m], mate)

    @pl.when(i == 0)
    def _():
        greet_head()
        greet_seq(count)

        def own(m, carry):
            rows = pl.ds(pl.multiple_of(m * TILE, TILE), TILE)
            grid_buf[m, me] = x_ref[rows, :]
            grid_buf[m + tiles, me] = c_ref[rows, :]
            return carry

        lax.fori_loop(0, tiles, own, 0)
        pl.semaphore_wait(pltpu.get_barrier_semaphore(), 3 + count - 1)
        for m in range(AHEAD):
            own_cross(m).start()
            own_mate(m).start()
        wcat[:, 0:128] = wq[...]
        wcat[:, 128:256] = wk[...]
        wcat[:, 256:512] = wv[...]
        wcat[:, 512:768] = wg[...]
        wcat[:, 768:896] = wr[...]
        causal, same = span_masks(TILE, TILE)
        tri[0:TILE, :] = jnp.where(causal, 1.0, 0.0).astype(BF16)
        tri[TILE : 2 * TILE, :] = jnp.where(same, 1.0, 0.0).astype(BF16)
        state[...] = jnp.zeros_like(state)
        decay[...] = jnp.ones_like(decay)

    @pl.when(i < total)
    def _():
        own_cross(i).wait_recv()
        onward(i).start()

    @pl.when(i + AHEAD < total)
    def _():
        own_cross(i + AHEAD).start()
        own_mate(i + AHEAD).start()

    @pl.when(i >= 1)
    def _():
        own_mate(i - 1).wait_recv()
        onward(i - 1).wait_recv()

    @pl.when((i >= 1) & (i <= tiles))
    def _():
        m = i - 1
        squares = jnp.zeros((TILE, 1), F32)
        for j in range(4):
            xj = grid_buf[m, j].astype(F32)
            squares = squares + jnp.sum(xj * xj, axis=1, keepdims=True)
        inv = lax.rsqrt(squares / MODEL_WIDTH + EPS)
        inv_o[...] = jnp.broadcast_to(inv, (TILE, 128))
        for j in range(4):
            cols = slice(j * BLOCK, (j + 1) * BLOCK)
            xj = grid_buf[m, j].astype(F32)
            na_o[:, cols] = (xj * inv * gain_ref[:, cols]).astype(BF16)
        proj = dot_nn(na_o[...], wcat[...])
        q = proj[:, 0:128]
        k = proj[:, 128:256]
        v = proj[:, 256:512].astype(BF16)
        o_o[:, 0:256] = proj[:, 512:768]
        lr = proj[:, 768:896].astype(BF16)
        z = dot_nn(lr, rup[...]) + bias_ref[...]
        g = (jnp.minimum(z, 0.0) - jnp.log1p(jnp.exp(-jnp.abs(z)))) / GATE_NORM
        sums = fold(dot_nn(tri[...], three(g)))
        b = sums[0:TILE]
        e = sums[TILE : 2 * TILE]
        fq = (HK ** (-0.5)) * jnp.exp(b - e)
        fk = jnp.exp(e - b)
        qf = q * fq
        kf = k * fk
        f_o[:, 0:128] = qf
        f_o[:, 128:256] = kf
        f_o[:, 256:384] = fq
        f_o[:, 384:512] = fk
        f_o[:, 512:640] = jax.nn.sigmoid(-z) / GATE_NORM
        qd = qf.astype(BF16)
        kd = kf.astype(BF16)
        causal, _ = span_masks(TILE, TILE)
        scores = jnp.where(causal, dot_nt(qd, kd), 0.0).astype(BF16)
        b_o[:, 0:256] = v
        b_o[:, 256:512] = scores
        b_o[:, 512:640] = lr
        o_o[:, 256:512] = dot_nn(scores, v)
        for c in range(PER):
            rows = slice(c * SPAN, (c + 1) * SPAN)
            update = dot_tn(v[rows], kd[rows])
            u_o[c] = update
            ee = jnp.exp(e[c * SPAN : c * SPAN + 1])
            e_o[0, c : c + 1, :] = ee
            through = keep_ref[m, c : c + 1, :] * ee
            state[...] = through * state[...] + update
            decay[...] = through * decay[...]

    @pl.when(i == tiles)
    def _():
        d_o[...] = decay[...]
        sbuf[0:HV, :] = state[...].astype(BF16)
        d = decay[...]
        hi = d.astype(BF16).astype(F32)
        first = lax.broadcasted_iota(jnp.int32, (16, 128), 0) < 8
        both = jnp.where(first, jnp.concatenate([hi, hi], axis=0), jnp.concatenate([d - hi, d - hi], axis=0))
        sbuf[HV : HV + 16, :] = both.astype(BF16)

        def send(p, carry):
            to_seq(sbuf, rbuf.at[place], esend.at[p], erecv.at[place], p).start()
            return carry

        lax.fori_loop(place + 1, count, send, 0)

    @pl.when(i > tiles)
    def _():
        m = i - 1
        for j in range(4):
            cg_o[:, j * BLOCK : (j + 1) * BLOCK] = grid_buf[m, j]

    @pl.when(i == total)
    def _():
        in_o[...] = jnp.zeros_like(in_o)

        def join(p, carry):
            to_seq(sbuf, rbuf.at[p], esend.at[p], erecv.at[p], place).wait_recv()
            got = rbuf[p].astype(F32)
            d = got[HV : HV + 1] + got[HV + 8 : HV + 9]
            in_o[...] = got[0:HV] + d * in_o[...]
            return carry

        lax.fori_loop(0, place, join, 0)

        def sent(p, carry):
            to_seq(sbuf, rbuf.at[place], esend.at[p], erecv.at[place], p).wait_send()
            return carry

        lax.fori_loop(place + 1, count, sent, 0)

        def out(m, carry):
            own_cross(m).wait_send()
            own_mate(m).wait_send()
            onward(m).wait_send()
            return carry

        lax.fori_loop(0, total, out, 0)


def whole(shape):
    zeros = (0,) * len(shape)
    return pl.BlockSpec(shape, lambda i: zeros, pipeline_mode=pl.Buffered(1))


def front(x, cot, keep, gain, wq, wk, wv, wg, wr, rup, bias):
    rows = x.shape[0]
    tiles = rows // TILE
    count = lax.axis_size("seq")

    def tile(shape, lag, axis0=True):
        rest = (0,) * (len(shape) - 1)
        return pl.BlockSpec(shape, lambda i: (jnp.clip(i - lag, 0, tiles - 1),) + rest)

    ins = (x, cot, keep, gain, wq, wk, wv, wg, wr, rup, bias)
    outs = [
        ((rows, MODEL_WIDTH), BF16, tile((TILE, MODEL_WIDTH), 1)),
        ((rows, MODEL_WIDTH), BF16, tile((TILE, MODEL_WIDTH), 1 + tiles)),
        ((rows, 128), F32, tile((TILE, 128), 1)),
        ((rows, 640), F32, tile((TILE, 640), 1)),
        ((rows, 640), BF16, tile((TILE, 640), 1)),
        ((rows, 512), F32, tile((TILE, 512), 1)),
        ((rows // SPAN, HV, HK), F32, tile((PER, HV, HK), 1)),
        ((tiles, 8, 128), F32, tile((1, 8, 128), 1)),
        ((HV, HK), F32, whole((HV, HK))),
        ((8, 128), F32, whole((8, 128))),
    ]
    return pl.pallas_call(
        functools.partial(front_kernel, tiles, count),
        grid=(2 * tiles + 1,),
        out_shape=[jax.ShapeDtypeStruct(s, d) for s, d, _ in outs],
        in_specs=[whole(a.shape) for a in ins],
        out_specs=[s for _, _, s in outs],
        scratch_shapes=[
            pltpu.VMEM((2 * tiles, 4, TILE, BLOCK), BF16),
            pltpu.VMEM((MODEL_WIDTH, 896), BF16),
            pltpu.VMEM((2 * TILE, TILE), BF16),
            pltpu.VMEM((HV, HK), F32),
            pltpu.VMEM((8, 128), F32),
            pltpu.VMEM((HV + 16, HK), BF16),
            pltpu.VMEM((count, HV + 16, HK), BF16),
            pltpu.SemaphoreType.DMA((6, 2 * tiles)),
            pltpu.SemaphoreType.DMA((count,)),
            pltpu.SemaphoreType.DMA((count,)),
        ],
        compiler_params=pltpu.CompilerParams(
            collective_id=1, has_side_effects=True, vmem_limit_bytes=VMEM_LIMIT,
            dimension_semantics=("arbitrary",),
        ),
        name="front",
    )(*ins)


def tile_spec(tiles, shape, lag, back=False, col=0):
    rest = (0,) * (len(shape) - 2) + (col,)

    def index(i):
        t = jnp.clip(i - lag, 0, tiles - 1)
        return ((tiles - 1 - t) if back else t,) + rest

    return pl.BlockSpec(shape, index)


def ffn_kernel(
    tiles,
    x_ref, keep_ref, in_ref, gg_ref, gain_ref, wout, wfg, wfu, wfd,
    f_ref, o_ref, u_ref, e_ref, cg_ref,
    gated_o, oo_o, ws_o, h_o, inv_o, gsend_o, gown_o, psend_o, pown_o, stat_o, dg_o, du_o, dd_o,
    state, pa, pp, pg, ma, mp, mg, sc, rc, own, hg, nf_s, ag, au, ad, st_s, st_r,
    asem, psem, gsem, csem, hsem, tsem,
):
    i = pl.program_id(0)
    me, mate, cross, far = peers()
    last = tiles - 1

    def pair(buf, got, sem, t, which):
        block = mate if which == 0 else far
        return to_head(buf.at[t, block], got.at[t, which], sem.at[2 * which, t], sem.at[2 * which + 1, t], mate)

    def over(t):
        return to_head(sc.at[t], rc.at[t], csem.at[0, t], csem.at[1, t], cross)

    def own_mate(t):
        return to_head(hg.at[t, me], hg.at[t, me], hsem.at[0, t], hsem.at[1, t], mate)

    def own_cross(t):
        return to_head(hg.at[t, me], hg.at[t, me], hsem.at[2, t], hsem.at[3, t], cross)

    def onward(t):
        return to_head(hg.at[t, cross], hg.at[t, cross], hsem.at[4, t], hsem.at[5, t], mate)

    def stats(n, other):
        return to_head(st_s, st_r.at[n], tsem.at[0, n], tsem.at[1, n], other)

    @pl.when(i == 0)
    def _():
        greet_head()
        state[...] = in_ref[...]
        ag[...] = jnp.zeros_like(ag)
        au[...] = jnp.zeros_like(au)
        ad[...] = jnp.zeros_like(ad)
        st_s[...] = jnp.zeros_like(st_s)
        pl.semaphore_wait(pltpu.get_barrier_semaphore(), 3)

    @pl.when((i >= 5) & (i - 5 <= last))
    def _():
        t = i - 5
        own_cross(t).wait_recv()
        onward(t).start()

    @pl.when((i >= 3) & (i - 3 <= last))
    def _():
        t = i - 3
        over(t).wait_recv()
        rows = pl.ds(pl.multiple_of(t * TILE, TILE), TILE)
        h = x_ref[rows, :].astype(F32) + (own[lax.rem(t, 4)] + rc[t].astype(F32))
        h_o[...] = h
        hg[t, me] = h.astype(BF16)
        own_cross(t).start()
        own_mate(t).start()

    @pl.when((i >= 1) & (i - 1 <= last))
    def _():
        t = i - 1
        pair(pa, ma, asem, t, 0).wait_recv()
        pair(pa, ma, asem, t, 1).wait_recv()
        sc[t] = (pa[t, cross].astype(F32) + ma[t, 1].astype(F32)).astype(BF16)
        over(t).start()
        own[lax.rem(t, 4)] = pa[t, me].astype(F32) + ma[t, 0].astype(F32)

    @pl.when(i <= last)
    def _():
        t = i
        for c in range(PER):
            rows = slice(c * SPAN, (c + 1) * SPAN)
            scaled = (keep_ref[t, c : c + 1, :] * e_ref[0, c : c + 1, :]) * state[...]
            low = scaled.astype(BF16)
            ws_o[c] = low
            state[...] = scaled + u_ref[c]
            oo_o[rows, :] = o_ref[rows, 256:512] + dot_nt(f_ref[rows, :].astype(BF16), low)
        o = oo_o[...]
        gz = o_ref[:, 0:256]
        inv = lax.rsqrt(jnp.mean(o * o, axis=1, keepdims=True) + EPS)
        gated = (o * inv * gg_ref[...] * (gz * jax.nn.sigmoid(gz))).astype(BF16)
        gated_o[...] = gated
        for j in range(4):
            pa[t, j] = dot_nn(gated, wout[:, j * BLOCK : (j + 1) * BLOCK]).astype(BF16)
        pair(pa, ma, asem, t, 1).start()
        pair(pa, ma, asem, t, 0).start()

    @pl.when((i >= 7) & (i - 7 <= last))
    def _():
        t = i - 7
        for which in range(2):
            pair(pp, mp, psem, t, which).wait_recv()
            pair(pg, mg, gsem, t, which).wait_recv()
        psend_o[...] = (pp[t, cross].astype(F32) + mp[t, 1].astype(F32)).astype(BF16)
        pown_o[...] = pp[t, me].astype(F32) + mp[t, 0].astype(F32)
        gsend_o[...] = (pg[t, cross].astype(F32) + mg[t, 1].astype(F32)).astype(BF16)
        gown_o[...] = pg[t, me].astype(F32) + mg[t, 0].astype(F32)

    @pl.when((i >= 6) & (i - 6 <= last))
    def _():
        t = i - 6
        own_mate(t).wait_recv()
        onward(t).wait_recv()
        squares = jnp.zeros((TILE, 1), F32)
        for j in range(4):
            hj = hg[t, j].astype(F32)
            squares = squares + jnp.sum(hj * hj, axis=1, keepdims=True)
        inv = lax.rsqrt(squares / MODEL_WIDTH + EPS)
        inv_o[...] = jnp.broadcast_to(inv, (TILE, 128))
        for j in range(4):
            cols = slice(j * BLOCK, (j + 1) * BLOCK)
            nf_s[:, cols] = (hg[t, j].astype(F32) * inv * gain_ref[:, cols]).astype(BF16)
        nf = nf_s[...]
        fg = dot_nn(nf, wfg[...])
        fu = dot_nn(nf, wfu[...])
        sig = jax.nn.sigmoid(fg)
        silu = fg * sig
        act = (silu * fu).astype(BF16)
        cg = cg_ref[...]
        for j in range(4):
            pp[t, j] = dot_nn(act, wfd[:, j * BLOCK : (j + 1) * BLOCK]).astype(BF16)
        for which in range(2):
            pair(pp, mp, psem, t, which).start()
        gact = dot_nt(cg, wfd[...])
        gfg = (gact * fu * (sig * (1.0 + fg * (1.0 - sig)))).astype(BF16)
        gfu = (gact * silu).astype(BF16)
        stat = jnp.zeros((TILE, 1), F32)
        for j in range(4):
            rows = slice(j * BLOCK, (j + 1) * BLOCK)
            gj = dot_nt(gfg, wfg[rows, :]) + dot_nt(gfu, wfu[rows, :])
            stat = stat + jnp.sum(gj * nf_s[:, rows].astype(F32), axis=1, keepdims=True)
            pg[t, j] = gj.astype(BF16)
        for which in range(2):
            pair(pg, mg, gsem, t, which).start()
        st_s[pl.ds(t, 1), :] = jnp.broadcast_to(stat, (TILE, 128)).T[0:1, :]
        ad[...] += dot_tn(act, cg)
        ag[...] += dot_tn(nf, gfg)
        au[...] += dot_tn(nf, gfu)

    @pl.when(i == last + 6)
    def _():
        for n, other in enumerate((mate, cross, far)):
            stats(n, other).start()

    @pl.when(i == last + 7)
    def _():
        dg_o[...] = ag[...].astype(BF16)
        du_o[...] = au[...].astype(BF16)
        dd_o[...] = ad[...].astype(BF16)
        for n, other in enumerate((mate, cross, far)):
            stats(n, other).wait()
        stat_o[...] = (st_s[...] + st_r[0]) + (st_r[1] + st_r[2])

        def out(t, carry):
            for which in range(2):
                pair(pa, ma, asem, t, which).wait_send()
                pair(pp, mp, psem, t, which).wait_send()
                pair(pg, mg, gsem, t, which).wait_send()
            over(t).wait_send()
            own_cross(t).wait_send()
            own_mate(t).wait_send()
            onward(t).wait_send()
            return carry

        lax.fori_loop(0, tiles, out, 0)


def ffn(x, keep, inc, gg, gain, wout, wfg, wfu, wfd, f, o, u, e, cg):
    rows = x.shape[0]
    tiles = rows // TILE
    hidden = wfg.shape[1]
    width = wfg.shape[0]
    assert tiles <= 8
    ts = functools.partial(tile_spec, tiles)
    ins = (x, keep, inc, gg, gain, wout, wfg, wfu, wfd)
    outs = [
        ((rows, BLOCK), BF16, ts((TILE, BLOCK), 0)),
        ((rows, HV), F32, ts((TILE, HV), 0)),
        ((rows // SPAN, HV, HK), BF16, ts((PER, HV, HK), 0)),
        ((rows, BLOCK), F32, ts((TILE, BLOCK), 3)),
        ((rows, 128), F32, ts((TILE, 128), 6)),
        ((rows, BLOCK), BF16, ts((TILE, BLOCK), 7)),
        ((rows, BLOCK), F32, ts((TILE, BLOCK), 7)),
        ((rows, BLOCK), BF16, ts((TILE, BLOCK), 7)),
        ((rows, BLOCK), F32, ts((TILE, BLOCK), 7)),
        ((8, TILE), F32, whole((8, TILE))),
        ((width, hidden), BF16, whole((width, hidden))),
        ((width, hidden), BF16, whole((width, hidden))),
        ((hidden, width), BF16, whole((hidden, width))),
    ]
    tiled = lambda n: pltpu.VMEM((tiles, n, TILE, BLOCK), BF16)
    return pl.pallas_call(
        functools.partial(ffn_kernel, tiles),
        grid=(tiles + 7,),
        out_shape=[jax.ShapeDtypeStruct(s, d) for s, d, _ in outs],
        in_specs=[whole(a.shape) for a in ins]
        + [
            ts((TILE, 128), 0), ts((TILE, 512), 0), ts((PER, HV, HK), 0), ts((1, 8, 128), 0),
            ts((TILE, MODEL_WIDTH), 6),
        ],
        out_specs=[s for _, _, s in outs],
        scratch_shapes=[
            pltpu.VMEM((HV, HK), F32),
            tiled(4), tiled(4), tiled(4), tiled(2), tiled(2), tiled(2),
            pltpu.VMEM((tiles, TILE, BLOCK), BF16),
            pltpu.VMEM((tiles, TILE, BLOCK), BF16),
            pltpu.VMEM((4, TILE, BLOCK), F32),
            tiled(4),
            pltpu.VMEM((TILE, MODEL_WIDTH), BF16),
            pltpu.VMEM((width, hidden), F32),
            pltpu.VMEM((width, hidden), F32),
            pltpu.VMEM((hidden, width), F32),
            pltpu.VMEM((8, TILE), F32),
            pltpu.VMEM((3, 8, TILE), F32),
            pltpu.SemaphoreType.DMA((4, tiles)),
            pltpu.SemaphoreType.DMA((4, tiles)),
            pltpu.SemaphoreType.DMA((4, tiles)),
            pltpu.SemaphoreType.DMA((2, tiles)),
            pltpu.SemaphoreType.DMA((6, tiles)),
            pltpu.SemaphoreType.DMA((2, 3)),
        ],
        compiler_params=pltpu.CompilerParams(
            collective_id=2, has_side_effects=True, vmem_limit_bytes=VMEM_LIMIT,
            dimension_semantics=("arbitrary",),
        ),
        name="ffn",
    )(*ins, f, o, u, e, cg)


def back_kernel(
    tiles, count,
    gsend, psend, x_ref, c_ref, keep_ref, d_ref, stat_ref, gg_ref, again, fgain, wout, wq, wk, wv, wg, wr, rup,
    gown, h1, invf, f1, gz_ref, oo_ref, gated, ws1, b1, e1,
    f2, b2, ws2, e2, na, h2, pown, inva,
    gt_o, lo_o, dq_o, dk_o, dv_o, dg_o, dr_o, dwo_o, dag_o, dfg_o, dgg_o, db_o, dup_o,
    wcat, tri, rg, rp, gh, gb, gat, gzs, gw, gqd, gkd, gv, state, sbuf, rbuf,
    gcat, pn, mn, sc, rc, own, st_s, st_r, dwa, dwo,
    gsem, psem, hsem, nsem, csem, tsem, esend, erecv,
):
    i = pl.program_id(0)
    me, mate, cross, far = peers()
    place = lax.axis_index("seq")
    last = tiles - 1
    second = tiles + 3

    def rows_of(t):
        return pl.ds(pl.multiple_of(t * TILE, TILE), TILE)

    def grads(t):
        return to_head(gsend.at[rows_of(t)], rg.at[t], gsem.at[0, t], gsem.at[1, t], cross)

    def feeds(t):
        return to_head(psend.at[rows_of(t)], rp.at[t], psem.at[0, t], psem.at[1, t], cross)

    def own_mate(t):
        return to_head(gb.at[t, me], gb.at[t, me], hsem.at[0, t], hsem.at[1, t], mate)

    def own_cross(t):
        return to_head(gb.at[t, me], gb.at[t, me], hsem.at[2, t], hsem.at[3, t], cross)

    def onward(t):
        return to_head(gb.at[t, cross], gb.at[t, cross], hsem.at[4, t], hsem.at[5, t], mate)

    def pair(t, which):
        block = mate if which == 0 else far
        return to_head(pn.at[t, block], mn.at[t, which], nsem.at[2 * which, t], nsem.at[2 * which + 1, t], mate)

    def over(t):
        return to_head(sc.at[t], rc.at[t], csem.at[0, t], csem.at[1, t], cross)

    def stats(t, n, other):
        return to_head(st_s.at[t], st_r.at[t, n], tsem.at[0, n, t], tsem.at[1, n, t], other)

    @pl.when(i == 0)
    def _():
        greet_head()
        greet_seq(count)
        pl.semaphore_wait(pltpu.get_barrier_semaphore(), 3 + count - 1)
        for n in range(AHEAD):
            grads(last - n).start()
        wcat[:, 0:128] = wq[...]
        wcat[:, 128:256] = wk[...]
        wcat[:, 256:512] = wv[...]
        wcat[:, 512:768] = wg[...]
        wcat[:, 768:896] = wr[...]
        r = lax.broadcasted_iota(jnp.int32, (TILE, TILE), 0)
        c = lax.broadcasted_iota(jnp.int32, (TILE, TILE), 1)
        tri[...] = jnp.where(((r >> 6) == (c >> 6)) & (r > c), 1.0, 0.0).astype(BF16)
        state[...] = jnp.zeros_like(state)
        dwa[...] = jnp.zeros_like(dwa)
        dwo[...] = jnp.zeros_like(dwo)
        dag_o[...] = jnp.zeros_like(dag_o)
        dfg_o[...] = jnp.zeros_like(dfg_o)
        dgg_o[...] = jnp.zeros_like(dgg_o)
        db_o[...] = jnp.zeros_like(db_o)
        dup_o[...] = jnp.zeros_like(dup_o)

    @pl.when(i + AHEAD <= last)
    def _():
        grads(last - i - AHEAD).start()

    @pl.when((i >= 2) & (i - 2 <= last))
    def _():
        t = last - (i - 2)
        own_cross(t).wait_recv()
        onward(t).start()

    @pl.when(i <= last)
    def _():
        t = last - i
        grads(t).wait_recv()
        gnf = gown[...] + rg[t].astype(F32)
        inv = invf[...][:, 0:1]
        hn = h1[...].astype(BF16).astype(F32) * inv
        row = stat_ref[pl.ds(t, 1), :]
        stat = jnp.broadcast_to(row, (128, TILE)).T[:, 0:1]
        grad = c_ref[rows_of(t), :].astype(F32) + inv * (fgain[me] * gnf - hn * (stat / MODEL_WIDTH))
        dfg_o[...] += jnp.sum(gnf * hn, axis=0, keepdims=True)
        gh[t] = grad
        gb[t, me] = grad.astype(BF16)
        own_cross(t).start()
        own_mate(t).start()

    @pl.when((i >= last) & (i - last <= (tiles - 1) // 2))
    def _():
        n = 2 * (i - last)
        feeds(last - n).start()

        @pl.when(n + 1 <= last)
        def _():
            feeds(last - n - 1).start()

    @pl.when((i >= 3) & (i - 3 <= last))
    def _():
        t = last - (i - 3)
        own_mate(t).wait_recv()
        onward(t).wait_recv()
        for j in range(4):
            gat[:, j * BLOCK : (j + 1) * BLOCK] = gb[t, j]
        g = gat[...]
        gt = dot_nt(g, wout[...])
        dwo[...] += dot_tn(gated[...], g)
        o = oo_ref[...]
        gz = gz_ref[...]
        inv = lax.rsqrt(jnp.mean(o * o, axis=1, keepdims=True) + EPS)
        on = o * inv
        sig = jax.nn.sigmoid(gz)
        gn = gt * (gz * sig)
        dgg_o[...] += jnp.sum(gn * on, axis=0, keepdims=True)
        gzs[t] = (gt * on * gg_ref[...] * (sig * (1.0 + gz * (1.0 - sig)))).astype(BF16)
        p = gn * gg_ref[...]
        go = (inv * (p - on * jnp.mean(p * on, axis=1, keepdims=True))).astype(BF16)
        qd = f1[:, 0:128].astype(BF16)
        kd = f1[:, 128:256].astype(BF16)
        v = b1[:, 0:256]
        causal, _ = span_masks(TILE, TILE)
        ga = jnp.where(causal, dot_nt(go, v), 0.0).astype(BF16)
        gqd[t] = dot_nn(ga, kd)
        gkd[t] = dot_tn(ga, qd)
        gv[t] = dot_tn(b1[:, 256:512], go)
        for c in range(PER - 1, -1, -1):
            rows = slice(c * SPAN, (c + 1) * SPAN)
            gqd[t, rows, :] += dot_nn(go[rows], ws1[c])
            fresh = dot_tn(go[rows], qd[rows])
            gw[t * PER + c] = fresh
            through = keep_ref[t, c : c + 1, :] * e1[0, c : c + 1, :]
            state[...] = through * (fresh + state[...])

    @pl.when(i == last + 3)
    def _():
        sbuf[...] = jnp.zeros_like(sbuf)
        sbuf[0:HV, :] = state[...].astype(BF16)
        d = d_ref[...]
        hi = d.astype(BF16).astype(F32)
        first = lax.broadcasted_iota(jnp.int32, (16, 128), 0) < 8
        both = jnp.where(first, jnp.concatenate([hi, hi], axis=0), jnp.concatenate([d - hi, d - hi], axis=0))
        sbuf[HV : HV + 16, :] = both.astype(BF16)

        def send(p, carry):
            to_seq(sbuf, rbuf.at[place], esend.at[p], erecv.at[place], p).start()
            return carry

        lax.fori_loop(0, place, send, 0)

    @pl.when(i == second)
    def _():
        state[...] = jnp.zeros_like(state)

        def join(n, carry):
            p = count - 1 - n
            to_seq(sbuf, rbuf.at[p], esend.at[p], erecv.at[p], place).wait_recv()
            got = rbuf[p].astype(F32)
            d = got[HV : HV + 1] + got[HV + 8 : HV + 9]
            state[...] = got[0:HV] + d * state[...]
            return carry

        lax.fori_loop(0, count - 1 - place, join, 0)

    @pl.when((i >= second + 3) & (i - second - 3 <= last))
    def _():
        t = last - (i - second - 3)
        over(t).wait_recv()
        for n, other in enumerate((mate, cross, far)):
            stats(t, n, other).wait_recv()
        gna = own[lax.rem(t, 4)] + rc[t].astype(F32)
        inv = inva[...][:, 0:1]
        xn = x_ref[rows_of(t), :].astype(F32) * inv
        row = (st_s[t] + st_r[t, 0]) + (st_r[t, 1] + st_r[t, 2])
        stat = jnp.broadcast_to(row[0:1], (128, TILE)).T[:, 0:1]
        gt_o[...] = gh[t] + inv * (again[me] * gna - xn * (stat / MODEL_WIDTH))
        dag_o[...] += jnp.sum(gna * xn, axis=0, keepdims=True)

    @pl.when((i >= second + 1) & (i - second - 1 <= last))
    def _():
        t = last - (i - second - 1)
        pair(t, 0).wait_recv()
        pair(t, 1).wait_recv()
        sc[t] = (pn[t, cross].astype(F32) + mn[t, 1].astype(F32)).astype(BF16)
        over(t).start()
        own[lax.rem(t, 4)] = pn[t, me].astype(F32) + mn[t, 0].astype(F32)

    @pl.when((i >= second) & (i - second <= last))
    def _():
        t = last - (i - second)
        qf = f2[:, 0:128]
        kf = f2[:, 128:256]
        kd = kf.astype(BF16)
        pieces = [None] * PER
        for c in range(PER - 1, -1, -1):
            rows = slice(c * SPAN, (c + 1) * SPAN)
            low = state[...].astype(BF16)
            gkd[t, rows, :] += dot_nn(b2[rows, 0:256], low)
            gv[t, rows, :] += dot_nt(kd[rows], low)
            ge = gw[t * PER + c] + state[...]
            pieces[c] = jnp.broadcast_to(jnp.sum(ge * ws2[c].astype(F32), axis=0, keepdims=True), (SPAN, HK))
            state[...] = (keep_ref[t, c : c + 1, :] * e2[0, c : c + 1, :]) * ge
        gq = gqd[t]
        gk = gkd[t]
        diff = gq * qf - gk * kf
        gg = jnp.concatenate(pieces, axis=0) - fold(dot_nn(tri[...], three(diff)))
        glogit = gg * f2[:, 512:640]
        db_o[...] += jnp.sum(glogit, axis=0, keepdims=True)
        hi = glogit.astype(BF16)
        lo = (glogit - hi.astype(F32)).astype(BF16)
        glr = dot_nt(hi, rup[...]) + dot_nt(lo, rup[...])
        lr = b2[:, 512:640]
        dup_o[...] += dot_tn(lr, hi) + dot_tn(lr, lo)
        gcat[:, 0:128] = (gq * f2[:, 256:384]).astype(BF16)
        gcat[:, 128:256] = (gk * f2[:, 384:512]).astype(BF16)
        gcat[:, 256:512] = gv[t].astype(BF16)
        gcat[:, 512:768] = gzs[t]
        gcat[:, 768:896] = glr.astype(BF16)
        g = gcat[...]
        stat = jnp.zeros((TILE, 1), F32)
        for j in range(4):
            cols = slice(j * BLOCK, (j + 1) * BLOCK)
            gj = dot_nt(g, wcat[cols, :])
            stat = stat + jnp.sum(gj * na[:, cols].astype(F32), axis=1, keepdims=True)
            pn[t, j] = gj.astype(BF16)
        pair(t, 1).start()
        pair(t, 0).start()
        st_s[t] = jnp.broadcast_to(stat, (TILE, 128)).T[0:8, :]
        for n, other in enumerate((mate, cross, far)):
            stats(t, n, other).start()
        dwa[...] += dot_tn(na[...], g)

    @pl.when((i >= second) & (i - second <= last))
    def _():
        t = last - (i - second)
        feeds(t).wait_recv()
        lo_o[...] = (h2[...] + (pown[...] + rp[t].astype(F32))).astype(BF16)

    @pl.when(i == second + last + 3)
    def _():
        dq_o[...] = dwa[:, 0:128].astype(BF16)
        dk_o[...] = dwa[:, 128:256].astype(BF16)
        dv_o[...] = dwa[:, 256:512].astype(BF16)
        dg_o[...] = dwa[:, 512:768].astype(BF16)
        dr_o[...] = dwa[:, 768:896]
        dwo_o[...] = dwo[...].astype(BF16)

        def sent(p, carry):
            to_seq(sbuf, rbuf.at[place], esend.at[p], erecv.at[place], p).wait_send()
            return carry

        lax.fori_loop(0, place, sent, 0)

        def out(t, carry):
            grads(t).wait_send()
            feeds(t).wait_send()
            own_cross(t).wait_send()
            own_mate(t).wait_send()
            onward(t).wait_send()
            pair(t, 0).wait_send()
            pair(t, 1).wait_send()
            over(t).wait_send()
            for n, other in enumerate((mate, cross, far)):
                stats(t, n, other).wait_send()
            return carry

        lax.fori_loop(0, tiles, out, 0)


def back(fixed, gown, h, invf, f, o, oo, gated, ws, b, e, na, pown, inva):
    rows = h.shape[0]
    tiles = rows // TILE
    count = lax.axis_size("seq")
    second = tiles + 3
    width = MODEL_WIDTH
    ts = functools.partial(tile_spec, tiles, back=True)
    outs = [
        ((rows, BLOCK), F32, ts((TILE, BLOCK), second + 3)),
        ((rows, BLOCK), BF16, ts((TILE, BLOCK), second)),
        ((width, 128), BF16, whole((width, 128))),
        ((width, 128), BF16, whole((width, 128))),
        ((width, 256), BF16, whole((width, 256))),
        ((width, 256), BF16, whole((width, 256))),
        ((width, 128), F32, whole((width, 128))),
        ((256, width), BF16, whole((256, width))),
        ((1, 256), F32, whole((1, 256))),
        ((1, 256), F32, whole((1, 256))),
        ((1, 256), F32, whole((1, 256))),
        ((1, 128), F32, whole((1, 128))),
        ((128, 128), F32, whole((128, 128))),
    ]
    tiled = lambda n: pltpu.VMEM((tiles, n, TILE, BLOCK), BF16)
    flat = lambda n, d: pltpu.VMEM((tiles, TILE, n), d)
    return pl.pallas_call(
        functools.partial(back_kernel, tiles, count),
        grid=(second + tiles + 3,),
        out_shape=[jax.ShapeDtypeStruct(s, d) for s, d, _ in outs],
        in_specs=[whole(a.shape) for a in fixed]
        + [
            ts((TILE, BLOCK), 0), ts((TILE, BLOCK), 0), ts((TILE, 128), 0),
            ts((TILE, 256), 3), ts((TILE, 256), 3), ts((TILE, 256), 3), ts((TILE, 256), 3),
            ts((PER, HV, HK), 3), ts((TILE, 640), 3), ts((1, 8, 128), 3),
            ts((TILE, 640), second), ts((TILE, 640), second), ts((PER, HV, HK), second), ts((1, 8, 128), second),
            ts((TILE, width), second), ts((TILE, BLOCK), second), ts((TILE, BLOCK), second),
            ts((TILE, 128), second + 3),
        ],
        out_specs=[s for _, _, s in outs],
        scratch_shapes=[
            pltpu.VMEM((width, 896), BF16),
            pltpu.VMEM((TILE, TILE), BF16),
            flat(BLOCK, BF16), flat(BLOCK, BF16), flat(BLOCK, F32),
            tiled(4),
            pltpu.VMEM((TILE, width), BF16),
            flat(BLOCK, BF16),
            pltpu.VMEM((rows // SPAN, HV, HK), F32),
            flat(HK, F32), flat(HK, F32), flat(HV, F32),
            pltpu.VMEM((HV, HK), F32),
            pltpu.VMEM((HV + 16, HK), BF16),
            pltpu.VMEM((count, HV + 16, HK), BF16),
            pltpu.VMEM((TILE, 896), BF16),
            tiled(4), tiled(2), flat(BLOCK, BF16), flat(BLOCK, BF16),
            pltpu.VMEM((4, TILE, BLOCK), F32),
            pltpu.VMEM((tiles, 8, TILE), F32),
            pltpu.VMEM((tiles, 3, 8, TILE), F32),
            pltpu.VMEM((width, 896), F32),
            pltpu.VMEM((256, width), F32),
            pltpu.SemaphoreType.DMA((2, tiles)),
            pltpu.SemaphoreType.DMA((2, tiles)),
            pltpu.SemaphoreType.DMA((6, tiles)),
            pltpu.SemaphoreType.DMA((4, tiles)),
            pltpu.SemaphoreType.DMA((2, tiles)),
            pltpu.SemaphoreType.DMA((2, 3, tiles)),
            pltpu.SemaphoreType.DMA((count,)),
            pltpu.SemaphoreType.DMA((count,)),
        ],
        compiler_params=pltpu.CompilerParams(
            collective_id=3, has_side_effects=True, vmem_limit_bytes=VMEM_LIMIT,
            dimension_semantics=("arbitrary",),
        ),
        name="back",
    )(*fixed, gown, h, invf, f, o, oo, gated, ws, b, e, f, b, ws, e, na, h, pown, inva)


def shards(
    tokens,
    row_starts,
    attn_gain,
    query_weight,
    key_weight,
    value_weight,
    gate_weight,
    rank_down,
    rank_up,
    rank_bias,
    group_gain,
    out_weight,
    feed_gain,
    feed_gate,
    feed_up,
    feed_down,
    cotangent,
):
    rows = tokens.shape[0]
    tiles = rows // TILE
    spans = rows // SPAN
    span_ids = lax.axis_index("seq") * spans + jnp.arange(spans, dtype=jnp.int32)
    resets = jnp.any((row_starts // SPAN)[None, :] == span_ids[:, None], axis=1).astype(F32)
    keep = jnp.pad((1.0 - resets).reshape(tiles, PER, 1), ((0, 0), (0, 8 - PER), (0, 0)))
    keep = jnp.broadcast_to(keep, (tiles, 8, 128))
    wide = jnp.pad(rank_down[0], ((0, 0), (0, 128 - RANK)))
    tall = jnp.pad(rank_up[0], ((0, 128 - RANK), (0, 0)))
    weights = (query_weight[0], key_weight[0], value_weight[0], gate_weight[0], wide, tall)
    again = attn_gain.astype(F32)
    fgain = feed_gain.astype(F32)
    ggain = group_gain.astype(F32)
    na, cg, inva, f, b, o, u, e, inc, dec = front(
        tokens, cotangent, keep, again, *weights, rank_bias.astype(F32)
    )
    gated, oo, ws, h, invf, gsend, gown, psend, pown, stat, dfg, dfu, dfd = ffn(
        tokens, keep, inc, ggain, fgain, out_weight[0], feed_gate[0], feed_up[0], feed_down[0], f, o, u, e, cg
    )
    dfg, dfu, dfd = lax.psum((dfg, dfu, dfd), "seq")
    fixed = (
        gsend, psend, tokens, cotangent, keep, dec, stat, ggain, again.reshape(4, 1, BLOCK), fgain.reshape(4, 1, BLOCK),
        out_weight[0],
    ) + weights
    grad_tokens, layer_out, dq, dk, dv, dg, dr, dwo, dag, dffg, dgg, db, dup = back(
        fixed, gown, h, invf, f, o, oo, gated, ws, b, e, na, pown, inva
    )
    dq, dk, dv, dg, dwo, dfg, dfu, dfd = lax.optimization_barrier((dq, dk, dv, dg, dwo, dfg, dfu, dfd))
    dr = dr[:, 0:RANK].T.reshape(128, 128)
    dr, dgg = lax.psum((dr.astype(BF16), dgg.astype(BF16)), "head")
    dq, dk, dv, dg, dwo, dr, dgg, dag, dffg, db, dup = lax.psum(
        (dq, dk, dv, dg, dwo, dr, dgg, dag.astype(BF16), dffg.astype(BF16), db.astype(BF16), dup[0:RANK].astype(BF16)),
        "seq",
    )
    dr = dr.reshape(RANK, MODEL_WIDTH).T
    grads = (dag, dq[None], dk[None], dv[None], dg[None], dr[None], dup[None], db, dgg, dwo[None], dffg, dfg[None], dfu[None], dfd[None])
    return (layer_out, grad_tokens) + tuple(g.astype(F32) for g in grads)


def solution(mesh):
    placed = (
        P("seq", "head"),
        P(),
        P(),
        P(None, None, "head"),
        P(None, None, "head"),
        P(None, None, "head"),
        P(None, None, "head"),
        P(),
        P(None, None, "head"),
        P(None, "head"),
        P(),
        P(None, "head", None),
        P(),
        P(None, None, "head"),
        P(None, None, "head"),
        P(None, "head", None),
        P("seq", "head"),
    )
    return jax.shard_map(
        shards,
        mesh=mesh,
        in_specs=placed,
        out_specs=(
            P("seq", "head"),
            P("seq", "head"),
            P(None, "head"),
            P(None, None, "head"),
            P(None, None, "head"),
            P(None, None, "head"),
            P(None, None, "head"),
            P(),
            P(None, None, "head"),
            P(None, "head"),
            P(),
            P(None, "head", None),
            P(None, "head"),
            P(None, None, "head"),
            P(None, None, "head"),
            P(None, "head", None),
        ),
        check_vma=False,
    )
```

```python
import functools

import jax
import jax.numpy as jnp
from jax import lax
from jax.experimental import pallas as pl
from jax.experimental.pallas import tpu as pltpu
from jax.sharding import PartitionSpec as P

MODEL_WIDTH = 1024
HK = 128
HV = 256
SPAN = 64
RANK = 16
EPS = 1e-06
GATE_NORM = 16.0
TILE = 256
PER = TILE // SPAN
BLOCK = 256
AHEAD = 3
F32 = jnp.float32
BF16 = jnp.bfloat16
MESH = pl.DeviceIdType.MESH
VMEM_LIMIT = 62 * 1024 * 1024


def dot_nn(a, b):
    return jnp.dot(a, b, preferred_element_type=F32)


def dot_nt(a, b):
    return lax.dot_general(a, b, (((1,), (1,)), ((), ())), preferred_element_type=F32)


def dot_tn(a, b):
    return lax.dot_general(a, b, (((0,), (0,)), ((), ())), preferred_element_type=F32)


def peers():
    me = lax.axis_index("head")
    mate = me + 1 - 2 * lax.rem(me, 2)
    cross = lax.rem(me + 2, 4)
    far = cross + 1 - 2 * lax.rem(cross, 2)
    return me, mate, cross, far


def greet_head():
    _, mate, cross, far = peers()
    barrier = pltpu.get_barrier_semaphore()
    for other in (mate, cross, far):
        pl.semaphore_signal(barrier, inc=1, device_id={"head": other}, device_id_type=MESH)


def greet_seq(count):
    place = lax.axis_index("seq")
    barrier = pltpu.get_barrier_semaphore()

    def one(step, carry):
        other = lax.rem(place + step, count)
        pl.semaphore_signal(barrier, inc=1, device_id={"seq": other}, device_id_type=MESH)
        return carry

    lax.fori_loop(1, count, one, 0)


def to_head(src, dst, send, recv, other):
    return pltpu.make_async_remote_copy(
        src_ref=src, dst_ref=dst, send_sem=send, recv_sem=recv,
        device_id={"head": other}, device_id_type=MESH,
    )


def to_seq(src, dst, send, recv, other):
    return pltpu.make_async_remote_copy(
        src_ref=src, dst_ref=dst, send_sem=send, recv_sem=recv,
        device_id={"seq": other}, device_id_type=MESH,
    )


def span_masks(rows, cols):
    r = lax.broadcasted_iota(jnp.int32, (rows, cols), 0)
    c = lax.broadcasted_iota(jnp.int32, (rows, cols), 1)
    same = (r >> 6) == (c >> 6)
    return same & (r >= c), same


def three(x):
    a = x.astype(BF16)
    rest = x - a.astype(F32)
    b = rest.astype(BF16)
    c = (rest - b.astype(F32)).astype(BF16)
    return jnp.concatenate([a, b, c], axis=1)


def fold(x):
    w = x.shape[1] // 3
    return x[:, :w] + x[:, w : 2 * w] + x[:, 2 * w :]


def front_kernel(
    tiles, count,
    x_ref, c_ref, keep_ref, gain_ref, wq, wk, wv, wg, wr, rup, bias_ref,
    na_o, cg_o, inv_o, f_o, b_o, o_o, u_o, e_o, in_o, d_o,
    grid_buf, wcat, tri, state, decay, sbuf, rbuf, sems, esend, erecv,
):
    i = pl.program_id(0)
    me, mate, cross, far = peers()
    place = lax.axis_index("seq")
    total = 2 * tiles

    def own_mate(m):
        return to_head(grid_buf.at[m, me], grid_buf.at[m, me], sems.at[0, m], sems.at[1, m], mate)

    def own_cross(m):
        return to_head(grid_buf.at[m, me], grid_buf.at[m, me], sems.at[2, m], sems.at[3, m], cross)

    def onward(m):
        return to_head(grid_buf.at[m, cross], grid_buf.at[m, cross], sems.at[4, m], sems.at[5, m], mate)

    @pl.when(i == 0)
    def _():
        greet_head()
        greet_seq(count)

        def own(m, carry):
            rows = pl.ds(pl.multiple_of(m * TILE, TILE), TILE)
            grid_buf[m, me] = x_ref[rows, :]
            grid_buf[m + tiles, me] = c_ref[rows, :]
            return carry

        lax.fori_loop(0, tiles, own, 0)
        pl.semaphore_wait(pltpu.get_barrier_semaphore(), 3 + count - 1)
        for m in range(AHEAD):
            own_cross(m).start()
            own_mate(m).start()
        wcat[:, 0:128] = wq[...]
        wcat[:, 128:256] = wk[...]
        wcat[:, 256:512] = wv[...]
        wcat[:, 512:768] = wg[...]
        causal, same = span_masks(TILE, TILE)
        tri[0:TILE, :] = jnp.where(causal, 1.0, 0.0).astype(BF16)
        tri[TILE : 2 * TILE, :] = jnp.where(same, 1.0, 0.0).astype(BF16)
        state[...] = jnp.zeros_like(state)
        decay[...] = jnp.ones_like(decay)

    @pl.when(i < total)
    def _():
        own_cross(i).wait_recv()
        onward(i).start()

    @pl.when(i + AHEAD < total)
    def _():
        own_cross(i + AHEAD).start()
        own_mate(i + AHEAD).start()

    @pl.when(i >= 1)
    def _():
        own_mate(i - 1).wait_recv()
        onward(i - 1).wait_recv()

    @pl.when((i >= 1) & (i <= tiles))
    def _():
        m = i - 1
        squares = jnp.zeros((TILE, 1), F32)
        for j in range(4):
            xj = grid_buf[m, j].astype(F32)
            squares = squares + jnp.sum(xj * xj, axis=1, keepdims=True)
        inv = lax.rsqrt(squares / MODEL_WIDTH + EPS)
        inv_o[...] = jnp.broadcast_to(inv, (TILE, 128))
        for j in range(4):
            cols = slice(j * BLOCK, (j + 1) * BLOCK)
            xj = grid_buf[m, j].astype(F32)
            na_o[:, cols] = (xj * inv * gain_ref[:, cols].astype(F32)).astype(BF16)
        proj = dot_nn(na_o[...], wcat[...])
        q = proj[:, 0:128]
        k = proj[:, 128:256]
        v = proj[:, 256:512].astype(BF16)
        o_o[:, 0:256] = proj[:, 512:768]
        lr = dot_nt(na_o[...], wr[...]).astype(BF16)
        z = dot_nn(lr, rup[...]) + bias_ref[...].astype(F32)
        g = (jnp.minimum(z, 0.0) - jnp.log1p(jnp.exp(-jnp.abs(z)))) / GATE_NORM
        sums = fold(dot_nn(tri[...], three(g)))
        b = sums[0:TILE]
        e = sums[TILE : 2 * TILE]
        fq = (HK ** (-0.5)) * jnp.exp(b - e)
        fk = jnp.exp(e - b)
        qf = q * fq
        kf = k * fk
        f_o[:, 0:128] = qf
        f_o[:, 128:256] = kf
        f_o[:, 256:384] = fq
        f_o[:, 384:512] = fk
        f_o[:, 512:640] = jax.nn.sigmoid(-z) / GATE_NORM
        qd = qf.astype(BF16)
        kd = kf.astype(BF16)
        causal, _ = span_masks(TILE, TILE)
        scores = jnp.where(causal, dot_nt(qd, kd), 0.0).astype(BF16)
        b_o[:, 0:256] = v
        b_o[:, 256:512] = scores
        b_o[:, 512 : 512 + RANK] = lr
        o_o[:, 256:512] = dot_nn(scores, v)
        for c in range(PER):
            rows = slice(c * SPAN, (c + 1) * SPAN)
            update = dot_tn(v[rows], kd[rows])
            u_o[c] = update
            ee = jnp.exp(e[c * SPAN : c * SPAN + 1])
            e_o[0, c : c + 1, :] = ee
            through = keep_ref[m, c : c + 1, :] * ee
            state[...] = through * state[...] + update
            decay[...] = through * decay[...]

    @pl.when(i == tiles)
    def _():
        d_o[...] = decay[...]
        sbuf[0:HV, :] = state[...].astype(BF16)
        d = decay[...]
        hi = d.astype(BF16).astype(F32)
        first = lax.broadcasted_iota(jnp.int32, (16, 128), 0) < 8
        both = jnp.where(first, jnp.concatenate([hi, hi], axis=0), jnp.concatenate([d - hi, d - hi], axis=0))
        sbuf[HV : HV + 16, :] = both.astype(BF16)

        def send(p, carry):
            to_seq(sbuf, rbuf.at[place], esend.at[p], erecv.at[place], p).start()
            return carry

        lax.fori_loop(place + 1, count, send, 0)

    @pl.when(i > tiles)
    def _():
        m = i - 1
        for j in range(4):
            cg_o[:, j * BLOCK : (j + 1) * BLOCK] = grid_buf[m, j]

    @pl.when(i == total)
    def _():
        in_o[...] = jnp.zeros_like(in_o)

        def join(p, carry):
            to_seq(sbuf, rbuf.at[p], esend.at[p], erecv.at[p], place).wait_recv()
            got = rbuf[p].astype(F32)
            d = got[HV : HV + 1] + got[HV + 8 : HV + 9]
            in_o[...] = got[0:HV] + d * in_o[...]
            return carry

        lax.fori_loop(0, place, join, 0)

        def sent(p, carry):
            to_seq(sbuf, rbuf.at[place], esend.at[p], erecv.at[place], p).wait_send()
            return carry

        lax.fori_loop(place + 1, count, sent, 0)

        def out(m, carry):
            own_cross(m).wait_send()
            own_mate(m).wait_send()
            onward(m).wait_send()
            return carry

        lax.fori_loop(0, total, out, 0)


def whole(shape):
    zeros = (0,) * len(shape)
    return pl.BlockSpec(shape, lambda i: zeros, pipeline_mode=pl.Buffered(1))


def front(x, cot, keep, gain, wq, wk, wv, wg, wr, rup, bias):
    rows = x.shape[0]
    tiles = rows // TILE
    count = lax.axis_size("seq")

    def tile(shape, lag, axis0=True):
        rest = (0,) * (len(shape) - 1)
        return pl.BlockSpec(shape, lambda i: (jnp.clip(i - lag, 0, tiles - 1),) + rest)

    ins = (x, cot, keep, gain, wq, wk, wv, wg, wr, rup, bias)
    outs = [
        ((rows, MODEL_WIDTH), BF16, tile((TILE, MODEL_WIDTH), 1)),
        ((rows, MODEL_WIDTH), BF16, tile((TILE, MODEL_WIDTH), 1 + tiles)),
        ((rows, 128), F32, tile((TILE, 128), 1)),
        ((rows, 640), F32, tile((TILE, 640), 1)),
        ((rows, 640), BF16, tile((TILE, 640), 1)),
        ((rows, 512), F32, tile((TILE, 512), 1)),
        ((rows // SPAN, HV, HK), F32, tile((PER, HV, HK), 1)),
        ((tiles, 8, 128), F32, tile((1, 8, 128), 1)),
        ((HV, HK), F32, whole((HV, HK))),
        ((8, 128), F32, whole((8, 128))),
    ]
    return pl.pallas_call(
        functools.partial(front_kernel, tiles, count),
        grid=(2 * tiles + 1,),
        out_shape=[jax.ShapeDtypeStruct(s, d) for s, d, _ in outs],
        in_specs=[whole(a.shape) for a in ins],
        out_specs=[s for _, _, s in outs],
        scratch_shapes=[
            pltpu.VMEM((2 * tiles, 4, TILE, BLOCK), BF16),
            pltpu.VMEM((MODEL_WIDTH, 768), BF16),
            pltpu.VMEM((2 * TILE, TILE), BF16),
            pltpu.VMEM((HV, HK), F32),
            pltpu.VMEM((8, 128), F32),
            pltpu.VMEM((HV + 16, HK), BF16),
            pltpu.VMEM((count, HV + 16, HK), BF16),
            pltpu.SemaphoreType.DMA((6, 2 * tiles)),
            pltpu.SemaphoreType.DMA((count,)),
            pltpu.SemaphoreType.DMA((count,)),
        ],
        compiler_params=pltpu.CompilerParams(
            collective_id=1, has_side_effects=True, vmem_limit_bytes=VMEM_LIMIT,
            dimension_semantics=("arbitrary",),
        ),
        name="front",
    )(*ins)


def tile_spec(tiles, shape, lag, back=False, col=0):
    rest = (0,) * (len(shape) - 2) + (col,)

    def index(i):
        t = jnp.clip(i - lag, 0, tiles - 1)
        return ((tiles - 1 - t) if back else t,) + rest

    return pl.BlockSpec(shape, index)


def up_to(n, step):
    return (n + step - 1) // step * step


def ffn_kernel(
    tiles,
    x_ref, keep_ref, in_ref, gg_ref, gain_ref, wout, wfg, wfu, wfd,
    f_ref, o_ref, u_ref, e_ref, cg_ref,
    gated_o, oo_o, ws_o, h_o, inv_o, gsend_o, gown_o, psend_o, pown_o, stat_o, wide_o,
    state, pa, pp, pg, ma, mp, mg, sc, rc, own, hg, nf_s, acc, st_s, st_r,
    asem, psem, gsem, csem, hsem, tsem,
):
    i = pl.program_id(0)
    me, mate, cross, far = peers()
    last = tiles - 1
    hidden = wfg.shape[0]

    def pair(buf, got, sem, t, which):
        block = mate if which == 0 else far
        return to_head(buf.at[t, block], got.at[t, which], sem.at[2 * which, t], sem.at[2 * which + 1, t], mate)

    def over(t):
        return to_head(sc.at[t], rc.at[t], csem.at[0, t], csem.at[1, t], cross)

    def own_mate(t):
        return to_head(hg.at[t, me], hg.at[t, me], hsem.at[0, t], hsem.at[1, t], mate)

    def own_cross(t):
        return to_head(hg.at[t, me], hg.at[t, me], hsem.at[2, t], hsem.at[3, t], cross)

    def onward(t):
        return to_head(hg.at[t, cross], hg.at[t, cross], hsem.at[4, t], hsem.at[5, t], mate)

    def stats(n, other):
        return to_head(st_s, st_r.at[n], tsem.at[0, n], tsem.at[1, n], other)

    @pl.when(i == 0)
    def _():
        greet_head()
        state[...] = in_ref[...]
        acc[...] = jnp.zeros_like(acc)
        st_s[...] = jnp.zeros_like(st_s)
        pl.semaphore_wait(pltpu.get_barrier_semaphore(), 3)

    @pl.when((i >= 5) & (i - 5 <= last))
    def _():
        t = i - 5
        own_cross(t).wait_recv()
        onward(t).start()

    @pl.when((i >= 3) & (i - 3 <= last))
    def _():
        t = i - 3
        over(t).wait_recv()
        rows = pl.ds(pl.multiple_of(t * TILE, TILE), TILE)
        h = x_ref[rows, :].astype(F32) + (own[lax.rem(t, 4)] + rc[t].astype(F32))
        h_o[...] = h
        hg[t, me] = h.astype(BF16)
        own_cross(t).start()
        own_mate(t).start()

    @pl.when((i >= 1) & (i - 1 <= last))
    def _():
        t = i - 1
        pair(pa, ma, asem, t, 0).wait_recv()
        pair(pa, ma, asem, t, 1).wait_recv()
        sc[t] = (pa[t, cross].astype(F32) + ma[t, 1].astype(F32)).astype(BF16)
        over(t).start()
        own[lax.rem(t, 4)] = pa[t, me].astype(F32) + ma[t, 0].astype(F32)

    @pl.when(i <= last)
    def _():
        t = i
        for c in range(PER):
            rows = slice(c * SPAN, (c + 1) * SPAN)
            scaled = (keep_ref[t, c : c + 1, :] * e_ref[0, c : c + 1, :]) * state[...]
            low = scaled.astype(BF16)
            ws_o[c] = low
            state[...] = scaled + u_ref[c]
            oo_o[rows, :] = o_ref[rows, 256:512] + dot_nt(f_ref[rows, :].astype(BF16), low)
        o = oo_o[...]
        gz = o_ref[:, 0:256]
        inv = lax.rsqrt(jnp.mean(o * o, axis=1, keepdims=True) + EPS)
        gated = (o * inv * gg_ref[...].astype(F32) * (gz * jax.nn.sigmoid(gz))).astype(BF16)
        gated_o[...] = gated
        for j in range(4):
            pa[t, j] = dot_nn(gated, wout[:, j * BLOCK : (j + 1) * BLOCK]).astype(BF16)
        pair(pa, ma, asem, t, 1).start()
        pair(pa, ma, asem, t, 0).start()

    @pl.when((i >= 7) & (i - 7 <= last))
    def _():
        t = i - 7
        for which in range(2):
            pair(pp, mp, psem, t, which).wait_recv()
            pair(pg, mg, gsem, t, which).wait_recv()
        psend_o[...] = (pp[t, cross].astype(F32) + mp[t, 1].astype(F32)).astype(BF16)
        pown_o[...] = pp[t, me].astype(F32) + mp[t, 0].astype(F32)
        gsend_o[...] = (pg[t, cross].astype(F32) + mg[t, 1].astype(F32)).astype(BF16)
        gown_o[...] = pg[t, me].astype(F32) + mg[t, 0].astype(F32)

    @pl.when((i >= 6) & (i - 6 <= last))
    def _():
        t = i - 6
        own_mate(t).wait_recv()
        onward(t).wait_recv()
        squares = jnp.zeros((TILE, 1), F32)
        for j in range(4):
            hj = hg[t, j].astype(F32)
            squares = squares + jnp.sum(hj * hj, axis=1, keepdims=True)
        inv = lax.rsqrt(squares / MODEL_WIDTH + EPS)
        inv_o[...] = jnp.broadcast_to(inv, (TILE, 128))
        for j in range(4):
            cols = slice(j * BLOCK, (j + 1) * BLOCK)
            nf_s[:, cols] = (hg[t, j].astype(F32) * inv * gain_ref[:, cols].astype(F32)).astype(BF16)
        nf = nf_s[...]
        fg = dot_nt(nf, wfg[...])
        fu = dot_nt(nf, wfu[...])
        sig = jax.nn.sigmoid(fg)
        silu = fg * sig
        act = (silu * fu).astype(BF16)
        cg = cg_ref[...]
        for j in range(4):
            pp[t, j] = dot_nn(act, wfd[:, j * BLOCK : (j + 1) * BLOCK]).astype(BF16)
        for which in range(2):
            pair(pp, mp, psem, t, which).start()
        gact = dot_nt(cg, wfd[...])
        gfg = (gact * fu * (sig * (1.0 + fg * (1.0 - sig)))).astype(BF16)
        gfu = (gact * silu).astype(BF16)
        stat = jnp.zeros((TILE, 1), F32)
        for j in range(4):
            rows = slice(j * BLOCK, (j + 1) * BLOCK)
            gj = dot_nn(gfg, wfg[:, rows]) + dot_nn(gfu, wfu[:, rows])
            stat = stat + jnp.sum(gj * nf_s[:, rows].astype(F32), axis=1, keepdims=True)
            pg[t, j] = gj.astype(BF16)
        for which in range(2):
            pair(pg, mg, gsem, t, which).start()
        st_s[pl.ds(t, 1), :] = jnp.broadcast_to(stat, (TILE, 128)).T[0:1, :]
        acc[0:hidden, :] += dot_tn(gfg, nf)
        acc[hidden : 2 * hidden, :] += dot_tn(gfu, nf)
        acc[2 * hidden : 3 * hidden, :] += dot_tn(act, cg)

    @pl.when(i == last + 6)
    def _():
        for n, other in enumerate((mate, cross, far)):
            stats(n, other).start()

    @pl.when(i == last + 7)
    def _():
        used = 3 * hidden // 16

        def unit(r, carry):
            wide_o[r] = acc[pl.ds(pl.multiple_of(r * 16, 16), 16), :].astype(BF16)
            return carry

        lax.fori_loop(0, used, unit, 0)
        if wide_o.shape[0] > used:
            wide_o[used:] = jnp.zeros((wide_o.shape[0] - used,) + wide_o.shape[1:], BF16)
        for n, other in enumerate((mate, cross, far)):
            stats(n, other).wait()
        stat_o[...] = (st_s[...] + st_r[0]) + (st_r[1] + st_r[2])

        def out(t, carry):
            for which in range(2):
                pair(pa, ma, asem, t, which).wait_send()
                pair(pp, mp, psem, t, which).wait_send()
                pair(pg, mg, gsem, t, which).wait_send()
            over(t).wait_send()
            own_cross(t).wait_send()
            own_mate(t).wait_send()
            onward(t).wait_send()
            return carry

        lax.fori_loop(0, tiles, out, 0)


def ffn(x, keep, inc, gg, gain, wout, wfg, wfu, wfd, f, o, u, e, cg):
    rows = x.shape[0]
    tiles = rows // TILE
    hidden, width = wfg.shape
    count = lax.axis_size("seq")
    units = up_to(3 * hidden // 16, count)
    assert tiles <= 8 and hidden % 16 == 0
    ts = functools.partial(tile_spec, tiles)
    ins = (x, keep, inc, gg, gain, wout, wfg, wfu, wfd)
    outs = [
        ((rows, BLOCK), BF16, ts((TILE, BLOCK), 0)),
        ((rows, HV), F32, ts((TILE, HV), 0)),
        ((rows // SPAN, HV, HK), BF16, ts((PER, HV, HK), 0)),
        ((rows, BLOCK), F32, ts((TILE, BLOCK), 3)),
        ((rows, 128), F32, ts((TILE, 128), 6)),
        ((rows, BLOCK), BF16, ts((TILE, BLOCK), 7)),
        ((rows, BLOCK), F32, ts((TILE, BLOCK), 7)),
        ((rows, BLOCK), BF16, ts((TILE, BLOCK), 7)),
        ((rows, BLOCK), F32, ts((TILE, BLOCK), 7)),
        ((8, TILE), F32, whole((8, TILE))),
        ((units, 16, width), BF16, whole((units, 16, width))),
    ]
    tiled = lambda n: pltpu.VMEM((tiles, n, TILE, BLOCK), BF16)
    return pl.pallas_call(
        functools.partial(ffn_kernel, tiles),
        grid=(tiles + 7,),
        out_shape=[jax.ShapeDtypeStruct(s, d) for s, d, _ in outs],
        in_specs=[whole(a.shape) for a in ins]
        + [
            ts((TILE, 128), 0), ts((TILE, 512), 0), ts((PER, HV, HK), 0), ts((1, 8, 128), 0),
            ts((TILE, MODEL_WIDTH), 6),
        ],
        out_specs=[s for _, _, s in outs],
        scratch_shapes=[
            pltpu.VMEM((HV, HK), F32),
            tiled(4), tiled(4), tiled(4), tiled(2), tiled(2), tiled(2),
            pltpu.VMEM((tiles, TILE, BLOCK), BF16),
            pltpu.VMEM((tiles, TILE, BLOCK), BF16),
            pltpu.VMEM((4, TILE, BLOCK), F32),
            tiled(4),
            pltpu.VMEM((TILE, MODEL_WIDTH), BF16),
            pltpu.VMEM((3 * hidden, width), F32),
            pltpu.VMEM((8, TILE), F32),
            pltpu.VMEM((3, 8, TILE), F32),
            pltpu.SemaphoreType.DMA((4, tiles)),
            pltpu.SemaphoreType.DMA((4, tiles)),
            pltpu.SemaphoreType.DMA((4, tiles)),
            pltpu.SemaphoreType.DMA((2, tiles)),
            pltpu.SemaphoreType.DMA((6, tiles)),
            pltpu.SemaphoreType.DMA((2, 3)),
        ],
        compiler_params=pltpu.CompilerParams(
            collective_id=2, has_side_effects=True, vmem_limit_bytes=VMEM_LIMIT,
            dimension_semantics=("arbitrary",),
        ),
        name="ffn",
    )(*ins, f, o, u, e, cg)


LAG = 2


def levels(count):
    bits = count.bit_length() - 1
    assert 1 << bits == count
    return bits


class Sum:
    def __init__(self, count, sources, dest, parts, first, gap, got, sems, lsem):
        self.count = count
        self.bits = levels(count)
        self.sources = sources
        self.dest = dest
        self.parts = parts
        self.first = first
        self.gap = gap
        self.got = got
        self.sems = sems
        self.lsem = lsem

    def where(self, k, level):
        place = lax.axis_index("seq")
        turn = lax.div(lax.rem(k, 4), 3)
        start = 0
        for step in range(level + 1):
            stride = 1 << step
            if step < 2:
                stride = stride + turn * (3 - 2 * stride)
            bit = lax.rem(lax.div(place, stride), 2)
            if step == level:
                return bit, place + stride * (1 - 2 * bit), start
            start = start + bit * (self.count >> (step + 1))

    def own(self, k):
        bit, _, _ = self.where(k, 0)
        half = self.count >> 1
        return pltpu.make_async_copy(
            self.sources[0](k, bit * half, half), self.dest(k, bit * half, half), self.lsem.at[k]
        )

    def scatter(self, k, level, kind):
        bit, partner, start = self.where(k, level)
        half = self.count >> (level + 1)
        if level == 0:
            src = self.sources[kind](k, start + (1 - bit) * half, half)
        else:
            src = self.got[level - 1].at[k, pl.ds((1 - bit) * half, half)]
        return to_seq(src, self.got[level].at[k], self.sems.at[0, level, k], self.sems.at[1, level, k], partner)

    def gather(self, k, level):
        bit, partner, start = self.where(k, level)
        half = self.count >> (level + 1)
        mine = start + bit * half
        ref = self.dest(k, mine, half)
        return to_seq(ref, ref, self.sems.at[2, level, k], self.sems.at[3, level, k], partner)

    def gathered(self, k, level):
        bit, partner, start = self.where(k, level)
        half = self.count >> (level + 1)
        ref = self.dest(k, start + (1 - bit) * half, half)
        return to_seq(ref, ref, self.sems.at[2, level, k], self.sems.at[3, level, k], partner)

    def begin(self, k, kind):
        self.scatter(k, 0, kind).start()
        if kind == 0:
            self.own(k).start()

    def add(self, k, kind, level):
        bit, _, start = self.where(k, level)
        half = self.count >> (level + 1)
        self.scatter(k, level, kind).wait_recv()
        if level == 0 and kind == 0:
            self.own(k).wait()
            mine = self.dest(k, bit * half, half)[...]
        elif level == 0:
            mine = self.sources[1](k, bit * half, half)[...]
        else:
            mine = self.got[level - 1][k, pl.ds(bit * half, half)]
        total = (self.got[level][k].astype(F32) + mine.astype(F32)).astype(BF16)
        if level + 1 < self.bits:
            self.got[level][k] = total
            self.scatter(k, level + 1, kind).start()
        else:
            self.dest(k, start + bit * half, half)[...] = total
            self.gather(k, level).start()

    def pass_on(self, k, kind, level):
        self.gathered(k, level).wait_recv()
        if level > 0:
            self.gather(k, level - 1).start()

    def at(self, j, body):
        @pl.when((j >= 0) & (j < self.first))
        def _():
            body(j, 0)

        @pl.when((j >= self.first + self.gap) & (j < self.parts + self.gap))
        def _():
            body(j - self.gap, 1)

    def step(self, i):
        stages = []
        for level in range(self.bits):
            stages.append(functools.partial(self.add, level=level))
        for level in range(self.bits - 1, -1, -1):
            stages.append(functools.partial(self.pass_on, level=level))
        for s in range(len(stages) - 1, -1, -1):
            self.at(i - LAG * (s + 1), stages[s])
        self.at(i, self.begin)

    def finish(self):
        def one(kind, k, carry):
            for level in range(self.bits):
                self.scatter(k, level, kind).wait_send()
                self.gather(k, level).wait_send()
            return carry

        lax.fori_loop(0, self.first, functools.partial(one, 0), 0)
        lax.fori_loop(self.first, self.parts, functools.partial(one, 1), 0)

    @staticmethod
    def scratch(count, parts, first, unit):
        bits = levels(count)
        return [pltpu.VMEM((parts, count >> (level + 1)) + unit, BF16) for level in range(bits)] + [
            pltpu.SemaphoreType.DMA((4, bits, parts)),
            pltpu.SemaphoreType.DMA((first,)),
        ]


def finish_kernel(fg, fu, fd, mixed, tail, dfg, dfu, dfd, dq, dk, dv, dg, dwo, dr, dup, dag, dffg, db, dgg):
    for src, dst in ((fg, dfg), (fu, dfu), (fd, dfd)):
        dst[...] = src[...].reshape(dst.shape).astype(F32)
    rows = mixed[...].reshape(-1, MODEL_WIDTH).astype(F32)
    dq[...] = rows[:, 0:128]
    dk[...] = rows[:, 128:256]
    dv[...] = rows[:, 256:512]
    dg[...] = rows[:, 512:768]
    dwo[...] = rows[:, 768:1024].T
    dr[...] = tail[0].astype(F32)
    last = tail[1].astype(F32)
    dup[...] = last[:, 0:128]
    dag[...] = last[0:1, 128:384]
    dffg[...] = last[1:2, 128:384]
    db[...] = last[3:4, 128:256]
    dgg[...] = last[2:3, 128:384]


def finish(units, hidden, first):
    width = units.shape[2]
    steps = 4
    per = hidden // 16 // steps
    assert per * steps * 16 == hidden
    rows = MODEL_WIDTH // steps
    wide_spec = lambda n: pl.BlockSpec((per, 16, width), lambda i: (i + n * steps, 0, 0))
    down = lambda r, c: ((r * steps, c), pl.BlockSpec((r, c), lambda i: (i, 0)))
    full = lambda r, c: ((r, c), pl.BlockSpec((r, c), lambda i: (0, 0)))
    outs = [
        down(per * 16, width), down(per * 16, width), down(per * 16, width),
        down(rows, 128), down(rows, 128), down(rows, 256), down(rows, 256),
        ((256, MODEL_WIDTH), pl.BlockSpec((256, rows), lambda i: (0, i))),
        full(RANK, MODEL_WIDTH), full(RANK, 128), full(1, 256), full(1, 256), full(1, 128), full(1, 256),
    ]
    return pl.pallas_call(
        finish_kernel,
        grid=(steps,),
        out_shape=[jax.ShapeDtypeStruct(s, F32) for s, _ in outs],
        in_specs=[
            wide_spec(0), wide_spec(1), wide_spec(2),
            pl.BlockSpec((pl.Element(rows // 16), pl.Element(16), pl.Element(width)), lambda i: (first + i * (rows // 16), 0, 0)),
            pl.BlockSpec((pl.Element(2), pl.Element(16), pl.Element(width)), lambda i: (first + MODEL_WIDTH // 16, 0, 0)),
        ],
        out_specs=[s for _, s in outs],
        compiler_params=pltpu.CompilerParams(
            vmem_limit_bytes=VMEM_LIMIT, dimension_semantics=("arbitrary",)
        ),
        name="finish",
    )(units, units, units, units, units)


def back_kernel(
    tiles, count, gap,
    keep_ref, d_ref, stat_ref, gg_ref, again, fgain, wout, wq, wk, wv, wg, wr, rup,
    wide_in, gsend, psend, x_ref, c_ref, gown, h1, invf, f1, gz_ref, oo_ref, gated, ws1, b1, e1,
    na1, f2, b2, ws2, e2, na, h2, pown, inva,
    gt_o, lo_o, units_o,
    tri, rg, gh, gb, gzs, gw, gqd, gkd, gv, state, sbuf, rbuf,
    gcat, mn, sc, rc, own, st_s, st_r, both, joint, small, held, wide_o, lot,
    gsem, psem, hsem, nsem, csem, tsem, esend, erecv, wsem, jsem, *rest,
):
    i = pl.program_id(0)
    me, mate, cross, far = peers()
    place = lax.axis_index("seq")
    last = tiles - 1
    second = tiles + 3

    def rows_of(t):
        return pl.ds(pl.multiple_of(t * TILE, TILE), TILE)

    def own_cols(ref):
        return ref[:, pl.ds(pl.multiple_of(me * BLOCK, BLOCK), BLOCK)].astype(F32)

    def grads(t):
        return to_head(gsend.at[rows_of(t)], rg.at[t], gsem.at[0, t], gsem.at[1, t], cross)

    def feeds(t):
        return to_head(psend.at[rows_of(t)], rg.at[t], psem.at[0, t], psem.at[1, t], cross)

    def own_mate(t):
        return to_head(gb.at[t, me], gb.at[t, me], hsem.at[0, t], hsem.at[1, t], mate)

    def own_cross(t):
        return to_head(gb.at[t, me], gb.at[t, me], hsem.at[2, t], hsem.at[3, t], cross)

    def onward(t):
        return to_head(gb.at[t, cross], gb.at[t, cross], hsem.at[4, t], hsem.at[5, t], mate)

    def pair(t, which):
        block = mate if which == 0 else far
        return to_head(gb.at[t, block], mn.at[t, which], nsem.at[2 * which, t], nsem.at[2 * which + 1, t], mate)

    def over(t):
        return to_head(sc.at[t], rc.at[t], csem.at[0, t], csem.at[1, t], cross)

    def stats(t, n, other):
        return to_head(st_s.at[t], st_r.at[t, n], tsem.at[0, n, t], tsem.at[1, n, t], other)

    first = wide_in.shape[0] // count
    parts = wide_o.shape[0] // count
    ready = second + tiles

    def early(k, start, n):
        return wide_in.at[pl.ds(k * count + start, n)]

    def late(k, start, n):
        return lot.at[pl.ds((k - first) * count + start, n)]

    def some(k, start, n):
        return wide_o.at[pl.ds(k * count + start, n)]

    wide_sum = Sum(count, (early, late), some, parts, first, gap, rest[:-2], rest[-2], rest[-1])

    @pl.when(i == 0)
    def _():
        greet_head()
        greet_seq(count)
        pl.semaphore_wait(pltpu.get_barrier_semaphore(), 3 + count - 1)
        for n in range(AHEAD):
            grads(last - n).start()
        def weave(r, carry):
            rows = pl.ds(pl.multiple_of(r * 16, 16), 16)
            lot[r, :, 0:128] = wq[rows, :]
            lot[r, :, 128:256] = wk[rows, :]
            lot[r, :, 256:512] = wv[rows, :]
            lot[r, :, 512:768] = wg[rows, :]
            return carry

        lax.fori_loop(0, MODEL_WIDTH // 16, weave, 0)
        r = lax.broadcasted_iota(jnp.int32, (TILE, TILE), 0)
        c = lax.broadcasted_iota(jnp.int32, (TILE, TILE), 1)
        tri[...] = jnp.where(((r >> 6) == (c >> 6)) & (r > c), 1.0, 0.0).astype(BF16)
        state[...] = jnp.zeros_like(state)
        both[...] = jnp.zeros_like(both)
        joint[...] = jnp.zeros_like(joint)
        small[...] = jnp.zeros_like(small)

    @pl.when(i + AHEAD <= last)
    def _():
        grads(last - i - AHEAD).start()

    def share(n, other):
        return to_head(joint, held.at[me], jsem.at[0, n], jsem.at[1, n], other)

    @pl.when(i == ready)
    def _():
        held[me] = joint[...]
        for n, other in enumerate((mate, cross, far)):
            share(n, other).start()

        def copy(r, carry):
            lot[r] = both[pl.ds(pl.multiple_of(r * 16, 16), 16), :].astype(BF16)
            return carry

        lax.fori_loop(0, MODEL_WIDTH // 16, copy, 0)
        used = MODEL_WIDTH // 16 + 2
        if lot.shape[0] > used:
            lot[used:] = jnp.zeros((lot.shape[0] - used,) + lot.shape[1:], BF16)

    @pl.when(i == ready + 3)
    def _():
        for n, other in enumerate((mate, cross, far)):
            to_head(joint, held.at[other], jsem.at[0, n], jsem.at[1, n], other).wait()
        base = MODEL_WIDTH // 16
        sums = (held[0] + held[1]) + (held[2] + held[3])
        lot[base] = sums[0:RANK].astype(BF16)
        lot[base + 1] = jnp.zeros((16, MODEL_WIDTH), BF16)
        small[2:3, 128:384] = sums[16:17, 0:256]
        lot[base + 1, :, 0:512] = small[...].astype(BF16)

    wide_sum.step(i)

    @pl.when((i >= 2) & (i - 2 <= last))
    def _():
        t = last - (i - 2)
        own_cross(t).wait_recv()
        onward(t).start()

    @pl.when(i <= last)
    def _():
        t = last - i
        grads(t).wait_recv()
        gnf = gown[...] + rg[t].astype(F32)
        inv = invf[...][:, 0:1]
        hn = h1[...].astype(BF16).astype(F32) * inv
        row = stat_ref[pl.ds(t, 1), :]
        stat = jnp.broadcast_to(row, (128, TILE)).T[:, 0:1]
        grad = c_ref[...].astype(F32) + inv * (own_cols(fgain) * gnf - hn * (stat / MODEL_WIDTH))
        small[1:2, 128:384] += jnp.sum(gnf * hn, axis=0, keepdims=True)
        gh[t] = grad
        gb[t, me] = grad.astype(BF16)
        own_cross(t).start()
        own_mate(t).start()

    @pl.when((i >= last) & (i - last <= (tiles - 1) // 2))
    def _():
        n = 2 * (i - last)
        feeds(last - n).start()

        @pl.when(n + 1 <= last)
        def _():
            feeds(last - n - 1).start()

    @pl.when((i >= 3) & (i - 3 <= last))
    def _():
        t = last - (i - 3)
        own_mate(t).wait_recv()
        onward(t).wait_recv()
        gt = jnp.zeros((TILE, BLOCK), F32)
        for j in range(4):
            cols = slice(j * BLOCK, (j + 1) * BLOCK)
            gt = gt + dot_nt(gb[t, j], wout[:, cols])
            both[cols, 768:1024] += dot_tn(gb[t, j], gated[...])
        o = oo_ref[...]
        gz = gz_ref[...]
        inv = lax.rsqrt(jnp.mean(o * o, axis=1, keepdims=True) + EPS)
        on = o * inv
        sig = jax.nn.sigmoid(gz)
        gn = gt * (gz * sig)
        joint[16:17, 0:256] += jnp.sum(gn * on, axis=0, keepdims=True)
        gain = gg_ref[...].astype(F32)
        ggz = (gt * on * gain * (sig * (1.0 + gz * (1.0 - sig)))).astype(BF16)
        gzs[t] = ggz
        both[:, 512:768] += dot_tn(na1[...], ggz)
        p = gn * gain
        go = (inv * (p - on * jnp.mean(p * on, axis=1, keepdims=True))).astype(BF16)
        qd = f1[:, 0:128].astype(BF16)
        kd = f1[:, 128:256].astype(BF16)
        v = b1[:, 0:256]
        causal, _ = span_masks(TILE, TILE)
        ga = jnp.where(causal, dot_nt(go, v), 0.0).astype(BF16)
        gqd[t] = dot_nn(ga, kd)
        gkd[t] = dot_tn(ga, qd)
        gv[t] = dot_tn(b1[:, 256:512], go)
        for c in range(PER - 1, -1, -1):
            rows = slice(c * SPAN, (c + 1) * SPAN)
            gqd[t, rows, :] += dot_nn(go[rows], ws1[c])
            fresh = dot_tn(go[rows], qd[rows])
            gw[t * PER + c] = fresh
            through = keep_ref[t, c : c + 1, :] * e1[0, c : c + 1, :]
            state[...] = through * (fresh + state[...])

    @pl.when(i == last + 3)
    def _():
        sbuf[...] = jnp.zeros_like(sbuf)
        sbuf[0:HV, :] = state[...].astype(BF16)
        d = d_ref[...]
        hi = d.astype(BF16).astype(F32)
        first = lax.broadcasted_iota(jnp.int32, (16, 128), 0) < 8
        both = jnp.where(first, jnp.concatenate([hi, hi], axis=0), jnp.concatenate([d - hi, d - hi], axis=0))
        sbuf[HV : HV + 16, :] = both.astype(BF16)

        def send(p, carry):
            to_seq(sbuf, rbuf.at[place], esend.at[p], erecv.at[place], p).start()
            return carry

        lax.fori_loop(0, place, send, 0)

    @pl.when(i == second)
    def _():
        def free(t, carry):
            own_cross(t).wait_send()
            own_mate(t).wait_send()
            onward(t).wait_send()
            return carry

        lax.fori_loop(0, tiles, free, 0)
        state[...] = jnp.zeros_like(state)

        def join(n, carry):
            p = count - 1 - n
            to_seq(sbuf, rbuf.at[p], esend.at[p], erecv.at[p], place).wait_recv()
            got = rbuf[p].astype(F32)
            d = got[HV : HV + 1] + got[HV + 8 : HV + 9]
            state[...] = got[0:HV] + d * state[...]
            return carry

        lax.fori_loop(0, count - 1 - place, join, 0)

    @pl.when((i >= second + 3) & (i - second - 3 <= last))
    def _():
        t = last - (i - second - 3)
        over(t).wait_recv()
        for n, other in enumerate((mate, cross, far)):
            stats(t, n, other).wait_recv()
        gna = own[lax.rem(t, 3)] + rc[t].astype(F32)
        inv = inva[...][:, 0:1]
        xn = x_ref[...].astype(F32) * inv
        row = (st_s[t] + st_r[t, 0]) + (st_r[t, 1] + st_r[t, 2])
        stat = jnp.broadcast_to(row[0:1], (128, TILE)).T[:, 0:1]
        gt_o[...] = gh[t] + inv * (own_cols(again) * gna - xn * (stat / MODEL_WIDTH))
        small[0:1, 128:384] += jnp.sum(gna * xn, axis=0, keepdims=True)

    @pl.when((i >= second + 1) & (i - second - 1 <= last))
    def _():
        t = last - (i - second - 1)
        pair(t, 0).wait_recv()
        pair(t, 1).wait_recv()
        sc[t] = (gb[t, cross].astype(F32) + mn[t, 1].astype(F32)).astype(BF16)
        over(t).start()
        own[lax.rem(t, 3)] = gb[t, me].astype(F32) + mn[t, 0].astype(F32)

    @pl.when((i >= second) & (i - second <= last))
    def _():
        t = last - (i - second)
        qf = f2[:, 0:128]
        kf = f2[:, 128:256]
        kd = kf.astype(BF16)
        pieces = [None] * PER
        for c in range(PER - 1, -1, -1):
            rows = slice(c * SPAN, (c + 1) * SPAN)
            low = state[...].astype(BF16)
            gkd[t, rows, :] += dot_nn(b2[rows, 0:256], low)
            gv[t, rows, :] += dot_nt(kd[rows], low)
            ge = gw[t * PER + c] + state[...]
            pieces[c] = jnp.broadcast_to(jnp.sum(ge * ws2[c].astype(F32), axis=0, keepdims=True), (SPAN, HK))
            state[...] = (keep_ref[t, c : c + 1, :] * e2[0, c : c + 1, :]) * ge
        gq = gqd[t]
        gk = gkd[t]
        diff = gq * qf - gk * kf
        gg = jnp.concatenate(pieces, axis=0) - fold(dot_nn(tri[...], three(diff)))
        glogit = gg * f2[:, 512:640]
        small[3:4, 128:256] += jnp.sum(glogit, axis=0, keepdims=True)
        hi = glogit.astype(BF16)
        lo = (glogit - hi.astype(F32)).astype(BF16)
        glr = dot_nt(hi, rup[...]) + dot_nt(lo, rup[...])
        lr = b2[:, 512 : 512 + RANK]
        small[:, 0:128] += dot_tn(lr, hi) + dot_tn(lr, lo)
        glr = glr.astype(BF16)
        joint[0:RANK, :] += dot_tn(glr, na[...])
        gcat[:, 0:128] = (gq * f2[:, 256:384]).astype(BF16)
        gcat[:, 128:256] = (gk * f2[:, 384:512]).astype(BF16)
        gcat[:, 256:512] = gv[t].astype(BF16)
        gcat[:, 512:768] = gzs[t]
        g = gcat[...]
        stat = jnp.zeros((TILE, 1), F32)
        for j in range(4):
            cols = slice(j * BLOCK, (j + 1) * BLOCK)
            gj = dot_nt(g, lot[16 * j : 16 * (j + 1), :, 0:768].reshape(BLOCK, 768)) + dot_nn(glr, wr[:, cols])
            stat = stat + jnp.sum(gj * na[:, cols].astype(F32), axis=1, keepdims=True)
            gb[t, j] = gj.astype(BF16)
        pair(t, 1).start()
        pair(t, 0).start()
        st_s[t] = jnp.broadcast_to(stat, (TILE, 128)).T[0:8, :]
        for n, other in enumerate((mate, cross, far)):
            stats(t, n, other).start()
        both[:, 0:512] += dot_tn(na[...], g[:, 0:512])

    @pl.when((i >= second) & (i - second <= last))
    def _():
        t = last - (i - second)
        feeds(t).wait_recv()
        lo_o[...] = (h2[...] + (pown[...] + rg[t].astype(F32))).astype(BF16)

    drained = first + 2 * levels(count) * LAG
    head_units = pl.ds(0, first * count)
    tail_units = pl.ds(first * count, (parts - first) * count)
    head_copy = pltpu.make_async_copy(wide_o.at[head_units], units_o.at[head_units], wsem.at[0])
    tail_copy = pltpu.make_async_copy(wide_o.at[tail_units], units_o.at[tail_units], wsem.at[1])

    @pl.when(i == drained)
    def _():
        head_copy.start()

    @pl.when(i == pl.num_programs(0) - 1)
    def _():
        tail_copy.start()
        wide_sum.finish()
        tail_copy.wait()
        head_copy.wait()

        def sent(p, carry):
            to_seq(sbuf, rbuf.at[place], esend.at[p], erecv.at[place], p).wait_send()
            return carry

        lax.fori_loop(0, place, sent, 0)

        def out(t, carry):
            grads(t).wait_send()
            feeds(t).wait_send()
            pair(t, 0).wait_send()
            pair(t, 1).wait_send()
            over(t).wait_send()
            for n, other in enumerate((mate, cross, far)):
                stats(t, n, other).wait_send()
            return carry

        lax.fori_loop(0, tiles, out, 0)


def back(fixed, wide, gsend, psend, x, cot, gown, h, invf, f, o, oo, gated, ws, b, e, na, pown, inva):
    rows = h.shape[0]
    tiles = rows // TILE
    count = lax.axis_size("seq")
    second = tiles + 3
    width = MODEL_WIDTH
    first = wide.shape[0] // count
    extra = up_to(width // 16 + 2, count)
    units = wide.shape[0] + extra
    parts = units // count
    gap = max(0, second + tiles - first, second + tiles + 3 - (first + extra // count - 1))
    steps = parts + gap + 2 * levels(count) * LAG + 1
    assert first + gap + extra // count - 1 >= second + tiles + 3
    ts = functools.partial(tile_spec, tiles, back=True)
    outs = [
        ((rows, BLOCK), F32, ts((TILE, BLOCK), second + 3)),
        ((rows, BLOCK), BF16, ts((TILE, BLOCK), second)),
        ((units, 16, width), BF16, pl.BlockSpec(memory_space=pl.ANY)),
    ]
    tiled = lambda n: pltpu.VMEM((tiles, n, TILE, BLOCK), BF16)
    flat = lambda n, d: pltpu.VMEM((tiles, TILE, n), d)
    return pl.pallas_call(
        functools.partial(back_kernel, tiles, count, gap),
        grid=(max(second + tiles + 3, steps),),
        out_shape=[jax.ShapeDtypeStruct(s, d) for s, d, _ in outs],
        in_specs=[whole(a.shape) for a in fixed]
        + [
            pl.BlockSpec(memory_space=pl.ANY), pl.BlockSpec(memory_space=pl.ANY), pl.BlockSpec(memory_space=pl.ANY),
            ts((TILE, BLOCK), second + 3), ts((TILE, BLOCK), 0),
            ts((TILE, BLOCK), 0), ts((TILE, BLOCK), 0), ts((TILE, 128), 0),
            ts((TILE, 256), 3), ts((TILE, 256), 3), ts((TILE, 256), 3), ts((TILE, 256), 3),
            ts((PER, HV, HK), 3), ts((TILE, 640), 3), ts((1, 8, 128), 3), ts((TILE, width), 3),
            ts((TILE, 640), second), ts((TILE, 640), second), ts((PER, HV, HK), second), ts((1, 8, 128), second),
            ts((TILE, width), second), ts((TILE, BLOCK), second), ts((TILE, BLOCK), second),
            ts((TILE, 128), second + 3),
        ],
        out_specs=[s for _, _, s in outs],
        scratch_shapes=[
            pltpu.VMEM((TILE, TILE), BF16),
            flat(BLOCK, BF16), flat(BLOCK, F32),
            tiled(4),
            flat(BLOCK, BF16),
            pltpu.VMEM((rows // SPAN, HV, HK), F32),
            flat(HK, F32), flat(HK, F32), flat(HV, F32),
            pltpu.VMEM((HV, HK), F32),
            pltpu.VMEM((HV + 16, HK), BF16),
            pltpu.VMEM((count, HV + 16, HK), BF16),
            pltpu.VMEM((TILE, 768), BF16),
            tiled(2), flat(BLOCK, BF16), flat(BLOCK, BF16),
            pltpu.VMEM((3, TILE, BLOCK), F32),
            pltpu.VMEM((tiles, 8, TILE), F32),
            pltpu.VMEM((tiles, 3, 8, TILE), F32),
            pltpu.VMEM((width, width), F32),
            pltpu.VMEM((24, width), F32),
            pltpu.VMEM((16, 512), F32),
            pltpu.VMEM((4, 24, width), F32),
            pltpu.VMEM((units, 16, width), BF16),
            pltpu.VMEM((extra, 16, width), BF16),
            pltpu.SemaphoreType.DMA((2, tiles)),
            pltpu.SemaphoreType.DMA((2, tiles)),
            pltpu.SemaphoreType.DMA((6, tiles)),
            pltpu.SemaphoreType.DMA((4, tiles)),
            pltpu.SemaphoreType.DMA((2, tiles)),
            pltpu.SemaphoreType.DMA((2, 3, tiles)),
            pltpu.SemaphoreType.DMA((count,)),
            pltpu.SemaphoreType.DMA((count,)),
            pltpu.SemaphoreType.DMA((2,)),
            pltpu.SemaphoreType.DMA((2, 3)),
        ]
        + Sum.scratch(count, parts, first, wide.shape[1:]),
        compiler_params=pltpu.CompilerParams(
            collective_id=3, has_side_effects=True, vmem_limit_bytes=VMEM_LIMIT,
            dimension_semantics=("arbitrary",),
        ),
        name="back",
    )(*fixed, wide, gsend, psend, x, cot, gown, h, invf, f, o, oo, gated, ws, b, e, na, f, b, ws, e, na, h, pown, inva)


def shards(
    tokens,
    row_starts,
    attn_gain,
    query_weight,
    key_weight,
    value_weight,
    gate_weight,
    rank_down,
    rank_up,
    rank_bias,
    group_gain,
    out_weight,
    feed_gain,
    feed_gate,
    feed_up,
    feed_down,
    cotangent,
):
    rows = tokens.shape[0]
    tiles = rows // TILE
    spans = rows // SPAN
    span_ids = lax.axis_index("seq") * spans + jnp.arange(spans, dtype=jnp.int32)
    resets = jnp.any((row_starts // SPAN)[None, :] == span_ids[:, None], axis=1).astype(F32)
    keep = jnp.pad((1.0 - resets).reshape(tiles, PER, 1), ((0, 0), (0, 8 - PER), (0, 0)))
    keep = jnp.broadcast_to(keep, (tiles, 8, 128))
    weights = (
        query_weight[0], key_weight[0], value_weight[0], gate_weight[0], jnp.swapaxes(rank_down[0], 0, 1), rank_up[0]
    )
    na, cg, inva, f, b, o, u, e, inc, dec = front(tokens, cotangent, keep, attn_gain, *weights, rank_bias)
    gated, oo, ws, h, invf, gsend, gown, psend, pown, stat, wide = ffn(
        tokens, keep, inc, group_gain, feed_gain, out_weight[0], jnp.swapaxes(feed_gate[0], 0, 1),
        jnp.swapaxes(feed_up[0], 0, 1), feed_down[0], f, o, u, e, cg,
    )
    fixed = (
        keep, dec, stat, group_gain, attn_gain, feed_gain, out_weight[0],
    ) + weights
    grad_tokens, layer_out, units = back(fixed, wide, gsend, psend, tokens, cotangent, gown, h, invf, f, o, oo, gated, ws, b, e, na, pown, inva)
    dfg, dfu, dfd, dq, dk, dv, dg, dwo, dr, dup, dag, dffg, db, dgg = finish(units, feed_gate.shape[2], wide.shape[0])
    dfg, dfu, dr = (jnp.swapaxes(a, 0, 1) for a in (dfg, dfu, dr))
    grads = (dag, dq[None], dk[None], dv[None], dg[None], dr[None], dup[None], db, dgg, dwo[None], dffg, dfg[None], dfu[None], dfd[None])
    return (layer_out, grad_tokens) + grads


def solution(mesh):
    placed = (
        P("seq", "head"),
        P(),
        P(),
        P(None, None, "head"),
        P(None, None, "head"),
        P(None, None, "head"),
        P(None, None, "head"),
        P(),
        P(None, None, "head"),
        P(None, "head"),
        P(),
        P(None, "head", None),
        P(),
        P(None, None, "head"),
        P(None, None, "head"),
        P(None, "head", None),
        P("seq", "head"),
    )
    return jax.shard_map(
        shards,
        mesh=mesh,
        in_specs=placed,
        out_specs=(
            P("seq", "head"),
            P("seq", "head"),
            P(None, "head"),
            P(None, None, "head"),
            P(None, None, "head"),
            P(None, None, "head"),
            P(None, None, "head"),
            P(),
            P(None, None, "head"),
            P(None, "head"),
            P(),
            P(None, "head", None),
            P(None, "head"),
            P(None, None, "head"),
            P(None, None, "head"),
            P(None, "head", None),
        ),
        check_vma=False,
    )
```

```python
import functools

import jax
import jax.numpy as jnp
from jax import lax
from jax.experimental import pallas as pl
from jax.experimental.pallas import tpu as pltpu
from jax.sharding import PartitionSpec as P

MODEL_WIDTH = 1024
HK = 128
HV = 256
SPAN = 64
RANK = 16
EPS = 1e-06
GATE_NORM = 16.0
TILE = 256
PER = TILE // SPAN
BLOCK = 256
AHEAD = 3
F32 = jnp.float32
BF16 = jnp.bfloat16
MESH = pl.DeviceIdType.MESH
VMEM_LIMIT = 62 * 1024 * 1024


def dot_nn(a, b):
    return jnp.dot(a, b, preferred_element_type=F32)


def dot_nt(a, b):
    return lax.dot_general(a, b, (((1,), (1,)), ((), ())), preferred_element_type=F32)


def dot_tn(a, b):
    return lax.dot_general(a, b, (((0,), (0,)), ((), ())), preferred_element_type=F32)


def peers():
    me = lax.axis_index("head")
    mate = me + 1 - 2 * lax.rem(me, 2)
    cross = lax.rem(me + 2, 4)
    far = cross + 1 - 2 * lax.rem(cross, 2)
    return me, mate, cross, far


def greet_head():
    _, mate, cross, far = peers()
    barrier = pltpu.get_barrier_semaphore()
    for other in (mate, cross, far):
        pl.semaphore_signal(barrier, inc=1, device_id={"head": other}, device_id_type=MESH)


def greet_seq(count):
    place = lax.axis_index("seq")
    barrier = pltpu.get_barrier_semaphore()

    def one(step, carry):
        other = lax.rem(place + step, count)
        pl.semaphore_signal(barrier, inc=1, device_id={"seq": other}, device_id_type=MESH)
        return carry

    lax.fori_loop(1, count, one, 0)


def to_head(src, dst, send, recv, other):
    return pltpu.make_async_remote_copy(
        src_ref=src, dst_ref=dst, send_sem=send, recv_sem=recv,
        device_id={"head": other}, device_id_type=MESH,
    )


def to_seq(src, dst, send, recv, other):
    return pltpu.make_async_remote_copy(
        src_ref=src, dst_ref=dst, send_sem=send, recv_sem=recv,
        device_id={"seq": other}, device_id_type=MESH,
    )


def span_masks(rows, cols):
    r = lax.broadcasted_iota(jnp.int32, (rows, cols), 0)
    c = lax.broadcasted_iota(jnp.int32, (rows, cols), 1)
    same = (r >> 6) == (c >> 6)
    return same & (r >= c), same


def three(x):
    a = x.astype(BF16)
    rest = x - a.astype(F32)
    b = rest.astype(BF16)
    c = (rest - b.astype(F32)).astype(BF16)
    return jnp.concatenate([a, b, c], axis=1)


def fold(x):
    w = x.shape[1] // 3
    return x[:, :w] + x[:, w : 2 * w] + x[:, 2 * w :]


def front_kernel(
    tiles, count,
    x_ref, c_ref, keep_ref, gain_ref, wq, wk, wv, wg, wr, rup, bias_ref,
    na_o, cg_o, inv_o, f_o, b_o, o_o, u_o, e_o, in_o, d_o,
    grid_buf, wcat, tri, state, decay, sbuf, rbuf, sems, esend, erecv,
):
    i = pl.program_id(0)
    me, mate, cross, far = peers()
    place = lax.axis_index("seq")
    total = 2 * tiles

    def own_mate(m):
        return to_head(grid_buf.at[m, me], grid_buf.at[m, me], sems.at[0, m], sems.at[1, m], mate)

    def own_cross(m):
        return to_head(grid_buf.at[m, me], grid_buf.at[m, me], sems.at[2, m], sems.at[3, m], cross)

    def onward(m):
        return to_head(grid_buf.at[m, cross], grid_buf.at[m, cross], sems.at[4, m], sems.at[5, m], mate)

    @pl.when(i == 0)
    def _():
        greet_head()
        greet_seq(count)

        def own(m, carry):
            rows = pl.ds(pl.multiple_of(m * TILE, TILE), TILE)
            grid_buf[m, me] = x_ref[rows, :]
            grid_buf[m + tiles, me] = c_ref[rows, :]
            return carry

        lax.fori_loop(0, tiles, own, 0)
        pl.semaphore_wait(pltpu.get_barrier_semaphore(), 3 + count - 1)
        for m in range(AHEAD):
            own_cross(m).start()
            own_mate(m).start()
        wcat[:, 0:128] = wq[...]
        wcat[:, 128:256] = wk[...]
        wcat[:, 256:512] = wv[...]
        wcat[:, 512:768] = wg[...]
        causal, same = span_masks(TILE, TILE)
        tri[0:TILE, :] = jnp.where(causal, 1.0, 0.0).astype(BF16)
        tri[TILE : 2 * TILE, :] = jnp.where(same, 1.0, 0.0).astype(BF16)
        state[...] = jnp.zeros_like(state)
        decay[...] = jnp.ones_like(decay)

    @pl.when(i < total)
    def _():
        own_cross(i).wait_recv()
        onward(i).start()

    @pl.when(i + AHEAD < total)
    def _():
        own_cross(i + AHEAD).start()
        own_mate(i + AHEAD).start()

    @pl.when(i >= 1)
    def _():
        own_mate(i - 1).wait_recv()
        onward(i - 1).wait_recv()

    @pl.when((i >= 1) & (i <= tiles))
    def _():
        m = i - 1
        squares = jnp.zeros((TILE, 1), F32)
        for j in range(4):
            xj = grid_buf[m, j].astype(F32)
            squares = squares + jnp.sum(xj * xj, axis=1, keepdims=True)
        inv = lax.rsqrt(squares / MODEL_WIDTH + EPS)
        inv_o[...] = jnp.broadcast_to(inv, (TILE, 128))
        for j in range(4):
            cols = slice(j * BLOCK, (j + 1) * BLOCK)
            xj = grid_buf[m, j].astype(F32)
            na_o[:, cols] = (xj * inv * gain_ref[:, cols].astype(F32)).astype(BF16)
        proj = dot_nn(na_o[...], wcat[...])
        q = proj[:, 0:128]
        k = proj[:, 128:256]
        v = proj[:, 256:512].astype(BF16)
        o_o[:, 0:256] = proj[:, 512:768]
        lr = dot_nt(na_o[...], wr[...]).astype(BF16)
        z = dot_nn(lr, rup[...]) + bias_ref[...].astype(F32)
        g = (jnp.minimum(z, 0.0) - jnp.log1p(jnp.exp(-jnp.abs(z)))) / GATE_NORM
        sums = fold(dot_nn(tri[...], three(g)))
        b = sums[0:TILE]
        e = sums[TILE : 2 * TILE]
        fq = (HK ** (-0.5)) * jnp.exp(b - e)
        fk = jnp.exp(e - b)
        qf = q * fq
        kf = k * fk
        f_o[:, 0:128] = qf
        f_o[:, 128:256] = kf
        f_o[:, 256:384] = fq
        f_o[:, 384:512] = fk
        f_o[:, 512:640] = jax.nn.sigmoid(-z) / GATE_NORM
        qd = qf.astype(BF16)
        kd = kf.astype(BF16)
        causal, _ = span_masks(TILE, TILE)
        scores = jnp.where(causal, dot_nt(qd, kd), 0.0).astype(BF16)
        b_o[:, 0:256] = v
        b_o[:, 256:512] = scores
        b_o[:, 512 : 512 + RANK] = lr
        o_o[:, 256:512] = dot_nn(scores, v)
        for c in range(PER):
            rows = slice(c * SPAN, (c + 1) * SPAN)
            update = dot_tn(v[rows], kd[rows])
            u_o[c] = update
            ee = jnp.exp(e[c * SPAN : c * SPAN + 1])
            e_o[0, c : c + 1, :] = ee
            through = keep_ref[m, c : c + 1, :] * ee
            state[...] = through * state[...] + update
            decay[...] = through * decay[...]

    @pl.when(i == tiles)
    def _():
        d_o[...] = decay[...]
        sbuf[0:HV, :] = state[...].astype(BF16)
        d = decay[...]
        hi = d.astype(BF16).astype(F32)
        first = lax.broadcasted_iota(jnp.int32, (16, 128), 0) < 8
        both = jnp.where(first, jnp.concatenate([hi, hi], axis=0), jnp.concatenate([d - hi, d - hi], axis=0))
        sbuf[HV : HV + 16, :] = both.astype(BF16)

        def send(p, carry):
            to_seq(sbuf, rbuf.at[place], esend.at[p], erecv.at[place], p).start()
            return carry

        lax.fori_loop(place + 1, count, send, 0)

    @pl.when(i > tiles)
    def _():
        m = i - 1
        for j in range(4):
            cg_o[:, j * BLOCK : (j + 1) * BLOCK] = grid_buf[m, j]

    @pl.when(i == total)
    def _():
        in_o[...] = jnp.zeros_like(in_o)

        def join(p, carry):
            to_seq(sbuf, rbuf.at[p], esend.at[p], erecv.at[p], place).wait_recv()
            got = rbuf[p].astype(F32)
            d = got[HV : HV + 1] + got[HV + 8 : HV + 9]
            in_o[...] = got[0:HV] + d * in_o[...]
            return carry

        lax.fori_loop(0, place, join, 0)

        def sent(p, carry):
            to_seq(sbuf, rbuf.at[place], esend.at[p], erecv.at[place], p).wait_send()
            return carry

        lax.fori_loop(place + 1, count, sent, 0)

        def out(m, carry):
            own_cross(m).wait_send()
            own_mate(m).wait_send()
            onward(m).wait_send()
            return carry

        lax.fori_loop(0, total, out, 0)


def whole(shape):
    zeros = (0,) * len(shape)
    return pl.BlockSpec(shape, lambda i: zeros, pipeline_mode=pl.Buffered(1))


def front(x, cot, keep, gain, wq, wk, wv, wg, wr, rup, bias):
    rows = x.shape[0]
    tiles = rows // TILE
    count = lax.axis_size("seq")

    def tile(shape, lag, axis0=True):
        rest = (0,) * (len(shape) - 1)
        return pl.BlockSpec(shape, lambda i: (jnp.clip(i - lag, 0, tiles - 1),) + rest)

    ins = (x, cot, keep, gain, wq, wk, wv, wg, wr, rup, bias)
    outs = [
        ((rows, MODEL_WIDTH), BF16, tile((TILE, MODEL_WIDTH), 1)),
        ((rows, MODEL_WIDTH), BF16, tile((TILE, MODEL_WIDTH), 1 + tiles)),
        ((rows, 128), F32, tile((TILE, 128), 1)),
        ((rows, 640), F32, tile((TILE, 640), 1)),
        ((rows, 640), BF16, tile((TILE, 640), 1)),
        ((rows, 512), F32, tile((TILE, 512), 1)),
        ((rows // SPAN, HV, HK), F32, tile((PER, HV, HK), 1)),
        ((tiles, 8, 128), F32, tile((1, 8, 128), 1)),
        ((HV, HK), F32, whole((HV, HK))),
        ((8, 128), F32, whole((8, 128))),
    ]
    return pl.pallas_call(
        functools.partial(front_kernel, tiles, count),
        grid=(2 * tiles + 1,),
        out_shape=[jax.ShapeDtypeStruct(s, d) for s, d, _ in outs],
        in_specs=[whole(a.shape) for a in ins],
        out_specs=[s for _, _, s in outs],
        scratch_shapes=[
            pltpu.VMEM((2 * tiles, 4, TILE, BLOCK), BF16),
            pltpu.VMEM((MODEL_WIDTH, 768), BF16),
            pltpu.VMEM((2 * TILE, TILE), BF16),
            pltpu.VMEM((HV, HK), F32),
            pltpu.VMEM((8, 128), F32),
            pltpu.VMEM((HV + 16, HK), BF16),
            pltpu.VMEM((count, HV + 16, HK), BF16),
            pltpu.SemaphoreType.DMA((6, 2 * tiles)),
            pltpu.SemaphoreType.DMA((count,)),
            pltpu.SemaphoreType.DMA((count,)),
        ],
        compiler_params=pltpu.CompilerParams(
            collective_id=1, has_side_effects=True, vmem_limit_bytes=VMEM_LIMIT,
            dimension_semantics=("arbitrary",),
        ),
        name="front",
    )(*ins)


def tile_spec(tiles, shape, lag, back=False, col=0):
    rest = (0,) * (len(shape) - 2) + (col,)

    def index(i):
        t = jnp.clip(i - lag, 0, tiles - 1)
        return ((tiles - 1 - t) if back else t,) + rest

    return pl.BlockSpec(shape, index)


def up_to(n, step):
    return (n + step - 1) // step * step


def ffn_kernel(
    tiles,
    x_ref, keep_ref, in_ref, gg_ref, gain_ref, wout, wfg, wfu, wfd,
    f_ref, o_ref, u_ref, e_ref, cg_ref,
    gated_o, oo_o, ws_o, h_o, inv_o, gsend_o, gown_o, psend_o, pown_o, stat_o, wide_o,
    state, pa, pp, pg, ma, mp, mg, sc, rc, own, hg, nf_s, acc, st_s, st_r,
    asem, psem, gsem, csem, hsem, tsem,
):
    i = pl.program_id(0)
    me, mate, cross, far = peers()
    last = tiles - 1
    hidden = wfg.shape[0]

    def pair(buf, got, sem, t, which):
        block = mate if which == 0 else far
        return to_head(buf.at[t, block], got.at[t, which], sem.at[2 * which, t], sem.at[2 * which + 1, t], mate)

    def over(t):
        return to_head(sc.at[t], rc.at[t], csem.at[0, t], csem.at[1, t], cross)

    def own_mate(t):
        return to_head(hg.at[t, me], hg.at[t, me], hsem.at[0, t], hsem.at[1, t], mate)

    def own_cross(t):
        return to_head(hg.at[t, me], hg.at[t, me], hsem.at[2, t], hsem.at[3, t], cross)

    def onward(t):
        return to_head(hg.at[t, cross], hg.at[t, cross], hsem.at[4, t], hsem.at[5, t], mate)

    def stats(n, other):
        return to_head(st_s, st_r.at[n], tsem.at[0, n], tsem.at[1, n], other)

    @pl.when(i == 0)
    def _():
        greet_head()
        state[...] = in_ref[...]
        acc[...] = jnp.zeros_like(acc)
        st_s[...] = jnp.zeros_like(st_s)
        pl.semaphore_wait(pltpu.get_barrier_semaphore(), 3)

    @pl.when((i >= 5) & (i - 5 <= last))
    def _():
        t = i - 5
        own_cross(t).wait_recv()
        onward(t).start()

    @pl.when((i >= 3) & (i - 3 <= last))
    def _():
        t = i - 3
        over(t).wait_recv()
        rows = pl.ds(pl.multiple_of(t * TILE, TILE), TILE)
        h = x_ref[rows, :].astype(F32) + (own[lax.rem(t, 4)] + rc[t].astype(F32))
        h_o[...] = h
        hg[t, me] = h.astype(BF16)
        own_cross(t).start()
        own_mate(t).start()

    @pl.when((i >= 1) & (i - 1 <= last))
    def _():
        t = i - 1
        pair(pa, ma, asem, t, 0).wait_recv()
        pair(pa, ma, asem, t, 1).wait_recv()
        sc[t] = (pa[t, cross].astype(F32) + ma[t, 1].astype(F32)).astype(BF16)
        over(t).start()
        own[lax.rem(t, 4)] = pa[t, me].astype(F32) + ma[t, 0].astype(F32)

    @pl.when(i <= last)
    def _():
        t = i
        for c in range(PER):
            rows = slice(c * SPAN, (c + 1) * SPAN)
            scaled = (keep_ref[t, c : c + 1, :] * e_ref[0, c : c + 1, :]) * state[...]
            low = scaled.astype(BF16)
            ws_o[c] = low
            state[...] = scaled + u_ref[c]
            oo_o[rows, :] = o_ref[rows, 256:512] + dot_nt(f_ref[rows, :].astype(BF16), low)
        o = oo_o[...]
        gz = o_ref[:, 0:256]
        inv = lax.rsqrt(jnp.mean(o * o, axis=1, keepdims=True) + EPS)
        gated = (o * inv * gg_ref[...].astype(F32) * (gz * jax.nn.sigmoid(gz))).astype(BF16)
        gated_o[...] = gated
        for j in range(4):
            pa[t, j] = dot_nn(gated, wout[:, j * BLOCK : (j + 1) * BLOCK]).astype(BF16)
        pair(pa, ma, asem, t, 1).start()
        pair(pa, ma, asem, t, 0).start()

    @pl.when((i >= 7) & (i - 7 <= last))
    def _():
        t = i - 7
        for which in range(2):
            pair(pp, mp, psem, t, which).wait_recv()
            pair(pg, mg, gsem, t, which).wait_recv()
        psend_o[...] = (pp[t, cross].astype(F32) + mp[t, 1].astype(F32)).astype(BF16)
        pown_o[...] = pp[t, me].astype(F32) + mp[t, 0].astype(F32)
        gsend_o[...] = (pg[t, cross].astype(F32) + mg[t, 1].astype(F32)).astype(BF16)
        gown_o[...] = pg[t, me].astype(F32) + mg[t, 0].astype(F32)

    @pl.when((i >= 6) & (i - 6 <= last))
    def _():
        t = i - 6
        own_mate(t).wait_recv()
        onward(t).wait_recv()
        squares = jnp.zeros((TILE, 1), F32)
        for j in range(4):
            hj = hg[t, j].astype(F32)
            squares = squares + jnp.sum(hj * hj, axis=1, keepdims=True)
        inv = lax.rsqrt(squares / MODEL_WIDTH + EPS)
        inv_o[...] = jnp.broadcast_to(inv, (TILE, 128))
        for j in range(4):
            cols = slice(j * BLOCK, (j + 1) * BLOCK)
            nf_s[:, cols] = (hg[t, j].astype(F32) * inv * gain_ref[:, cols].astype(F32)).astype(BF16)
        nf = nf_s[...]
        fg = dot_nt(nf, wfg[...])
        fu = dot_nt(nf, wfu[...])
        sig = jax.nn.sigmoid(fg)
        silu = fg * sig
        act = (silu * fu).astype(BF16)
        cg = cg_ref[...]
        for j in range(4):
            pp[t, j] = dot_nn(act, wfd[:, j * BLOCK : (j + 1) * BLOCK]).astype(BF16)
        for which in range(2):
            pair(pp, mp, psem, t, which).start()
        gact = dot_nt(cg, wfd[...])
        gfg = (gact * fu * (sig * (1.0 + fg * (1.0 - sig)))).astype(BF16)
        gfu = (gact * silu).astype(BF16)
        stat = jnp.zeros((TILE, 1), F32)
        for j in range(4):
            rows = slice(j * BLOCK, (j + 1) * BLOCK)
            gj = dot_nn(gfg, wfg[:, rows]) + dot_nn(gfu, wfu[:, rows])
            stat = stat + jnp.sum(gj * nf_s[:, rows].astype(F32), axis=1, keepdims=True)
            pg[t, j] = gj.astype(BF16)
        for which in range(2):
            pair(pg, mg, gsem, t, which).start()
        st_s[pl.ds(t, 1), :] = jnp.broadcast_to(stat, (TILE, 128)).T[0:1, :]
        acc[0:hidden, :] += dot_tn(gfg, nf)
        acc[hidden : 2 * hidden, :] += dot_tn(gfu, nf)
        acc[2 * hidden : 3 * hidden, :] += dot_tn(act, cg)

    @pl.when(i == last + 6)
    def _():
        for n, other in enumerate((mate, cross, far)):
            stats(n, other).start()

    @pl.when(i == last + 7)
    def _():
        used = 3 * hidden // 16

        def unit(r, carry):
            wide_o[r] = acc[pl.ds(pl.multiple_of(r * 16, 16), 16), :].astype(BF16)
            return carry

        lax.fori_loop(0, used, unit, 0)
        for n, other in enumerate((mate, cross, far)):
            stats(n, other).wait()
        stat_o[...] = (st_s[...] + st_r[0]) + (st_r[1] + st_r[2])

        def out(t, carry):
            for which in range(2):
                pair(pa, ma, asem, t, which).wait_send()
                pair(pp, mp, psem, t, which).wait_send()
                pair(pg, mg, gsem, t, which).wait_send()
            over(t).wait_send()
            own_cross(t).wait_send()
            own_mate(t).wait_send()
            onward(t).wait_send()
            return carry

        lax.fori_loop(0, tiles, out, 0)


def ffn(x, keep, inc, gg, gain, wout, wfg, wfu, wfd, f, o, u, e, cg):
    rows = x.shape[0]
    tiles = rows // TILE
    hidden, width = wfg.shape
    units = 3 * hidden // 16
    assert tiles <= 8 and hidden % 16 == 0
    ts = functools.partial(tile_spec, tiles)
    ins = (x, keep, inc, gg, gain, wout, wfg, wfu, wfd)
    outs = [
        ((rows, BLOCK), BF16, ts((TILE, BLOCK), 0)),
        ((rows, HV), F32, ts((TILE, HV), 0)),
        ((rows // SPAN, HV, HK), BF16, ts((PER, HV, HK), 0)),
        ((rows, BLOCK), F32, ts((TILE, BLOCK), 3)),
        ((rows, 128), F32, ts((TILE, 128), 6)),
        ((rows, BLOCK), BF16, ts((TILE, BLOCK), 7)),
        ((rows, BLOCK), F32, ts((TILE, BLOCK), 7)),
        ((rows, BLOCK), BF16, ts((TILE, BLOCK), 7)),
        ((rows, BLOCK), F32, ts((TILE, BLOCK), 7)),
        ((8, TILE), F32, whole((8, TILE))),
        ((units, 16, width), BF16, whole((units, 16, width))),
    ]
    tiled = lambda n: pltpu.VMEM((tiles, n, TILE, BLOCK), BF16)
    return pl.pallas_call(
        functools.partial(ffn_kernel, tiles),
        grid=(tiles + 7,),
        out_shape=[jax.ShapeDtypeStruct(s, d) for s, d, _ in outs],
        in_specs=[whole(a.shape) for a in ins]
        + [
            ts((TILE, 128), 0), ts((TILE, 512), 0), ts((PER, HV, HK), 0), ts((1, 8, 128), 0),
            ts((TILE, MODEL_WIDTH), 6),
        ],
        out_specs=[s for _, _, s in outs],
        scratch_shapes=[
            pltpu.VMEM((HV, HK), F32),
            tiled(4), tiled(4), tiled(4), tiled(2), tiled(2), tiled(2),
            pltpu.VMEM((tiles, TILE, BLOCK), BF16),
            pltpu.VMEM((tiles, TILE, BLOCK), BF16),
            pltpu.VMEM((4, TILE, BLOCK), F32),
            tiled(4),
            pltpu.VMEM((TILE, MODEL_WIDTH), BF16),
            pltpu.VMEM((3 * hidden, width), F32),
            pltpu.VMEM((8, TILE), F32),
            pltpu.VMEM((3, 8, TILE), F32),
            pltpu.SemaphoreType.DMA((4, tiles)),
            pltpu.SemaphoreType.DMA((4, tiles)),
            pltpu.SemaphoreType.DMA((4, tiles)),
            pltpu.SemaphoreType.DMA((2, tiles)),
            pltpu.SemaphoreType.DMA((6, tiles)),
            pltpu.SemaphoreType.DMA((2, 3)),
        ],
        compiler_params=pltpu.CompilerParams(
            collective_id=2, has_side_effects=True, vmem_limit_bytes=VMEM_LIMIT,
            dimension_semantics=("arbitrary",),
        ),
        name="ffn",
    )(*ins, f, o, u, e, cg)


LAGS = (2, 2, 2)


def levels(count):
    bits = count.bit_length() - 1
    assert 1 << bits == count
    return bits


def folds(count):
    return count == 8


class Sum:
    def __init__(self, count, sources, dest, segments, scratch):
        self.count = count
        self.bits = levels(count)
        self.folds = folds(count)
        self.sources = sources
        self.dest = dest
        self.segments = segments
        self.got = scratch[: self.bits]
        self.ring, self.side_sum, self.line_sum = scratch[self.bits : self.bits + 3]
        self.sems, self.lsem = scratch[self.bits + 3 :]

    def slot(self, k):
        if not self.folds:
            return k
        odd = lax.rem(lax.rem(k, 5), 2)
        return (3 - odd) * lax.div(k, 5) + lax.div(lax.rem(k, 5), 2)

    def where(self, k, level):
        place = lax.axis_index("seq")
        turn = 1 if self.folds else lax.div(lax.rem(k, 4), 3)
        start = 0
        for step in range(level + 1):
            stride = 1 << step
            if step < 2:
                stride = stride + turn * (3 - 2 * stride)
            bit = lax.rem(lax.div(place, stride), 2)
            if step == level:
                return bit, place + stride * (1 - 2 * bit), start
            start = start + bit * (self.count >> (step + 1))

    def own(self, k):
        bit, _, _ = self.where(k, 0)
        half = self.count >> 1
        return pltpu.make_async_copy(
            self.sources[0](k, bit * half, half), self.dest(k, bit * half, half), self.lsem.at[k]
        )

    def scatter(self, k, level, kind):
        bit, partner, start = self.where(k, level)
        half = self.count >> (level + 1)
        if level == 0:
            src = self.sources[kind](k, start + (1 - bit) * half, half)
        else:
            src = self.got[level - 1].at[self.slot(k), pl.ds((1 - bit) * half, half)]
        return to_seq(src, self.got[level].at[self.slot(k)], self.sems.at[0, level, k], self.sems.at[1, level, k], partner)

    def gather(self, k, level):
        bit, partner, start = self.where(k, level)
        half = self.count >> (level + 1)
        mine = start + bit * half
        ref = self.dest(k, mine, half)
        return to_seq(ref, ref, self.sems.at[2, level, k], self.sems.at[3, level, k], partner)

    def gathered(self, k, level):
        bit, partner, start = self.where(k, level)
        half = self.count >> (level + 1)
        ref = self.dest(k, start + (1 - bit) * half, half)
        return to_seq(ref, ref, self.sems.at[2, level, k], self.sems.at[3, level, k], partner)

    def begin(self, k, kind):
        self.scatter(k, 0, kind).start()
        if kind == 0:
            self.own(k).start()

    def add(self, k, kind, level):
        bit, _, start = self.where(k, level)
        half = self.count >> (level + 1)
        self.scatter(k, level, kind).wait_recv()
        if level == 0 and kind == 0:
            self.own(k).wait()
            mine = self.dest(k, bit * half, half)[...]
        elif level == 0:
            mine = self.sources[kind](k, bit * half, half)[...]
        else:
            mine = self.got[level - 1][self.slot(k), pl.ds(bit * half, half)]
        total = (self.got[level][self.slot(k)].astype(F32) + mine.astype(F32)).astype(BF16)
        if level + 1 < self.bits:
            self.got[level][self.slot(k)] = total
            self.scatter(k, level + 1, kind).start()
        else:
            self.dest(k, start + bit * half, half)[...] = total
            self.gather(k, level).start()

    def pass_on(self, k, kind, level):
        self.gathered(k, level).wait_recv()
        if level > 0:
            self.gather(k, level - 1).start()

    def spot(self):
        place = lax.axis_index("seq")
        side = lax.rem(place, 2)
        z = lax.div(place, 2)
        low = lax.rem(z, 2)
        end = low == lax.div(z, 2)
        return side, place + 1 - 2 * side, place + 2 * (1 - 2 * low), 2 * (3 - z) + side, end

    def half_of(self, k, which):
        half = self.count >> 1
        return self.dest(k, which * half, half)

    def fold_own(self, k):
        half = self.count >> 1
        return pltpu.make_async_copy(
            self.sources[0](k, self.spot()[0] * half, half), self.ring.at[lax.rem(k, 4)], self.lsem.at[k]
        )

    def fold_side(self, k, kind):
        side, twin, _, _, _ = self.spot()
        half = self.count >> 1
        src = self.sources[kind](k, (1 - side) * half, half)
        return to_seq(src, self.side_sum.at[self.slot(k)], self.sems.at[0, 0, k], self.sems.at[1, 0, k], twin)

    def fold_in(self, k):
        n = self.slot(k)
        return to_seq(
            self.side_sum.at[n], self.line_sum.at[n], self.sems.at[0, 1, k], self.sems.at[1, 1, k], self.spot()[2]
        )

    def fold_cross(self, k):
        side, _, _, other, _ = self.spot()
        return to_seq(
            self.line_sum.at[self.slot(k)], self.half_of(k, side), self.sems.at[0, 2, k], self.sems.at[1, 2, k], other
        )

    def fold_out(self, k):
        side, _, across, _, _ = self.spot()
        ref = self.half_of(k, side)
        return to_seq(ref, ref, self.sems.at[2, 1, k], self.sems.at[3, 1, k], across)

    def fold_back(self, k, mine):
        side, twin, _, _, _ = self.spot()
        ref = self.half_of(k, side if mine else 1 - side)
        return to_seq(ref, ref, self.sems.at[2, 0, k], self.sems.at[3, 0, k], twin)

    def fold_begin(self, k, kind):
        self.fold_side(k, kind).start()
        if kind == 0:
            self.fold_own(k).start()

    def fold_1(self, k, kind):
        side, _, _, _, end = self.spot()
        half = self.count >> 1
        n = self.slot(k)
        self.fold_side(k, kind).wait_recv()
        if kind == 0:
            self.fold_own(k).wait()
            mine = self.ring[lax.rem(k, 4)]
        else:
            mine = self.sources[kind](k, side * half, half)[...]
        self.side_sum[n] = (self.side_sum[n].astype(F32) + mine.astype(F32)).astype(BF16)

        @pl.when(end)
        def _():
            self.fold_in(k).start()

    def fold_2(self, k, kind):
        n = self.slot(k)

        @pl.when(jnp.logical_not(self.spot()[4]))
        def _():
            self.fold_in(k).wait_recv()
            self.line_sum[n] = (self.line_sum[n].astype(F32) + self.side_sum[n].astype(F32)).astype(BF16)
            self.fold_cross(k).start()

    def fold_3(self, k, kind):
        side, _, _, _, end = self.spot()

        @pl.when(jnp.logical_not(end))
        def _():
            self.fold_cross(k).wait_recv()
            ref = self.half_of(k, side)
            ref[...] = (ref[...].astype(F32) + self.line_sum[self.slot(k)].astype(F32)).astype(BF16)
            self.fold_out(k).start()
            self.fold_back(k, True).start()

    def fold_4(self, k, kind):
        end = self.spot()[4]

        @pl.when(end)
        def _():
            self.fold_out(k).wait_recv()
            self.fold_back(k, True).start()

        @pl.when(jnp.logical_not(end))
        def _():
            self.fold_back(k, False).wait_recv()

    def fold_5(self, k, kind):
        @pl.when(self.spot()[4])
        def _():
            self.fold_back(k, False).wait_recv()

    def at(self, i, stage, body, fold):
        for kind, (low, high, gap) in enumerate(self.segments):
            k = i - gap - LAGS[kind] * stage
            here = (k >= low) & (k < high)
            if not self.folds:

                @pl.when(here)
                def _(kind=kind, k=k):
                    body(k, kind)

                continue
            odd = lax.rem(lax.rem(jnp.maximum(k, 0), 5), 2) == 1

            @pl.when(here & odd)
            def _(kind=kind, k=k):
                body(k, kind)

            if fold is not None:

                @pl.when(here & jnp.logical_not(odd))
                def _(kind=kind, k=k):
                    fold(k, kind)

    def step(self, i):
        stages = []
        for level in range(self.bits):
            stages.append(functools.partial(self.add, level=level))
        for level in range(self.bits - 1, -1, -1):
            stages.append(functools.partial(self.pass_on, level=level))
        folded = [self.fold_1, self.fold_2, self.fold_3, self.fold_4, self.fold_5]
        folded = folded + [None] * (len(stages) - len(folded))
        for s in range(len(stages) - 1, -1, -1):
            self.at(i, s + 1, stages[s], folded[s])
        self.at(i, 0, self.begin, self.fold_begin)

    def finish(self):
        def halving(k, kind):
            for level in range(self.bits):
                self.scatter(k, level, kind).wait_send()
                self.gather(k, level).wait_send()

        def folding(k, kind):
            end = self.spot()[4]
            self.fold_side(k, kind).wait_send()
            self.fold_back(k, True).wait_send()

            @pl.when(end)
            def _():
                self.fold_in(k).wait_send()

            @pl.when(jnp.logical_not(end))
            def _():
                self.fold_cross(k).wait_send()
                self.fold_out(k).wait_send()

        def one(kind, k, carry):
            if not self.folds:
                halving(k, kind)
                return carry
            odd = lax.rem(lax.rem(k, 5), 2) == 1

            @pl.when(odd)
            def _():
                halving(k, kind)

            @pl.when(jnp.logical_not(odd))
            def _():
                folding(k, kind)

            return carry

        for kind, (low, high, _) in enumerate(self.segments):
            lax.fori_loop(low, high, functools.partial(one, kind), 0)

    @staticmethod
    def scratch(count, parts, first, unit):
        bits = levels(count)
        odd = parts
        even = 1
        half = 16
        if folds(count):
            odd = sum(1 for k in range(parts) if k % 5 % 2 == 1)
            even = parts - odd
            half = count // 2
        one = (1,) + unit if not folds(count) else (half,) + unit
        return [pltpu.VMEM((odd, count >> (level + 1)) + unit, BF16) for level in range(bits)] + [
            pltpu.VMEM((4 if folds(count) else 1,) + one, BF16),
            pltpu.VMEM((even,) + one, BF16),
            pltpu.VMEM((even,) + one, BF16),
            pltpu.SemaphoreType.DMA((4, bits, parts)),
            pltpu.SemaphoreType.DMA((first,)),
        ]


def plan(count, wide, tiles):
    second = tiles + 3
    a = wide // count
    b = a + 32 // count
    c = b + up_to(34 + wide % count, count) // count
    gap = max(0, second - a)
    late = max(gap, second + tiles - b, second + tiles + 3 - (c - 1))
    return (0, a, 0), (a, b, gap), (b, c, late)


def finish_kernel(fg, fu, fd, first, second, tail, extra, dfg, dfu, dfd, dq, dk, dv, dg, dwo, dr, dup, dag, dffg, db, dgg):
    for src, dst in ((fg, dfg), (fu, dfu), (fd, dfd)):
        dst[...] = src[...].reshape(dst.shape).astype(F32)

    @pl.when(pl.program_id(0) == pl.num_programs(0) - 1)
    def _():
        tail_rows = extra.shape[0] * 16
        dfd[dfd.shape[0] - tail_rows :, :] = extra[...].reshape(tail_rows, -1).astype(F32)

    rows = first[...].reshape(-1, 512).astype(F32)
    dg[...] = rows[:, 0:256]
    dwo[...] = rows[:, 256:512].T
    rows = second[...].reshape(-1, 512).astype(F32)
    dq[...] = rows[:, 0:128]
    dk[...] = rows[:, 128:256]
    dv[...] = rows[:, 256:512]
    dr[...] = tail[0].astype(F32)
    last = tail[1].astype(F32)
    dup[...] = last[:, 0:128]
    dag[...] = last[0:1, 128:384]
    dffg[...] = last[1:2, 128:384]
    db[...] = last[3:4, 128:256]
    dgg[...] = last[2:3, 128:384]


def finish(units, hidden, wide, count):
    first = wide // count * count
    rest = wide % count
    width = units.shape[2]
    steps = 4
    per = hidden // 16 // steps
    assert per * steps * 16 == hidden and 0 < rest <= per
    rows = MODEL_WIDTH // steps
    wide_spec = lambda n: pl.BlockSpec((per, 16, width), lambda i: (i + n * steps, 0, 0))
    half_spec = lambda n: pl.BlockSpec(
        (pl.Element(rows // 16), pl.Element(16), pl.Element(512)),
        lambda i: (first + n + (i % 2) * (rows // 16), 0, (i // 2) * 512),
    )
    down = lambda r, c: ((r * steps, c), pl.BlockSpec((r, c), lambda i: (i, 0)))
    full = lambda r, c: ((r, c), pl.BlockSpec((r, c), lambda i: (0, 0)))
    outs = [
        down(per * 16, width), down(per * 16, width), down(per * 16, width),
        down(rows, 128), down(rows, 128), down(rows, 256), down(rows, 256),
        ((256, MODEL_WIDTH), pl.BlockSpec((256, rows), lambda i: (0, i))),
        full(RANK, MODEL_WIDTH), full(RANK, 128), full(1, 256), full(1, 256), full(1, 128), full(1, 256),
    ]
    return pl.pallas_call(
        finish_kernel,
        grid=(steps,),
        out_shape=[jax.ShapeDtypeStruct(s, F32) for s, _ in outs],
        in_specs=[
            wide_spec(0), wide_spec(1), wide_spec(2),
            half_spec(0), half_spec(32),
            pl.BlockSpec((pl.Element(2), pl.Element(16), pl.Element(width)), lambda i: (first + 64, 0, 0)),
            pl.BlockSpec((pl.Element(rest), pl.Element(16), pl.Element(width)), lambda i: (first + 66, 0, 0)),
        ],
        out_specs=[s for _, s in outs],
        compiler_params=pltpu.CompilerParams(
            vmem_limit_bytes=VMEM_LIMIT, dimension_semantics=("arbitrary",)
        ),
        name="finish",
    )(units, units, units, units, units, units, units)


def back_kernel(
    tiles, count, segments,
    keep_ref, d_ref, stat_ref, gg_ref, again, fgain, wout, wq, wk, wv, wg, wr, rup,
    wide_in, gsend, psend, x_ref, c_ref, gown, h1, invf, f1, gz_ref, oo_ref, gated, ws1, b1, e1,
    na1, f2, b2, ws2, e2, na, h2, pown, inva,
    gt_o, lo_o, units_o,
    tri, rg, gh, gb, gzs, gw, gqd, gkd, gv, state, sbuf, rbuf,
    gcat, mn, sc, rc, own, st_s, st_r, both, joint, small, held, wide_o, few, lot,
    gsem, psem, hsem, nsem, csem, tsem, esend, erecv, wsem, jsem, *rest,
):
    i = pl.program_id(0)
    me, mate, cross, far = peers()
    place = lax.axis_index("seq")
    last = tiles - 1
    second = tiles + 3

    def rows_of(t):
        return pl.ds(pl.multiple_of(t * TILE, TILE), TILE)

    def own_cols(ref):
        return ref[:, pl.ds(pl.multiple_of(me * BLOCK, BLOCK), BLOCK)].astype(F32)

    def grads(t):
        return to_head(gsend.at[rows_of(t)], rg.at[t], gsem.at[0, t], gsem.at[1, t], cross)

    def feeds(t):
        return to_head(psend.at[rows_of(t)], rg.at[t], psem.at[0, t], psem.at[1, t], cross)

    def own_mate(t):
        return to_head(gb.at[t, me], gb.at[t, me], hsem.at[0, t], hsem.at[1, t], mate)

    def own_cross(t):
        return to_head(gb.at[t, me], gb.at[t, me], hsem.at[2, t], hsem.at[3, t], cross)

    def onward(t):
        return to_head(gb.at[t, cross], gb.at[t, cross], hsem.at[4, t], hsem.at[5, t], mate)

    def pair(t, which):
        block = mate if which == 0 else far
        return to_head(gb.at[t, block], mn.at[t, which], nsem.at[2 * which, t], nsem.at[2 * which + 1, t], mate)

    def over(t):
        return to_head(sc.at[t], rc.at[t], csem.at[0, t], csem.at[1, t], cross)

    def stats(t, n, other):
        return to_head(st_s.at[t], st_r.at[t, n], tsem.at[0, n, t], tsem.at[1, n, t], other)

    first = wide_in.shape[0] // count
    spare = wide_in.shape[0] - first * count
    parts = wide_o.shape[0] // count
    ready = second + tiles
    feed = ready + 4

    def early(k, start, n):
        return wide_in.at[pl.ds(k * count + start, n)]

    def middle(k, start, n):
        return few.at[pl.ds((k - segments[1][0]) * count + start, n)]

    def late(k, start, n):
        return lot.at[pl.ds((k - segments[2][0]) * count + start, n)]

    def some(k, start, n):
        return wide_o.at[pl.ds(k * count + start, n)]

    wide_sum = Sum(count, (early, middle, late), some, segments, rest)

    @pl.when(i == 0)
    def _():
        greet_head()
        greet_seq(count)
        pl.semaphore_wait(pltpu.get_barrier_semaphore(), 3 + count - 1)
        for n in range(AHEAD):
            grads(last - n).start()
        def weave(r, carry):
            rows = pl.ds(pl.multiple_of(r * 16, 16), 16)
            lot[r, :, 0:128] = wq[rows, :]
            lot[r, :, 128:256] = wk[rows, :]
            lot[r, :, 256:512] = wv[rows, :]
            lot[r, :, 512:768] = wg[rows, :]
            return carry

        lax.fori_loop(0, MODEL_WIDTH // 16, weave, 0)
        r = lax.broadcasted_iota(jnp.int32, (TILE, TILE), 0)
        c = lax.broadcasted_iota(jnp.int32, (TILE, TILE), 1)
        tri[...] = jnp.where(((r >> 6) == (c >> 6)) & (r > c), 1.0, 0.0).astype(BF16)
        state[...] = jnp.zeros_like(state)
        both[...] = jnp.zeros_like(both)
        joint[...] = jnp.zeros_like(joint)
        small[...] = jnp.zeros_like(small)

    @pl.when(i + AHEAD <= last)
    def _():
        grads(last - i - AHEAD).start()

    def share(n, other):
        return to_head(joint, held.at[me], jsem.at[0, n], jsem.at[1, n], other)

    spare_copy = pltpu.make_async_copy(
        wide_in.at[pl.ds(first * count, spare)], lot.at[pl.ds(34, spare)], wsem.at[2]
    )

    def lay(dst, col):
        def copy(r, carry):
            for side in range(2):
                rows = pl.ds(pl.multiple_of(side * (MODEL_WIDTH // 2) + r * 16, 16), 16)
                dst[r, :, side * 512 : (side + 1) * 512] = both[rows, col : col + 512].astype(BF16)
            return carry

        lax.fori_loop(0, 32, copy, 0)

    @pl.when(i == second)
    def _():
        lay(few, 512)

    @pl.when(i == ready)
    def _():
        held[me] = joint[...]
        for n, other in enumerate((mate, cross, far)):
            share(n, other).start()
        lay(lot, 0)
        lot[32:] = jnp.zeros((lot.shape[0] - 32,) + lot.shape[1:], BF16)
        spare_copy.start()

    @pl.when(i == ready + 3)
    def _():
        spare_copy.wait()
        for n, other in enumerate((mate, cross, far)):
            to_head(joint, held.at[other], jsem.at[0, n], jsem.at[1, n], other).wait()
        base = 32
        sums = (held[0] + held[1]) + (held[2] + held[3])
        lot[base] = sums[0:RANK].astype(BF16)
        lot[base + 1] = jnp.zeros((16, MODEL_WIDTH), BF16)
        small[2:3, 128:384] = sums[16:17, 0:256]
        lot[base + 1, :, 0:512] = small[...].astype(BF16)

    wide_sum.step(i)

    @pl.when((i >= 2) & (i - 2 <= last))
    def _():
        t = last - (i - 2)
        own_cross(t).wait_recv()
        onward(t).start()

    @pl.when(i <= last)
    def _():
        t = last - i
        grads(t).wait_recv()
        gnf = gown[...] + rg[t].astype(F32)
        inv = invf[...][:, 0:1]
        hn = h1[...].astype(BF16).astype(F32) * inv
        row = stat_ref[pl.ds(t, 1), :]
        stat = jnp.broadcast_to(row, (128, TILE)).T[:, 0:1]
        grad = c_ref[...].astype(F32) + inv * (own_cols(fgain) * gnf - hn * (stat / MODEL_WIDTH))
        small[1:2, 128:384] += jnp.sum(gnf * hn, axis=0, keepdims=True)
        gh[t] = grad
        gb[t, me] = grad.astype(BF16)
        own_cross(t).start()
        own_mate(t).start()

    half = tiles // 2

    def some_feeds(low, high, at):
        @pl.when((i >= at) & (low + 2 * (i - at) < high))
        def _():
            n = low + 2 * (i - at)
            feeds(last - n).start()

            @pl.when(n + 1 < high)
            def _():
                feeds(last - n - 1).start()

    some_feeds(0, half, last + 2)
    some_feeds(half, tiles, ready)

    @pl.when((i >= 3) & (i - 3 <= last))
    def _():
        t = last - (i - 3)
        own_mate(t).wait_recv()
        onward(t).wait_recv()
        gt = jnp.zeros((TILE, BLOCK), F32)
        for j in range(4):
            cols = slice(j * BLOCK, (j + 1) * BLOCK)
            gt = gt + dot_nt(gb[t, j], wout[:, cols])
            both[cols, 768:1024] += dot_tn(gb[t, j], gated[...])
        o = oo_ref[...]
        gz = gz_ref[...]
        inv = lax.rsqrt(jnp.mean(o * o, axis=1, keepdims=True) + EPS)
        on = o * inv
        sig = jax.nn.sigmoid(gz)
        gn = gt * (gz * sig)
        joint[16:17, 0:256] += jnp.sum(gn * on, axis=0, keepdims=True)
        gain = gg_ref[...].astype(F32)
        ggz = (gt * on * gain * (sig * (1.0 + gz * (1.0 - sig)))).astype(BF16)
        gzs[t] = ggz
        both[:, 512:768] += dot_tn(na1[...], ggz)
        p = gn * gain
        go = (inv * (p - on * jnp.mean(p * on, axis=1, keepdims=True))).astype(BF16)
        qd = f1[:, 0:128].astype(BF16)
        kd = f1[:, 128:256].astype(BF16)
        v = b1[:, 0:256]
        causal, _ = span_masks(TILE, TILE)
        ga = jnp.where(causal, dot_nt(go, v), 0.0).astype(BF16)
        gqd[t] = dot_nn(ga, kd)
        gkd[t] = dot_tn(ga, qd)
        gv[t] = dot_tn(b1[:, 256:512], go)
        for c in range(PER - 1, -1, -1):
            rows = slice(c * SPAN, (c + 1) * SPAN)
            gqd[t, rows, :] += dot_nn(go[rows], ws1[c])
            fresh = dot_tn(go[rows], qd[rows])
            gw[t * PER + c] = fresh
            through = keep_ref[t, c : c + 1, :] * e1[0, c : c + 1, :]
            state[...] = through * (fresh + state[...])

    @pl.when(i == last + 3)
    def _():
        sbuf[...] = jnp.zeros_like(sbuf)
        sbuf[0:HV, :] = state[...].astype(BF16)
        d = d_ref[...]
        hi = d.astype(BF16).astype(F32)
        first = lax.broadcasted_iota(jnp.int32, (16, 128), 0) < 8
        both = jnp.where(first, jnp.concatenate([hi, hi], axis=0), jnp.concatenate([d - hi, d - hi], axis=0))
        sbuf[HV : HV + 16, :] = both.astype(BF16)

        def send(p, carry):
            to_seq(sbuf, rbuf.at[place], esend.at[p], erecv.at[place], p).start()
            return carry

        lax.fori_loop(0, place, send, 0)

    @pl.when(i == second)
    def _():
        def free(t, carry):
            own_cross(t).wait_send()
            own_mate(t).wait_send()
            onward(t).wait_send()
            return carry

        lax.fori_loop(0, tiles, free, 0)
        state[...] = jnp.zeros_like(state)

        def join(n, carry):
            p = count - 1 - n
            to_seq(sbuf, rbuf.at[p], esend.at[p], erecv.at[p], place).wait_recv()
            got = rbuf[p].astype(F32)
            d = got[HV : HV + 1] + got[HV + 8 : HV + 9]
            state[...] = got[0:HV] + d * state[...]
            return carry

        lax.fori_loop(0, count - 1 - place, join, 0)

    @pl.when((i >= second + 3) & (i - second - 3 <= last))
    def _():
        t = last - (i - second - 3)
        over(t).wait_recv()
        for n, other in enumerate((mate, cross, far)):
            stats(t, n, other).wait_recv()
        gna = own[lax.rem(t, 3)] + rc[t].astype(F32)
        inv = inva[...][:, 0:1]
        xn = x_ref[...].astype(F32) * inv
        row = (st_s[t] + st_r[t, 0]) + (st_r[t, 1] + st_r[t, 2])
        stat = jnp.broadcast_to(row[0:1], (128, TILE)).T[:, 0:1]
        gt_o[...] = gh[t] + inv * (own_cols(again) * gna - xn * (stat / MODEL_WIDTH))
        small[0:1, 128:384] += jnp.sum(gna * xn, axis=0, keepdims=True)

    @pl.when((i >= second + 1) & (i - second - 1 <= last))
    def _():
        t = last - (i - second - 1)
        pair(t, 0).wait_recv()
        pair(t, 1).wait_recv()
        sc[t] = (gb[t, cross].astype(F32) + mn[t, 1].astype(F32)).astype(BF16)
        over(t).start()
        own[lax.rem(t, 3)] = gb[t, me].astype(F32) + mn[t, 0].astype(F32)

    @pl.when((i >= second) & (i - second <= last))
    def _():
        t = last - (i - second)
        qf = f2[:, 0:128]
        kf = f2[:, 128:256]
        kd = kf.astype(BF16)
        pieces = [None] * PER
        for c in range(PER - 1, -1, -1):
            rows = slice(c * SPAN, (c + 1) * SPAN)
            low = state[...].astype(BF16)
            gkd[t, rows, :] += dot_nn(b2[rows, 0:256], low)
            gv[t, rows, :] += dot_nt(kd[rows], low)
            ge = gw[t * PER + c] + state[...]
            pieces[c] = jnp.broadcast_to(jnp.sum(ge * ws2[c].astype(F32), axis=0, keepdims=True), (SPAN, HK))
            state[...] = (keep_ref[t, c : c + 1, :] * e2[0, c : c + 1, :]) * ge
        gq = gqd[t]
        gk = gkd[t]
        diff = gq * qf - gk * kf
        gg = jnp.concatenate(pieces, axis=0) - fold(dot_nn(tri[...], three(diff)))
        glogit = gg * f2[:, 512:640]
        small[3:4, 128:256] += jnp.sum(glogit, axis=0, keepdims=True)
        hi = glogit.astype(BF16)
        lo = (glogit - hi.astype(F32)).astype(BF16)
        glr = dot_nt(hi, rup[...]) + dot_nt(lo, rup[...])
        lr = b2[:, 512 : 512 + RANK]
        small[:, 0:128] += dot_tn(lr, hi) + dot_tn(lr, lo)
        glr = glr.astype(BF16)
        joint[0:RANK, :] += dot_tn(glr, na[...])
        gcat[:, 0:128] = (gq * f2[:, 256:384]).astype(BF16)
        gcat[:, 128:256] = (gk * f2[:, 384:512]).astype(BF16)
        gcat[:, 256:512] = gv[t].astype(BF16)
        gcat[:, 512:768] = gzs[t]
        g = gcat[...]
        stat = jnp.zeros((TILE, 1), F32)
        for j in range(4):
            cols = slice(j * BLOCK, (j + 1) * BLOCK)
            gj = dot_nt(g, lot[16 * j : 16 * (j + 1), :, 0:768].reshape(BLOCK, 768)) + dot_nn(glr, wr[:, cols])
            stat = stat + jnp.sum(gj * na[:, cols].astype(F32), axis=1, keepdims=True)
            gb[t, j] = gj.astype(BF16)
        pair(t, 1).start()
        pair(t, 0).start()
        st_s[t] = jnp.broadcast_to(stat, (TILE, 128)).T[0:8, :]
        for n, other in enumerate((mate, cross, far)):
            stats(t, n, other).start()
        both[:, 0:512] += dot_tn(na[...], g[:, 0:512])

    @pl.when((i >= feed) & (i - feed <= last))
    def _():
        t = last - (i - feed)
        feeds(t).wait_recv()
        lo_o[...] = (h2[...] + (pown[...] + rg[t].astype(F32))).astype(BF16)

    drained = first + 2 * levels(count) * LAGS[0]
    head_units = pl.ds(0, first * count)
    tail_units = pl.ds(first * count, (parts - first) * count)
    head_copy = pltpu.make_async_copy(wide_o.at[head_units], units_o.at[head_units], wsem.at[0])
    tail_copy = pltpu.make_async_copy(wide_o.at[tail_units], units_o.at[tail_units], wsem.at[1])

    @pl.when(i == drained)
    def _():
        head_copy.start()

    @pl.when(i == pl.num_programs(0) - 1)
    def _():
        tail_copy.start()
        wide_sum.finish()
        tail_copy.wait()
        head_copy.wait()

        def sent(p, carry):
            to_seq(sbuf, rbuf.at[place], esend.at[p], erecv.at[place], p).wait_send()
            return carry

        lax.fori_loop(0, place, sent, 0)

        def out(t, carry):
            grads(t).wait_send()
            feeds(t).wait_send()
            pair(t, 0).wait_send()
            pair(t, 1).wait_send()
            over(t).wait_send()
            for n, other in enumerate((mate, cross, far)):
                stats(t, n, other).wait_send()
            return carry

        lax.fori_loop(0, tiles, out, 0)


def back(fixed, wide, gsend, psend, x, cot, gown, h, invf, f, o, oo, gated, ws, b, e, na, pown, inva):
    rows = h.shape[0]
    tiles = rows // TILE
    count = lax.axis_size("seq")
    second = tiles + 3
    width = MODEL_WIDTH
    segments = plan(count, wide.shape[0], tiles)
    first = segments[0][1]
    parts = segments[2][1]
    units = parts * count
    feed = second + tiles + 4
    stages = 2 * levels(count)
    steps = max([feed + tiles] + [end + gap + stages * lag + 1 for (_, end, gap), lag in zip(segments, LAGS)])
    ts = functools.partial(tile_spec, tiles, back=True)
    outs = [
        ((rows, BLOCK), F32, ts((TILE, BLOCK), second + 3)),
        ((rows, BLOCK), BF16, ts((TILE, BLOCK), feed)),
        ((units, 16, width), BF16, pl.BlockSpec(memory_space=pl.ANY)),
    ]
    tiled = lambda n: pltpu.VMEM((tiles, n, TILE, BLOCK), BF16)
    flat = lambda n, d: pltpu.VMEM((tiles, TILE, n), d)
    return pl.pallas_call(
        functools.partial(back_kernel, tiles, count, segments),
        grid=(steps,),
        out_shape=[jax.ShapeDtypeStruct(s, d) for s, d, _ in outs],
        in_specs=[whole(a.shape) for a in fixed]
        + [
            pl.BlockSpec(memory_space=pl.ANY), pl.BlockSpec(memory_space=pl.ANY), pl.BlockSpec(memory_space=pl.ANY),
            ts((TILE, BLOCK), second + 3), ts((TILE, BLOCK), 0),
            ts((TILE, BLOCK), 0), ts((TILE, BLOCK), 0), ts((TILE, 128), 0),
            ts((TILE, 256), 3), ts((TILE, 256), 3), ts((TILE, 256), 3), ts((TILE, 256), 3),
            ts((PER, HV, HK), 3), ts((TILE, 640), 3), ts((1, 8, 128), 3), ts((TILE, width), 3),
            ts((TILE, 640), second), ts((TILE, 640), second), ts((PER, HV, HK), second), ts((1, 8, 128), second),
            ts((TILE, width), second), ts((TILE, BLOCK), feed), ts((TILE, BLOCK), feed),
            ts((TILE, 128), second + 3),
        ],
        out_specs=[s for _, _, s in outs],
        scratch_shapes=[
            pltpu.VMEM((TILE, TILE), BF16),
            flat(BLOCK, BF16), flat(BLOCK, F32),
            tiled(4),
            flat(BLOCK, BF16),
            pltpu.VMEM((rows // SPAN, HV, HK), F32),
            flat(HK, F32), flat(HK, F32), flat(HV, F32),
            pltpu.VMEM((HV, HK), F32),
            pltpu.VMEM((HV + 16, HK), BF16),
            pltpu.VMEM((count, HV + 16, HK), BF16),
            pltpu.VMEM((TILE, 768), BF16),
            tiled(2), flat(BLOCK, BF16), flat(BLOCK, BF16),
            pltpu.VMEM((3, TILE, BLOCK), F32),
            pltpu.VMEM((tiles, 8, TILE), F32),
            pltpu.VMEM((tiles, 3, 8, TILE), F32),
            pltpu.VMEM((width, width), F32),
            pltpu.VMEM((24, width), F32),
            pltpu.VMEM((16, 512), F32),
            pltpu.VMEM((4, 24, width), F32),
            pltpu.VMEM((units, 16, width), BF16),
            pltpu.VMEM((32, 16, width), BF16),
            pltpu.VMEM((max(width // 16, (parts - segments[2][0]) * count), 16, width), BF16),
            pltpu.SemaphoreType.DMA((2, tiles)),
            pltpu.SemaphoreType.DMA((2, tiles)),
            pltpu.SemaphoreType.DMA((6, tiles)),
            pltpu.SemaphoreType.DMA((4, tiles)),
            pltpu.SemaphoreType.DMA((2, tiles)),
            pltpu.SemaphoreType.DMA((2, 3, tiles)),
            pltpu.SemaphoreType.DMA((count,)),
            pltpu.SemaphoreType.DMA((count,)),
            pltpu.SemaphoreType.DMA((3,)),
            pltpu.SemaphoreType.DMA((2, 3)),
        ]
        + Sum.scratch(count, parts, first, wide.shape[1:]),
        compiler_params=pltpu.CompilerParams(
            collective_id=3, has_side_effects=True, vmem_limit_bytes=VMEM_LIMIT,
            dimension_semantics=("arbitrary",),
        ),
        name="back",
    )(*fixed, wide, gsend, psend, x, cot, gown, h, invf, f, o, oo, gated, ws, b, e, na, f, b, ws, e, na, h, pown, inva)


def shards(
    tokens,
    row_starts,
    attn_gain,
    query_weight,
    key_weight,
    value_weight,
    gate_weight,
    rank_down,
    rank_up,
    rank_bias,
    group_gain,
    out_weight,
    feed_gain,
    feed_gate,
    feed_up,
    feed_down,
    cotangent,
):
    rows = tokens.shape[0]
    tiles = rows // TILE
    spans = rows // SPAN
    span_ids = lax.axis_index("seq") * spans + jnp.arange(spans, dtype=jnp.int32)
    resets = jnp.any((row_starts // SPAN)[None, :] == span_ids[:, None], axis=1).astype(F32)
    keep = jnp.pad((1.0 - resets).reshape(tiles, PER, 1), ((0, 0), (0, 8 - PER), (0, 0)))
    keep = jnp.broadcast_to(keep, (tiles, 8, 128))
    weights = (
        query_weight[0], key_weight[0], value_weight[0], gate_weight[0], jnp.swapaxes(rank_down[0], 0, 1), rank_up[0]
    )
    na, cg, inva, f, b, o, u, e, inc, dec = front(tokens, cotangent, keep, attn_gain, *weights, rank_bias)
    gated, oo, ws, h, invf, gsend, gown, psend, pown, stat, wide = ffn(
        tokens, keep, inc, group_gain, feed_gain, out_weight[0], jnp.swapaxes(feed_gate[0], 0, 1),
        jnp.swapaxes(feed_up[0], 0, 1), feed_down[0], f, o, u, e, cg,
    )
    fixed = (
        keep, dec, stat, group_gain, attn_gain, feed_gain, out_weight[0],
    ) + weights
    grad_tokens, layer_out, units = back(fixed, wide, gsend, psend, tokens, cotangent, gown, h, invf, f, o, oo, gated, ws, b, e, na, pown, inva)
    dfg, dfu, dfd, dq, dk, dv, dg, dwo, dr, dup, dag, dffg, db, dgg = finish(
        units, feed_gate.shape[2], wide.shape[0], lax.axis_size("seq")
    )
    dfg, dfu, dr = (jnp.swapaxes(a, 0, 1) for a in (dfg, dfu, dr))
    grads = (dag, dq[None], dk[None], dv[None], dg[None], dr[None], dup[None], db, dgg, dwo[None], dffg, dfg[None], dfu[None], dfd[None])
    return (layer_out, grad_tokens) + grads


def solution(mesh):
    placed = (
        P("seq", "head"),
        P(),
        P(),
        P(None, None, "head"),
        P(None, None, "head"),
        P(None, None, "head"),
        P(None, None, "head"),
        P(),
        P(None, None, "head"),
        P(None, "head"),
        P(),
        P(None, "head", None),
        P(),
        P(None, None, "head"),
        P(None, None, "head"),
        P(None, "head", None),
        P("seq", "head"),
    )
    return jax.shard_map(
        shards,
        mesh=mesh,
        in_specs=placed,
        out_specs=(
            P("seq", "head"),
            P("seq", "head"),
            P(None, "head"),
            P(None, None, "head"),
            P(None, None, "head"),
            P(None, None, "head"),
            P(None, None, "head"),
            P(),
            P(None, None, "head"),
            P(None, "head"),
            P(),
            P(None, "head", None),
            P(None, "head"),
            P(None, None, "head"),
            P(None, None, "head"),
            P(None, "head", None),
        ),
        check_vma=False,
    )
```

```python
import functools

import jax
import jax.numpy as jnp
from jax import lax
from jax.experimental import pallas as pl
from jax.experimental.pallas import tpu as pltpu
from jax.sharding import PartitionSpec as P

MODEL_WIDTH = 1024
HK = 128
HV = 256
SPAN = 64
RANK = 16
EPS = 1e-06
GATE_NORM = 16.0
TILE = 256
PER = TILE // SPAN
BLOCK = 256
AHEAD = 3
F32 = jnp.float32
BF16 = jnp.bfloat16
MESH = pl.DeviceIdType.MESH
VMEM_LIMIT = 62 * 1024 * 1024


def dot_nn(a, b):
    return jnp.dot(a, b, preferred_element_type=F32)


def dot_nt(a, b):
    return lax.dot_general(a, b, (((1,), (1,)), ((), ())), preferred_element_type=F32)


def dot_tn(a, b):
    return lax.dot_general(a, b, (((0,), (0,)), ((), ())), preferred_element_type=F32)


def peers():
    me = lax.axis_index("head")
    mate = me + 1 - 2 * lax.rem(me, 2)
    cross = lax.rem(me + 2, 4)
    far = cross + 1 - 2 * lax.rem(cross, 2)
    return me, mate, cross, far


def greet_head():
    _, mate, cross, far = peers()
    barrier = pltpu.get_barrier_semaphore()
    for other in (mate, cross, far):
        pl.semaphore_signal(barrier, inc=1, device_id={"head": other}, device_id_type=MESH)


def greet_seq(count):
    place = lax.axis_index("seq")
    barrier = pltpu.get_barrier_semaphore()

    def one(step, carry):
        other = lax.rem(place + step, count)
        pl.semaphore_signal(barrier, inc=1, device_id={"seq": other}, device_id_type=MESH)
        return carry

    lax.fori_loop(1, count, one, 0)


def to_head(src, dst, send, recv, other):
    return pltpu.make_async_remote_copy(
        src_ref=src, dst_ref=dst, send_sem=send, recv_sem=recv,
        device_id={"head": other}, device_id_type=MESH,
    )


def to_seq(src, dst, send, recv, other):
    return pltpu.make_async_remote_copy(
        src_ref=src, dst_ref=dst, send_sem=send, recv_sem=recv,
        device_id={"seq": other}, device_id_type=MESH,
    )


def span_masks(rows, cols):
    r = lax.broadcasted_iota(jnp.int32, (rows, cols), 0)
    c = lax.broadcasted_iota(jnp.int32, (rows, cols), 1)
    same = (r >> 6) == (c >> 6)
    return same & (r >= c), same


def three(x):
    a = x.astype(BF16)
    rest = x - a.astype(F32)
    b = rest.astype(BF16)
    c = (rest - b.astype(F32)).astype(BF16)
    return jnp.concatenate([a, b, c], axis=1)


def fold(x):
    w = x.shape[1] // 3
    return x[:, :w] + x[:, w : 2 * w] + x[:, 2 * w :]


def front_kernel(
    tiles, count,
    x_ref, c_ref, keep_ref, gain_ref, wq, wk, wv, wg, wr, rup, bias_ref,
    na_o, cg_o, inv_o, f_o, b_o, o_o, u_o, e_o, in_o, d_o,
    grid_buf, wcat, tri, state, decay, sbuf, rbuf, sems, esend, erecv,
):
    i = pl.program_id(0)
    me, mate, cross, far = peers()
    place = lax.axis_index("seq")
    total = 2 * tiles

    def own_mate(m):
        return to_head(grid_buf.at[m, me], grid_buf.at[m, me], sems.at[0, m], sems.at[1, m], mate)

    def own_cross(m):
        return to_head(grid_buf.at[m, me], grid_buf.at[m, me], sems.at[2, m], sems.at[3, m], cross)

    def onward(m):
        return to_head(grid_buf.at[m, cross], grid_buf.at[m, cross], sems.at[4, m], sems.at[5, m], mate)

    @pl.when(i == 0)
    def _():
        greet_head()
        greet_seq(count)

        def own(m, carry):
            rows = pl.ds(pl.multiple_of(m * TILE, TILE), TILE)
            grid_buf[m, me] = x_ref[rows, :]
            grid_buf[m + tiles, me] = c_ref[rows, :]
            return carry

        lax.fori_loop(0, tiles, own, 0)
        pl.semaphore_wait(pltpu.get_barrier_semaphore(), 3 + count - 1)
        for m in range(AHEAD):
            own_cross(m).start()
            own_mate(m).start()
        wcat[:, 0:128] = wq[...]
        wcat[:, 128:256] = wk[...]
        wcat[:, 256:512] = wv[...]
        wcat[:, 512:768] = wg[...]
        causal, same = span_masks(TILE, TILE)
        tri[0:TILE, :] = jnp.where(causal, 1.0, 0.0).astype(BF16)
        tri[TILE : 2 * TILE, :] = jnp.where(same, 1.0, 0.0).astype(BF16)
        state[...] = jnp.zeros_like(state)
        decay[...] = jnp.ones_like(decay)

    @pl.when(i < total)
    def _():
        own_cross(i).wait_recv()
        onward(i).start()

    @pl.when(i + AHEAD < total)
    def _():
        own_cross(i + AHEAD).start()
        own_mate(i + AHEAD).start()

    @pl.when(i >= 1)
    def _():
        own_mate(i - 1).wait_recv()
        onward(i - 1).wait_recv()

    @pl.when((i >= 1) & (i <= tiles))
    def _():
        m = i - 1
        squares = jnp.zeros((TILE, 1), F32)
        for j in range(4):
            xj = grid_buf[m, j].astype(F32)
            squares = squares + jnp.sum(xj * xj, axis=1, keepdims=True)
        inv = lax.rsqrt(squares / MODEL_WIDTH + EPS)
        inv_o[...] = jnp.broadcast_to(inv, (TILE, 128))
        for j in range(4):
            cols = slice(j * BLOCK, (j + 1) * BLOCK)
            xj = grid_buf[m, j].astype(F32)
            na_o[:, cols] = (xj * inv * gain_ref[:, cols].astype(F32)).astype(BF16)
        proj = dot_nn(na_o[...], wcat[...])
        q = proj[:, 0:128]
        k = proj[:, 128:256]
        v = proj[:, 256:512].astype(BF16)
        o_o[:, 0:256] = proj[:, 512:768]
        lr = dot_nt(na_o[...], wr[...]).astype(BF16)
        z = dot_nn(lr, rup[...]) + bias_ref[...].astype(F32)
        g = (jnp.minimum(z, 0.0) - jnp.log1p(jnp.exp(-jnp.abs(z)))) / GATE_NORM
        sums = fold(dot_nn(tri[...], three(g)))
        b = sums[0:TILE]
        e = sums[TILE : 2 * TILE]
        fq = (HK ** (-0.5)) * jnp.exp(b - e)
        fk = jnp.exp(e - b)
        qf = q * fq
        kf = k * fk
        f_o[:, 0:128] = qf
        f_o[:, 128:256] = kf
        f_o[:, 256:384] = fq
        f_o[:, 384:512] = fk
        f_o[:, 512:640] = jax.nn.sigmoid(-z) / GATE_NORM
        qd = qf.astype(BF16)
        kd = kf.astype(BF16)
        causal, _ = span_masks(TILE, TILE)
        scores = jnp.where(causal, dot_nt(qd, kd), 0.0).astype(BF16)
        b_o[:, 0:256] = v
        b_o[:, 256:512] = scores
        b_o[:, 512 : 512 + RANK] = lr
        o_o[:, 256:512] = dot_nn(scores, v)
        for c in range(PER):
            rows = slice(c * SPAN, (c + 1) * SPAN)
            update = dot_tn(v[rows], kd[rows])
            u_o[c] = update
            ee = jnp.exp(e[c * SPAN : c * SPAN + 1])
            e_o[0, c : c + 1, :] = ee
            through = keep_ref[m, c : c + 1, :] * ee
            state[...] = through * state[...] + update
            decay[...] = through * decay[...]

    @pl.when(i == tiles)
    def _():
        d_o[...] = decay[...]
        sbuf[0:HV, :] = state[...].astype(BF16)
        d = decay[...]
        hi = d.astype(BF16).astype(F32)
        first = lax.broadcasted_iota(jnp.int32, (16, 128), 0) < 8
        both = jnp.where(first, jnp.concatenate([hi, hi], axis=0), jnp.concatenate([d - hi, d - hi], axis=0))
        sbuf[HV : HV + 16, :] = both.astype(BF16)

        def send(p, carry):
            to_seq(sbuf, rbuf.at[place], esend.at[p], erecv.at[place], p).start()
            return carry

        lax.fori_loop(place + 1, count, send, 0)

    @pl.when(i > tiles)
    def _():
        m = i - 1
        for j in range(4):
            cg_o[:, j * BLOCK : (j + 1) * BLOCK] = grid_buf[m, j]

    @pl.when(i == total)
    def _():
        in_o[...] = jnp.zeros_like(in_o)

        def join(p, carry):
            to_seq(sbuf, rbuf.at[p], esend.at[p], erecv.at[p], place).wait_recv()
            got = rbuf[p].astype(F32)
            d = got[HV : HV + 1] + got[HV + 8 : HV + 9]
            in_o[...] = got[0:HV] + d * in_o[...]
            return carry

        lax.fori_loop(0, place, join, 0)

        def sent(p, carry):
            to_seq(sbuf, rbuf.at[place], esend.at[p], erecv.at[place], p).wait_send()
            return carry

        lax.fori_loop(place + 1, count, sent, 0)

        def out(m, carry):
            own_cross(m).wait_send()
            own_mate(m).wait_send()
            onward(m).wait_send()
            return carry

        lax.fori_loop(0, total, out, 0)


def whole(shape):
    zeros = (0,) * len(shape)
    return pl.BlockSpec(shape, lambda i: zeros, pipeline_mode=pl.Buffered(1))


def front(x, cot, keep, gain, wq, wk, wv, wg, wr, rup, bias):
    rows = x.shape[0]
    tiles = rows // TILE
    count = lax.axis_size("seq")

    def tile(shape, lag, axis0=True):
        rest = (0,) * (len(shape) - 1)
        return pl.BlockSpec(shape, lambda i: (jnp.clip(i - lag, 0, tiles - 1),) + rest)

    ins = (x, cot, keep, gain, wq, wk, wv, wg, wr, rup, bias)
    outs = [
        ((rows, MODEL_WIDTH), BF16, tile((TILE, MODEL_WIDTH), 1)),
        ((rows, MODEL_WIDTH), BF16, tile((TILE, MODEL_WIDTH), 1 + tiles)),
        ((rows, 128), F32, tile((TILE, 128), 1)),
        ((rows, 640), F32, tile((TILE, 640), 1)),
        ((rows, 640), BF16, tile((TILE, 640), 1)),
        ((rows, 512), F32, tile((TILE, 512), 1)),
        ((rows // SPAN, HV, HK), F32, tile((PER, HV, HK), 1)),
        ((tiles, 8, 128), F32, tile((1, 8, 128), 1)),
        ((HV, HK), F32, whole((HV, HK))),
        ((8, 128), F32, whole((8, 128))),
    ]
    return pl.pallas_call(
        functools.partial(front_kernel, tiles, count),
        grid=(2 * tiles + 1,),
        out_shape=[jax.ShapeDtypeStruct(s, d) for s, d, _ in outs],
        in_specs=[whole(a.shape) for a in ins],
        out_specs=[s for _, _, s in outs],
        scratch_shapes=[
            pltpu.VMEM((2 * tiles, 4, TILE, BLOCK), BF16),
            pltpu.VMEM((MODEL_WIDTH, 768), BF16),
            pltpu.VMEM((2 * TILE, TILE), BF16),
            pltpu.VMEM((HV, HK), F32),
            pltpu.VMEM((8, 128), F32),
            pltpu.VMEM((HV + 16, HK), BF16),
            pltpu.VMEM((count, HV + 16, HK), BF16),
            pltpu.SemaphoreType.DMA((6, 2 * tiles)),
            pltpu.SemaphoreType.DMA((count,)),
            pltpu.SemaphoreType.DMA((count,)),
        ],
        compiler_params=pltpu.CompilerParams(
            collective_id=1, has_side_effects=True, vmem_limit_bytes=VMEM_LIMIT,
            dimension_semantics=("arbitrary",),
        ),
        name="front",
    )(*ins)


def tile_spec(tiles, shape, lag, back=False, col=0):
    rest = (0,) * (len(shape) - 2) + (col,)

    def index(i):
        t = jnp.clip(i - lag, 0, tiles - 1)
        return ((tiles - 1 - t) if back else t,) + rest

    return pl.BlockSpec(shape, index)


def up_to(n, step):
    return (n + step - 1) // step * step


def ffn_kernel(
    tiles,
    x_ref, keep_ref, in_ref, gg_ref, gain_ref, wout, wfg_in, wfu_in, wfd_in,
    f_ref, o_ref, u_ref, e_ref, cg_ref,
    gated_o, oo_o, ws_o, h_o, inv_o, gsend_o, gown_o, psend_o, pown_o, stat_o, wide_o, gx_o,
    state, pa, pp, pg, ma, mp, mg, sc, rc, own, hg, nf_s, acc, wfg, wfu, wfd, st_s, st_r, gxs, gxr,
    asem, psem, gsem, csem, hsem, tsem, wsem, xsem,
):
    i = pl.program_id(0)
    me, mate, cross, far = peers()
    last = tiles - 1
    hidden = wfg.shape[0]

    def pair(buf, got, sem, t, which):
        block = mate if which == 0 else far
        return to_head(buf.at[t, block], got.at[t, which], sem.at[2 * which, t], sem.at[2 * which + 1, t], mate)

    def over(t):
        return to_head(sc.at[t], rc.at[t], csem.at[0, t], csem.at[1, t], cross)

    def own_mate(t):
        return to_head(hg.at[t, me], hg.at[t, me], hsem.at[0, t], hsem.at[1, t], mate)

    def own_cross(t):
        return to_head(hg.at[t, me], hg.at[t, me], hsem.at[2, t], hsem.at[3, t], cross)

    def onward(t):
        return to_head(hg.at[t, cross], hg.at[t, cross], hsem.at[4, t], hsem.at[5, t], mate)

    some = gxs.shape[0]

    def early(t):
        return to_head(gxs.at[t], gxr.at[t], xsem.at[0, t], xsem.at[1, t], cross)

    def stats(n, other):
        return to_head(st_s, st_r.at[n], tsem.at[0, n], tsem.at[1, n], other)

    fetches = [
        pltpu.make_async_copy(src, dst, wsem.at[n])
        for n, (src, dst) in enumerate(((wfg_in, wfg), (wfu_in, wfu), (wfd_in, wfd)))
    ]

    @pl.when(i == 4)
    def _():
        for fetch in fetches:
            fetch.wait()

    @pl.when(i == 0)
    def _():
        for fetch in fetches:
            fetch.start()
        greet_head()
        state[...] = in_ref[...]
        acc[...] = jnp.zeros_like(acc)
        st_s[...] = jnp.zeros_like(st_s)
        pl.semaphore_wait(pltpu.get_barrier_semaphore(), 3)

    @pl.when((i >= 6) & (i - 6 <= last))
    def _():
        t = i - 6
        own_mate(t).wait_recv()
        onward(t).wait_recv()
        squares = jnp.zeros((TILE, 1), F32)
        for j in range(4):
            hj = hg[t, j].astype(F32)
            squares = squares + jnp.sum(hj * hj, axis=1, keepdims=True)
        inv = lax.rsqrt(squares / MODEL_WIDTH + EPS)
        inv_o[...] = jnp.broadcast_to(inv, (TILE, 128))
        for j in range(4):
            cols = slice(j * BLOCK, (j + 1) * BLOCK)
            nf_s[:, cols] = (hg[t, j].astype(F32) * inv * gain_ref[:, cols].astype(F32)).astype(BF16)
        nf = nf_s[...]
        fg = dot_nt(nf, wfg[...])
        fu = dot_nt(nf, wfu[...])
        sig = jax.nn.sigmoid(fg)
        silu = fg * sig
        act = (silu * fu).astype(BF16)
        cg = cg_ref[...]
        for j in range(4):
            pp[t, j] = dot_nn(act, wfd[:, j * BLOCK : (j + 1) * BLOCK]).astype(BF16)
        for which in range(2):
            pair(pp, mp, psem, t, which).start()
        gact = dot_nt(cg, wfd[...])
        gfg = (gact * fu * (sig * (1.0 + fg * (1.0 - sig)))).astype(BF16)
        gfu = (gact * silu).astype(BF16)
        stat = jnp.zeros((TILE, 1), F32)
        for j in range(4):
            rows = slice(j * BLOCK, (j + 1) * BLOCK)
            gj = dot_nn(gfg, wfg[:, rows]) + dot_nn(gfu, wfu[:, rows])
            stat = stat + jnp.sum(gj * nf_s[:, rows].astype(F32), axis=1, keepdims=True)
            pg[t, j] = gj.astype(BF16)
        for which in range(2):
            pair(pg, mg, gsem, t, which).start()
        st_s[pl.ds(t, 1), :] = jnp.broadcast_to(stat, (TILE, 128)).T[0:1, :]
        acc[0:hidden, :] += dot_tn(gfg, nf)
        acc[hidden : 2 * hidden, :] += dot_tn(gfu, nf)
        acc[2 * hidden : 3 * hidden, :] += dot_tn(act, cg)

    @pl.when((i >= 5) & (i - 5 <= last))
    def _():
        t = i - 5
        own_cross(t).wait_recv()
        onward(t).start()

    @pl.when((i >= 3) & (i - 3 <= last))
    def _():
        t = i - 3
        over(t).wait_recv()
        rows = pl.ds(pl.multiple_of(t * TILE, TILE), TILE)
        h = x_ref[rows, :].astype(F32) + (own[lax.rem(t, 4)] + rc[t].astype(F32))
        h_o[...] = h
        hg[t, me] = h.astype(BF16)
        own_cross(t).start()
        own_mate(t).start()

    @pl.when((i >= 1) & (i - 1 <= last))
    def _():
        t = i - 1
        pair(pa, ma, asem, t, 0).wait_recv()
        pair(pa, ma, asem, t, 1).wait_recv()
        sc[t] = (pa[t, cross].astype(F32) + ma[t, 1].astype(F32)).astype(BF16)
        over(t).start()
        own[lax.rem(t, 4)] = pa[t, me].astype(F32) + ma[t, 0].astype(F32)

    @pl.when(i <= last)
    def _():
        t = i
        for c in range(PER):
            rows = slice(c * SPAN, (c + 1) * SPAN)
            scaled = (keep_ref[t, c : c + 1, :] * e_ref[0, c : c + 1, :]) * state[...]
            low = scaled.astype(BF16)
            ws_o[c] = low
            state[...] = scaled + u_ref[c]
            oo_o[rows, :] = o_ref[rows, 256:512] + dot_nt(f_ref[rows, :].astype(BF16), low)
        o = oo_o[...]
        gz = o_ref[:, 0:256]
        inv = lax.rsqrt(jnp.mean(o * o, axis=1, keepdims=True) + EPS)
        gated = (o * inv * gg_ref[...].astype(F32) * (gz * jax.nn.sigmoid(gz))).astype(BF16)
        gated_o[...] = gated
        for j in range(4):
            pa[t, j] = dot_nn(gated, wout[:, j * BLOCK : (j + 1) * BLOCK]).astype(BF16)
        pair(pa, ma, asem, t, 1).start()
        pair(pa, ma, asem, t, 0).start()

    @pl.when((i >= 7) & (i - 7 <= last))
    def _():
        t = i - 7
        for which in range(2):
            pair(pp, mp, psem, t, which).wait_recv()
            pair(pg, mg, gsem, t, which).wait_recv()
        psend_o[...] = (pp[t, cross].astype(F32) + mp[t, 1].astype(F32)).astype(BF16)
        pown_o[...] = pp[t, me].astype(F32) + mp[t, 0].astype(F32)
        gs = (pg[t, cross].astype(F32) + mg[t, 1].astype(F32)).astype(BF16)
        gsend_o[...] = gs

        @pl.when(t < some)
        def _():
            gxs[t] = gs

        gown_o[...] = pg[t, me].astype(F32) + mg[t, 0].astype(F32)

    @pl.when(i == some + 6)
    def _():
        for t in range(some):
            early(t).start()

    @pl.when(i == last + 6)
    def _():
        for n, other in enumerate((mate, cross, far)):
            stats(n, other).start()

    @pl.when(i == last + 7)
    def _():
        used = 3 * hidden // 16

        def unit(r, carry):
            wide_o[r] = acc[pl.ds(pl.multiple_of(r * 16, 16), 16), :].astype(BF16)
            return carry

        lax.fori_loop(0, used, unit, 0)
        for n, other in enumerate((mate, cross, far)):
            stats(n, other).wait()
        for t in range(some):
            early(t).wait()
            gx_o[t * TILE : (t + 1) * TILE, :] = gxr[t]
        stat_o[...] = (st_s[...] + st_r[0]) + (st_r[1] + st_r[2])

        def out(t, carry):
            for which in range(2):
                pair(pa, ma, asem, t, which).wait_send()
                pair(pp, mp, psem, t, which).wait_send()
                pair(pg, mg, gsem, t, which).wait_send()
            over(t).wait_send()
            own_cross(t).wait_send()
            own_mate(t).wait_send()
            onward(t).wait_send()
            return carry

        lax.fori_loop(0, tiles, out, 0)


def ffn(x, keep, inc, gg, gain, wout, wfg, wfu, wfd, f, o, u, e, cg):
    rows = x.shape[0]
    tiles = rows // TILE
    hidden, width = wfg.shape
    units = 3 * hidden // 16
    some = tiles - 3
    assert 3 < tiles <= 8 and hidden % 16 == 0
    ts = functools.partial(tile_spec, tiles)
    ins = (x, keep, inc, gg, gain, wout)
    outs = [
        ((rows, BLOCK), BF16, ts((TILE, BLOCK), 0)),
        ((rows, HV), F32, ts((TILE, HV), 0)),
        ((rows // SPAN, HV, HK), BF16, ts((PER, HV, HK), 0)),
        ((rows, BLOCK), F32, ts((TILE, BLOCK), 3)),
        ((rows, 128), F32, ts((TILE, 128), 6)),
        ((rows, BLOCK), BF16, ts((TILE, BLOCK), 7)),
        ((rows, BLOCK), F32, ts((TILE, BLOCK), 7)),
        ((rows, BLOCK), BF16, ts((TILE, BLOCK), 7)),
        ((rows, BLOCK), F32, ts((TILE, BLOCK), 7)),
        ((8, TILE), F32, whole((8, TILE))),
        ((units, 16, width), BF16, whole((units, 16, width))),
        ((some * TILE, BLOCK), BF16, whole((some * TILE, BLOCK))),
    ]
    tiled = lambda n: pltpu.VMEM((tiles, n, TILE, BLOCK), BF16)
    return pl.pallas_call(
        functools.partial(ffn_kernel, tiles),
        grid=(tiles + 7,),
        out_shape=[jax.ShapeDtypeStruct(s, d) for s, d, _ in outs],
        in_specs=[whole(a.shape) for a in ins]
        + [pl.BlockSpec(memory_space=pl.ANY)] * 3
        + [
            ts((TILE, 128), 0), ts((TILE, 512), 0), ts((PER, HV, HK), 0), ts((1, 8, 128), 0),
            ts((TILE, MODEL_WIDTH), 6),
        ],
        out_specs=[s for _, _, s in outs],
        scratch_shapes=[
            pltpu.VMEM((HV, HK), F32),
            tiled(4), tiled(4), tiled(4), tiled(2), tiled(2), tiled(2),
            pltpu.VMEM((tiles, TILE, BLOCK), BF16),
            pltpu.VMEM((tiles, TILE, BLOCK), BF16),
            pltpu.VMEM((4, TILE, BLOCK), F32),
            tiled(4),
            pltpu.VMEM((TILE, MODEL_WIDTH), BF16),
            pltpu.VMEM((3 * hidden, width), F32),
            pltpu.VMEM((hidden, width), BF16),
            pltpu.VMEM((hidden, width), BF16),
            pltpu.VMEM((hidden, width), BF16),
            pltpu.VMEM((8, TILE), F32),
            pltpu.VMEM((3, 8, TILE), F32),
            pltpu.VMEM((some, TILE, BLOCK), BF16),
            pltpu.VMEM((some, TILE, BLOCK), BF16),
            pltpu.SemaphoreType.DMA((4, tiles)),
            pltpu.SemaphoreType.DMA((4, tiles)),
            pltpu.SemaphoreType.DMA((4, tiles)),
            pltpu.SemaphoreType.DMA((2, tiles)),
            pltpu.SemaphoreType.DMA((6, tiles)),
            pltpu.SemaphoreType.DMA((2, 3)),
            pltpu.SemaphoreType.DMA((3,)),
            pltpu.SemaphoreType.DMA((2, some)),
        ],
        compiler_params=pltpu.CompilerParams(
            collective_id=2, has_side_effects=True, vmem_limit_bytes=VMEM_LIMIT,
            dimension_semantics=("arbitrary",),
        ),
        name="ffn",
    )(*ins, wfg, wfu, wfd, f, o, u, e, cg)


LAGS = (2, 2, 2)
CYCLE = 5
WAIT = 0


def levels(count):
    bits = count.bit_length() - 1
    assert 1 << bits == count
    return bits


def folds(count):
    return count == 8


class Sum:
    def __init__(self, count, sources, dest, segments, scratch):
        self.count = count
        self.bits = levels(count)
        self.folds = folds(count)
        self.sources = sources
        self.dest = dest
        self.segments = segments
        self.got = scratch[: self.bits]
        self.ring, self.side_sum, self.line_sum = scratch[self.bits : self.bits + 3]
        self.sems, self.lsem = scratch[self.bits + 3 :]

    def slot(self, k):
        if not self.folds:
            return k
        odd = lax.rem(lax.rem(k, CYCLE), 2)
        return ((CYCLE + 1) // 2 - odd) * lax.div(k, CYCLE) + lax.div(lax.rem(k, CYCLE), 2)

    def where(self, k, level):
        place = lax.axis_index("seq")
        turn = 1 if self.folds else lax.div(lax.rem(k, 4), 3)
        start = 0
        for step in range(level + 1):
            stride = 1 << step
            if step < 2:
                stride = stride + turn * (3 - 2 * stride)
            bit = lax.rem(lax.div(place, stride), 2)
            if step == level:
                return bit, place + stride * (1 - 2 * bit), start
            start = start + bit * (self.count >> (step + 1))

    def own(self, k):
        bit, _, _ = self.where(k, 0)
        half = self.count >> 1
        return pltpu.make_async_copy(
            self.sources[0](k, bit * half, half), self.dest(k, bit * half, half), self.lsem.at[k]
        )

    def scatter(self, k, level, kind):
        bit, partner, start = self.where(k, level)
        half = self.count >> (level + 1)
        if level == 0:
            src = self.sources[kind](k, start + (1 - bit) * half, half)
        else:
            src = self.got[level - 1].at[self.slot(k), pl.ds((1 - bit) * half, half)]
        return to_seq(src, self.got[level].at[self.slot(k)], self.sems.at[0, level, k], self.sems.at[1, level, k], partner)

    def gather(self, k, level):
        bit, partner, start = self.where(k, level)
        half = self.count >> (level + 1)
        mine = start + bit * half
        ref = self.dest(k, mine, half)
        return to_seq(ref, ref, self.sems.at[2, level, k], self.sems.at[3, level, k], partner)

    def gathered(self, k, level):
        bit, partner, start = self.where(k, level)
        half = self.count >> (level + 1)
        ref = self.dest(k, start + (1 - bit) * half, half)
        return to_seq(ref, ref, self.sems.at[2, level, k], self.sems.at[3, level, k], partner)

    def begin(self, k, kind):
        self.scatter(k, 0, kind).start()
        if kind == 0:
            self.own(k).start()

    def add(self, k, kind, level):
        bit, _, start = self.where(k, level)
        half = self.count >> (level + 1)
        self.scatter(k, level, kind).wait_recv()
        if level == 0 and kind == 0:
            self.own(k).wait()
            mine = self.dest(k, bit * half, half)[...]
        elif level == 0:
            mine = self.sources[kind](k, bit * half, half)[...]
        else:
            mine = self.got[level - 1][self.slot(k), pl.ds(bit * half, half)]
        total = (self.got[level][self.slot(k)].astype(F32) + mine.astype(F32)).astype(BF16)
        if level + 1 < self.bits:
            self.got[level][self.slot(k)] = total
            self.scatter(k, level + 1, kind).start()
        else:
            self.dest(k, start + bit * half, half)[...] = total
            self.gather(k, level).start()

    def pass_on(self, k, kind, level):
        self.gathered(k, level).wait_recv()
        if level > 0:
            self.gather(k, level - 1).start()

    def spot(self):
        place = lax.axis_index("seq")
        side = lax.rem(place, 2)
        z = lax.div(place, 2)
        low = lax.rem(z, 2)
        end = low == lax.div(z, 2)
        return side, place + 1 - 2 * side, place + 2 * (1 - 2 * low), 2 * (3 - z) + side, end

    def half_of(self, k, which):
        half = self.count >> 1
        return self.dest(k, which * half, half)

    def fold_own(self, k):
        half = self.count >> 1
        return pltpu.make_async_copy(
            self.sources[0](k, self.spot()[0] * half, half), self.ring.at[lax.rem(k, 4)], self.lsem.at[k]
        )

    def fold_side(self, k, kind):
        side, twin, _, _, _ = self.spot()
        half = self.count >> 1
        src = self.sources[kind](k, (1 - side) * half, half)
        return to_seq(src, self.side_sum.at[self.slot(k)], self.sems.at[0, 0, k], self.sems.at[1, 0, k], twin)

    def fold_in(self, k):
        n = self.slot(k)
        return to_seq(
            self.side_sum.at[n], self.line_sum.at[n], self.sems.at[0, 1, k], self.sems.at[1, 1, k], self.spot()[2]
        )

    def fold_cross(self, k):
        side, _, _, other, _ = self.spot()
        return to_seq(
            self.line_sum.at[self.slot(k)], self.half_of(k, side), self.sems.at[0, 2, k], self.sems.at[1, 2, k], other
        )

    def fold_out(self, k):
        side, _, across, _, _ = self.spot()
        ref = self.half_of(k, side)
        return to_seq(ref, ref, self.sems.at[2, 1, k], self.sems.at[3, 1, k], across)

    def fold_back(self, k, mine):
        side, twin, _, _, _ = self.spot()
        ref = self.half_of(k, side if mine else 1 - side)
        return to_seq(ref, ref, self.sems.at[2, 0, k], self.sems.at[3, 0, k], twin)

    def fold_begin(self, k, kind):
        self.fold_side(k, kind).start()
        if kind == 0:
            self.fold_own(k).start()

    def fold_1(self, k, kind):
        side, _, _, _, end = self.spot()
        half = self.count >> 1
        n = self.slot(k)
        self.fold_side(k, kind).wait_recv()
        if kind == 0:
            self.fold_own(k).wait()
            mine = self.ring[lax.rem(k, 4)]
        else:
            mine = self.sources[kind](k, side * half, half)[...]
        self.side_sum[n] = (self.side_sum[n].astype(F32) + mine.astype(F32)).astype(BF16)

        @pl.when(end)
        def _():
            self.fold_in(k).start()

    def fold_2(self, k, kind):
        n = self.slot(k)

        @pl.when(jnp.logical_not(self.spot()[4]))
        def _():
            self.fold_in(k).wait_recv()
            self.line_sum[n] = (self.line_sum[n].astype(F32) + self.side_sum[n].astype(F32)).astype(BF16)
            self.fold_cross(k).start()

    def fold_3(self, k, kind):
        side, _, _, _, end = self.spot()

        @pl.when(jnp.logical_not(end))
        def _():
            self.fold_cross(k).wait_recv()
            ref = self.half_of(k, side)
            ref[...] = (ref[...].astype(F32) + self.line_sum[self.slot(k)].astype(F32)).astype(BF16)
            self.fold_out(k).start()
            self.fold_back(k, True).start()

    def fold_4(self, k, kind):
        end = self.spot()[4]

        @pl.when(end)
        def _():
            self.fold_out(k).wait_recv()
            self.fold_back(k, True).start()

        @pl.when(jnp.logical_not(end))
        def _():
            self.fold_back(k, False).wait_recv()

    def fold_5(self, k, kind):
        @pl.when(self.spot()[4])
        def _():
            self.fold_back(k, False).wait_recv()

    def at(self, i, stage, body, fold):
        for kind, (low, high, gap) in enumerate(self.segments):
            k = i - gap - LAGS[kind] * stage
            here = (k >= low) & (k < high)
            if not self.folds:

                @pl.when(here)
                def _(kind=kind, k=k):
                    body(k, kind)

                continue
            odd = lax.rem(lax.rem(jnp.maximum(k, 0), CYCLE), 2) == 1

            @pl.when(here & odd)
            def _(kind=kind, k=k):
                body(k, kind)

            if fold is not None:

                @pl.when(here & jnp.logical_not(odd))
                def _(kind=kind, k=k):
                    fold(k, kind)

    def step(self, i):
        stages = []
        for level in range(self.bits):
            stages.append(functools.partial(self.add, level=level))
        for level in range(self.bits - 1, -1, -1):
            stages.append(functools.partial(self.pass_on, level=level))
        folded = [self.fold_1, self.fold_2, self.fold_3, self.fold_4, self.fold_5]
        folded = folded + [None] * (len(stages) - len(folded))
        for s in range(len(stages) - 1, -1, -1):
            self.at(i, s + 1, stages[s], folded[s])
        self.at(i, 0, self.begin, self.fold_begin)

    def finish(self):
        def halving(k, kind):
            for level in range(self.bits):
                self.scatter(k, level, kind).wait_send()
                self.gather(k, level).wait_send()

        def folding(k, kind):
            end = self.spot()[4]
            self.fold_side(k, kind).wait_send()
            self.fold_back(k, True).wait_send()

            @pl.when(end)
            def _():
                self.fold_in(k).wait_send()

            @pl.when(jnp.logical_not(end))
            def _():
                self.fold_cross(k).wait_send()
                self.fold_out(k).wait_send()

        def one(kind, k, carry):
            if not self.folds:
                halving(k, kind)
                return carry
            odd = lax.rem(lax.rem(k, CYCLE), 2) == 1

            @pl.when(odd)
            def _():
                halving(k, kind)

            @pl.when(jnp.logical_not(odd))
            def _():
                folding(k, kind)

            return carry

        for kind, (low, high, _) in enumerate(self.segments):
            lax.fori_loop(low, high, functools.partial(one, kind), 0)

    @staticmethod
    def scratch(count, parts, first, unit):
        bits = levels(count)
        odd = parts
        even = 1
        half = 16
        if folds(count):
            odd = sum(1 for k in range(parts) if k % CYCLE % 2 == 1)
            even = parts - odd
            half = count // 2
        one = (1,) + unit if not folds(count) else (half,) + unit
        return [pltpu.VMEM((odd, count >> (level + 1)) + unit, BF16) for level in range(bits)] + [
            pltpu.VMEM((4 if folds(count) else 1,) + one, BF16),
            pltpu.VMEM((even,) + one, BF16),
            pltpu.VMEM((even,) + one, BF16),
            pltpu.SemaphoreType.DMA((4, bits, parts)),
            pltpu.SemaphoreType.DMA((first,)),
        ]


def plan(count, wide, tiles):
    second = tiles + 3 + WAIT
    a = wide // count
    b = a + 32 // count
    c = b + up_to(34 + wide % count, count) // count
    gap = max(0, second - a)
    late = max(gap, second + tiles - b, second + tiles + 3 - (c - 1))
    return (0, a, 0), (a, b, gap), (b, c, late)


def last_step(count, segments):
    latest = 0
    for kind, (low, high, gap) in enumerate(segments):
        for k in range(low, high):
            stages = 2 * levels(count) - (1 if folds(count) and k % CYCLE % 2 == 0 else 0)
            latest = max(latest, k + gap + stages * LAGS[kind])
    return latest


def finish_kernel(fg, fu, fd, first, second, tail, extra, dfg, dfu, dfd, dq, dk, dv, dg, dwo, dr, dup, dag, dffg, db, dgg):
    for src, dst in ((fg, dfg), (fu, dfu), (fd, dfd)):
        dst[...] = src[...].reshape(dst.shape).astype(F32)

    @pl.when(pl.program_id(0) == pl.num_programs(0) - 1)
    def _():
        tail_rows = extra.shape[0] * 16
        dfd[dfd.shape[0] - tail_rows :, :] = extra[...].reshape(tail_rows, -1).astype(F32)

    rows = first[...].reshape(-1, 512).astype(F32)
    dg[...] = rows[:, 0:256]
    dwo[...] = rows[:, 256:512].T
    rows = second[...].reshape(-1, 512).astype(F32)
    dq[...] = rows[:, 0:128]
    dk[...] = rows[:, 128:256]
    dv[...] = rows[:, 256:512]
    dr[...] = tail[0].astype(F32)
    last = tail[1].astype(F32)
    dup[...] = last[:, 0:128]
    dag[...] = last[0:1, 128:384]
    dffg[...] = last[1:2, 128:384]
    db[...] = last[3:4, 128:256]
    dgg[...] = last[2:3, 128:384]


def finish(units, hidden, wide, count):
    first = wide // count * count
    rest = wide % count
    width = units.shape[2]
    steps = 4
    per = hidden // 16 // steps
    assert per * steps * 16 == hidden and 0 < rest <= per
    rows = MODEL_WIDTH // steps
    wide_spec = lambda n: pl.BlockSpec((per, 16, width), lambda i: (i + n * steps, 0, 0))
    half_spec = lambda n: pl.BlockSpec(
        (pl.Element(rows // 16), pl.Element(16), pl.Element(512)),
        lambda i: (first + n + (i % 2) * (rows // 16), 0, (i // 2) * 512),
    )
    down = lambda r, c: ((r * steps, c), pl.BlockSpec((r, c), lambda i: (i, 0)))
    full = lambda r, c: ((r, c), pl.BlockSpec((r, c), lambda i: (0, 0)))
    outs = [
        down(per * 16, width), down(per * 16, width), down(per * 16, width),
        down(rows, 128), down(rows, 128), down(rows, 256), down(rows, 256),
        ((256, MODEL_WIDTH), pl.BlockSpec((256, rows), lambda i: (0, i))),
        full(RANK, MODEL_WIDTH), full(RANK, 128), full(1, 256), full(1, 256), full(1, 128), full(1, 256),
    ]
    return pl.pallas_call(
        finish_kernel,
        grid=(steps,),
        out_shape=[jax.ShapeDtypeStruct(s, F32) for s, _ in outs],
        in_specs=[
            wide_spec(0), wide_spec(1), wide_spec(2),
            half_spec(0), half_spec(32),
            pl.BlockSpec((pl.Element(2), pl.Element(16), pl.Element(width)), lambda i: (first + 64, 0, 0)),
            pl.BlockSpec((pl.Element(rest), pl.Element(16), pl.Element(width)), lambda i: (first + 66, 0, 0)),
        ],
        out_specs=[s for _, s in outs],
        compiler_params=pltpu.CompilerParams(
            vmem_limit_bytes=VMEM_LIMIT, dimension_semantics=("arbitrary",)
        ),
        name="finish",
    )(units, units, units, units, units, units, units)


def back_kernel(
    tiles, count, segments,
    keep_ref, d_ref, stat_ref, gg_ref, again, fgain, wout, wq, wk, wv, wg, wr, rup,
    wide_in, gsend, psend, x_ref, c_ref, gx, gown, h1, invf, f1, gz_ref, oo_ref, gated, ws1, b1, e1,
    na1, f2, b2, ws2, e2, na, h2, pown, inva,
    gt_o, lo_o, units_o,
    tri, rg, gh, gb, gzs, gw, gqd, gkd, gv, state, sbuf, rbuf,
    gcat, mn, sc, rc, own, st_s, st_r, both, joint, small, held, wide_o, few, lot,
    gsem, psem, hsem, nsem, csem, tsem, esend, erecv, wsem, jsem, *rest,
):
    i = pl.program_id(0)
    me, mate, cross, far = peers()
    place = lax.axis_index("seq")
    last = tiles - 1
    second = tiles + 3 + WAIT

    some = tiles - 3

    def rows_of(t):
        return pl.ds(pl.multiple_of(t * TILE, TILE), TILE)

    def own_cols(ref):
        return ref[:, pl.ds(pl.multiple_of(me * BLOCK, BLOCK), BLOCK)].astype(F32)

    def grads(t):
        return to_head(gsend.at[rows_of(t)], rg.at[t], gsem.at[0, t], gsem.at[1, t], cross)

    def feeds(t):
        return to_head(psend.at[rows_of(t)], rg.at[t], psem.at[0, t], psem.at[1, t], cross)

    def own_mate(t):
        return to_head(gb.at[t, me], gb.at[t, me], hsem.at[0, t], hsem.at[1, t], mate)

    def own_cross(t):
        return to_head(gb.at[t, me], gb.at[t, me], hsem.at[2, t], hsem.at[3, t], cross)

    def onward(t):
        return to_head(gb.at[t, cross], gb.at[t, cross], hsem.at[4, t], hsem.at[5, t], mate)

    def pair(t, which):
        block = mate if which == 0 else far
        return to_head(gb.at[t, block], mn.at[t, which], nsem.at[2 * which, t], nsem.at[2 * which + 1, t], mate)

    def over(t):
        return to_head(sc.at[t], rc.at[t], csem.at[0, t], csem.at[1, t], cross)

    def stats(t, n, other):
        return to_head(st_s.at[t], st_r.at[t, n], tsem.at[0, n, t], tsem.at[1, n, t], other)

    first = wide_in.shape[0] // count
    spare = wide_in.shape[0] - first * count
    parts = wide_o.shape[0] // count
    ready = second + tiles
    feed = ready + 4

    def early(k, start, n):
        return wide_in.at[pl.ds(k * count + start, n)]

    def middle(k, start, n):
        return few.at[pl.ds((k - segments[1][0]) * count + start, n)]

    def late(k, start, n):
        return lot.at[pl.ds((k - segments[2][0]) * count + start, n)]

    def place_of(k, start, n):
        return wide_o.at[pl.ds(k * count + start, n)]

    wide_sum = Sum(count, (early, middle, late), place_of, segments, rest)

    @pl.when(i == 0)
    def _():
        greet_head()
        greet_seq(count)
        pl.semaphore_wait(pltpu.get_barrier_semaphore(), 3 + count - 1)
        for n in range(tiles - some):
            grads(last - n).start()
        r = lax.broadcasted_iota(jnp.int32, (TILE, TILE), 0)
        c = lax.broadcasted_iota(jnp.int32, (TILE, TILE), 1)
        tri[...] = jnp.where(((r >> 6) == (c >> 6)) & (r > c), 1.0, 0.0).astype(BF16)
        state[...] = jnp.zeros_like(state)
        both[...] = jnp.zeros_like(both)
        joint[...] = jnp.zeros_like(joint)
        small[...] = jnp.zeros_like(small)

    def share(n, other):
        return to_head(joint, held.at[me], jsem.at[0, n], jsem.at[1, n], other)

    spare_copy = pltpu.make_async_copy(
        wide_in.at[pl.ds(first * count, spare)], lot.at[pl.ds(34, spare)], wsem.at[2]
    )

    def lay(dst, col):
        def copy(r, carry):
            for side in range(2):
                rows = pl.ds(pl.multiple_of(side * (MODEL_WIDTH // 2) + r * 16, 16), 16)
                dst[r, :, side * 512 : (side + 1) * 512] = both[rows, col : col + 512].astype(BF16)
            return carry

        lax.fori_loop(0, 32, copy, 0)

    @pl.when(i == second)
    def _():
        lay(few, 512)

    @pl.when(i == ready)
    def _():
        held[me] = joint[...]
        for n, other in enumerate((mate, cross, far)):
            share(n, other).start()
        lay(lot, 0)
        lot[32:] = jnp.zeros((lot.shape[0] - 32,) + lot.shape[1:], BF16)
        spare_copy.start()

    @pl.when(i == ready + 3)
    def _():
        spare_copy.wait()
        for n, other in enumerate((mate, cross, far)):
            to_head(joint, held.at[other], jsem.at[0, n], jsem.at[1, n], other).wait()
        base = 32
        sums = (held[0] + held[1]) + (held[2] + held[3])
        lot[base] = sums[0:RANK].astype(BF16)
        lot[base + 1] = jnp.zeros((16, MODEL_WIDTH), BF16)
        small[2:3, 128:384] = sums[16:17, 0:256]
        lot[base + 1, :, 0:512] = small[...].astype(BF16)

    wide_sum.step(i)

    @pl.when(i == 1)
    def _():
        def weave(r, carry):
            rows = pl.ds(pl.multiple_of(r * 16, 16), 16)
            lot[r, :, 0:128] = wq[rows, :]
            lot[r, :, 128:256] = wk[rows, :]
            lot[r, :, 256:512] = wv[rows, :]
            lot[r, :, 512:768] = wg[rows, :]
            return carry

        lax.fori_loop(0, MODEL_WIDTH // 16, weave, 0)

    @pl.when((i >= 2) & (i - 2 <= last))
    def _():
        t = last - (i - 2)
        own_cross(t).wait_recv()
        onward(t).start()

    @pl.when(i <= last)
    def _():
        t = last - i

        @pl.when(t >= some)
        def _():
            grads(t).wait_recv()

        @pl.when(t < some)
        def _():
            rg[t] = gx[...]

        gnf = gown[...] + rg[t].astype(F32)
        inv = invf[...][:, 0:1]
        hn = h1[...].astype(BF16).astype(F32) * inv
        row = stat_ref[pl.ds(t, 1), :]
        stat = jnp.broadcast_to(row, (128, TILE)).T[:, 0:1]
        grad = c_ref[...].astype(F32) + inv * (own_cols(fgain) * gnf - hn * (stat / MODEL_WIDTH))
        small[1:2, 128:384] += jnp.sum(gnf * hn, axis=0, keepdims=True)
        gh[t] = grad
        gb[t, me] = grad.astype(BF16)
        own_cross(t).start()
        own_mate(t).start()

    half = tiles // 2

    def some_feeds(low, high, at):
        @pl.when((i >= at) & (low + 2 * (i - at) < high))
        def _():
            n = low + 2 * (i - at)
            feeds(last - n).start()

            @pl.when(n + 1 < high)
            def _():
                feeds(last - n - 1).start()

    some_feeds(0, half, last + 2)
    some_feeds(half, tiles, ready)

    @pl.when((i >= 3) & (i - 3 <= last))
    def _():
        t = last - (i - 3)
        own_mate(t).wait_recv()
        onward(t).wait_recv()
        gt = jnp.zeros((TILE, BLOCK), F32)
        for j in range(4):
            cols = slice(j * BLOCK, (j + 1) * BLOCK)
            gt = gt + dot_nt(gb[t, j], wout[:, cols])
            both[cols, 768:1024] += dot_tn(gb[t, j], gated[...])
        o = oo_ref[...]
        gz = gz_ref[...]
        inv = lax.rsqrt(jnp.mean(o * o, axis=1, keepdims=True) + EPS)
        on = o * inv
        sig = jax.nn.sigmoid(gz)
        gn = gt * (gz * sig)
        joint[16:17, 0:256] += jnp.sum(gn * on, axis=0, keepdims=True)
        gain = gg_ref[...].astype(F32)
        ggz = (gt * on * gain * (sig * (1.0 + gz * (1.0 - sig)))).astype(BF16)
        gzs[t] = ggz
        both[:, 512:768] += dot_tn(na1[...], ggz)
        p = gn * gain
        go = (inv * (p - on * jnp.mean(p * on, axis=1, keepdims=True))).astype(BF16)
        qd = f1[:, 0:128].astype(BF16)
        kd = f1[:, 128:256].astype(BF16)
        v = b1[:, 0:256]
        causal, _ = span_masks(TILE, TILE)
        ga = jnp.where(causal, dot_nt(go, v), 0.0).astype(BF16)
        gqd[t] = dot_nn(ga, kd)
        gkd[t] = dot_tn(ga, qd)
        gv[t] = dot_tn(b1[:, 256:512], go)
        for c in range(PER - 1, -1, -1):
            rows = slice(c * SPAN, (c + 1) * SPAN)
            gqd[t, rows, :] += dot_nn(go[rows], ws1[c])
            fresh = dot_tn(go[rows], qd[rows])
            gw[t * PER + c] = fresh
            through = keep_ref[t, c : c + 1, :] * e1[0, c : c + 1, :]
            state[...] = through * (fresh + state[...])

    @pl.when(i == last + 3)
    def _():
        sbuf[...] = jnp.zeros_like(sbuf)
        sbuf[0:HV, :] = state[...].astype(BF16)
        d = d_ref[...]
        hi = d.astype(BF16).astype(F32)
        first = lax.broadcasted_iota(jnp.int32, (16, 128), 0) < 8
        both = jnp.where(first, jnp.concatenate([hi, hi], axis=0), jnp.concatenate([d - hi, d - hi], axis=0))
        sbuf[HV : HV + 16, :] = both.astype(BF16)

        def send(p, carry):
            to_seq(sbuf, rbuf.at[place], esend.at[p], erecv.at[place], p).start()
            return carry

        lax.fori_loop(0, place, send, 0)

    @pl.when(i == second)
    def _():
        def free(t, carry):
            own_cross(t).wait_send()
            own_mate(t).wait_send()
            onward(t).wait_send()
            return carry

        lax.fori_loop(0, tiles, free, 0)
        state[...] = jnp.zeros_like(state)

        def join(n, carry):
            p = count - 1 - n
            to_seq(sbuf, rbuf.at[p], esend.at[p], erecv.at[p], place).wait_recv()
            got = rbuf[p].astype(F32)
            d = got[HV : HV + 1] + got[HV + 8 : HV + 9]
            state[...] = got[0:HV] + d * state[...]
            return carry

        lax.fori_loop(0, count - 1 - place, join, 0)

    @pl.when((i >= second + 3) & (i - second - 3 <= last))
    def _():
        t = last - (i - second - 3)
        over(t).wait_recv()
        for n, other in enumerate((mate, cross, far)):
            stats(t, n, other).wait_recv()
        gna = own[lax.rem(t, 3)] + rc[t].astype(F32)
        inv = inva[...][:, 0:1]
        xn = x_ref[...].astype(F32) * inv
        row = (st_s[t] + st_r[t, 0]) + (st_r[t, 1] + st_r[t, 2])
        stat = jnp.broadcast_to(row[0:1], (128, TILE)).T[:, 0:1]
        gt_o[...] = gh[t] + inv * (own_cols(again) * gna - xn * (stat / MODEL_WIDTH))
        small[0:1, 128:384] += jnp.sum(gna * xn, axis=0, keepdims=True)

    @pl.when((i >= second + 1) & (i - second - 1 <= last))
    def _():
        t = last - (i - second - 1)
        pair(t, 0).wait_recv()
        pair(t, 1).wait_recv()
        sc[t] = (gb[t, cross].astype(F32) + mn[t, 1].astype(F32)).astype(BF16)
        over(t).start()
        own[lax.rem(t, 3)] = gb[t, me].astype(F32) + mn[t, 0].astype(F32)

    @pl.when((i >= second) & (i - second <= last))
    def _():
        t = last - (i - second)
        qf = f2[:, 0:128]
        kf = f2[:, 128:256]
        kd = kf.astype(BF16)
        pieces = [None] * PER
        for c in range(PER - 1, -1, -1):
            rows = slice(c * SPAN, (c + 1) * SPAN)
            low = state[...].astype(BF16)
            gkd[t, rows, :] += dot_nn(b2[rows, 0:256], low)
            gv[t, rows, :] += dot_nt(kd[rows], low)
            ge = gw[t * PER + c] + state[...]
            pieces[c] = jnp.broadcast_to(jnp.sum(ge * ws2[c].astype(F32), axis=0, keepdims=True), (SPAN, HK))
            state[...] = (keep_ref[t, c : c + 1, :] * e2[0, c : c + 1, :]) * ge
        gq = gqd[t]
        gk = gkd[t]
        diff = gq * qf - gk * kf
        gg = jnp.concatenate(pieces, axis=0) - fold(dot_nn(tri[...], three(diff)))
        glogit = gg * f2[:, 512:640]
        small[3:4, 128:256] += jnp.sum(glogit, axis=0, keepdims=True)
        hi = glogit.astype(BF16)
        lo = (glogit - hi.astype(F32)).astype(BF16)
        glr = dot_nt(hi, rup[...]) + dot_nt(lo, rup[...])
        lr = b2[:, 512 : 512 + RANK]
        small[:, 0:128] += dot_tn(lr, hi) + dot_tn(lr, lo)
        glr = glr.astype(BF16)
        joint[0:RANK, :] += dot_tn(glr, na[...])
        gcat[:, 0:128] = (gq * f2[:, 256:384]).astype(BF16)
        gcat[:, 128:256] = (gk * f2[:, 384:512]).astype(BF16)
        gcat[:, 256:512] = gv[t].astype(BF16)
        gcat[:, 512:768] = gzs[t]
        g = gcat[...]
        stat = jnp.zeros((TILE, 1), F32)
        for j in range(4):
            cols = slice(j * BLOCK, (j + 1) * BLOCK)
            gj = dot_nt(g, lot[16 * j : 16 * (j + 1), :, 0:768].reshape(BLOCK, 768)) + dot_nn(glr, wr[:, cols])
            stat = stat + jnp.sum(gj * na[:, cols].astype(F32), axis=1, keepdims=True)
            gb[t, j] = gj.astype(BF16)
        pair(t, 1).start()
        pair(t, 0).start()
        st_s[t] = jnp.broadcast_to(stat, (TILE, 128)).T[0:8, :]
        for n, other in enumerate((mate, cross, far)):
            stats(t, n, other).start()
        both[:, 0:512] += dot_tn(na[...], g[:, 0:512])

    @pl.when((i >= feed) & (i - feed <= last))
    def _():
        t = last - (i - feed)
        feeds(t).wait_recv()
        lo_o[...] = (h2[...] + (pown[...] + rg[t].astype(F32))).astype(BF16)

    drained = first + 2 * levels(count) * LAGS[0]
    head_units = pl.ds(0, first * count)
    tail_units = pl.ds(first * count, (parts - first) * count)
    head_copy = pltpu.make_async_copy(wide_o.at[head_units], units_o.at[head_units], wsem.at[0])
    tail_copy = pltpu.make_async_copy(wide_o.at[tail_units], units_o.at[tail_units], wsem.at[1])

    @pl.when(i == drained)
    def _():
        head_copy.start()

    @pl.when(i == pl.num_programs(0) - 1)
    def _():
        tail_copy.start()
        wide_sum.finish()
        tail_copy.wait()
        head_copy.wait()

        def sent(p, carry):
            to_seq(sbuf, rbuf.at[place], esend.at[p], erecv.at[place], p).wait_send()
            return carry

        lax.fori_loop(0, place, sent, 0)

        def out(t, carry):
            @pl.when(t >= some)
            def _():
                grads(t).wait_send()

            feeds(t).wait_send()
            pair(t, 0).wait_send()
            pair(t, 1).wait_send()
            over(t).wait_send()
            for n, other in enumerate((mate, cross, far)):
                stats(t, n, other).wait_send()
            return carry

        lax.fori_loop(0, tiles, out, 0)


def back(fixed, wide, gsend, psend, x, cot, gx, gown, h, invf, f, o, oo, gated, ws, b, e, na, pown, inva):
    rows = h.shape[0]
    tiles = rows // TILE
    count = lax.axis_size("seq")
    second = tiles + 3 + WAIT
    width = MODEL_WIDTH
    segments = plan(count, wide.shape[0], tiles)
    first = segments[0][1]
    parts = segments[2][1]
    units = parts * count
    feed = second + tiles + 4
    steps = max(feed + tiles, last_step(count, segments) + 1)
    ts = functools.partial(tile_spec, tiles, back=True)
    outs = [
        ((rows, BLOCK), F32, ts((TILE, BLOCK), second + 3)),
        ((rows, BLOCK), BF16, ts((TILE, BLOCK), feed)),
        ((units, 16, width), BF16, pl.BlockSpec(memory_space=pl.ANY)),
    ]
    tiled = lambda n: pltpu.VMEM((tiles, n, TILE, BLOCK), BF16)
    flat = lambda n, d: pltpu.VMEM((tiles, TILE, n), d)
    return pl.pallas_call(
        functools.partial(back_kernel, tiles, count, segments),
        grid=(steps,),
        out_shape=[jax.ShapeDtypeStruct(s, d) for s, d, _ in outs],
        in_specs=[whole(a.shape) for a in fixed]
        + [
            pl.BlockSpec(memory_space=pl.ANY), pl.BlockSpec(memory_space=pl.ANY), pl.BlockSpec(memory_space=pl.ANY),
            ts((TILE, BLOCK), second + 3), ts((TILE, BLOCK), 0),
            pl.BlockSpec((TILE, BLOCK), lambda i: (jnp.clip(tiles - 1 - i, 0, tiles - 4), 0)),
            ts((TILE, BLOCK), 0), ts((TILE, BLOCK), 0), ts((TILE, 128), 0),
            ts((TILE, 256), 3), ts((TILE, 256), 3), ts((TILE, 256), 3), ts((TILE, 256), 3),
            ts((PER, HV, HK), 3), ts((TILE, 640), 3), ts((1, 8, 128), 3), ts((TILE, width), 3),
            ts((TILE, 640), second), ts((TILE, 640), second), ts((PER, HV, HK), second), ts((1, 8, 128), second),
            ts((TILE, width), second), ts((TILE, BLOCK), feed), ts((TILE, BLOCK), feed),
            ts((TILE, 128), second + 3),
        ],
        out_specs=[s for _, _, s in outs],
        scratch_shapes=[
            pltpu.VMEM((TILE, TILE), BF16),
            flat(BLOCK, BF16), flat(BLOCK, F32),
            tiled(4),
            flat(BLOCK, BF16),
            pltpu.VMEM((rows // SPAN, HV, HK), F32),
            flat(HK, F32), flat(HK, F32), flat(HV, F32),
            pltpu.VMEM((HV, HK), F32),
            pltpu.VMEM((HV + 16, HK), BF16),
            pltpu.VMEM((count, HV + 16, HK), BF16),
            pltpu.VMEM((TILE, 768), BF16),
            tiled(2), flat(BLOCK, BF16), flat(BLOCK, BF16),
            pltpu.VMEM((3, TILE, BLOCK), F32),
            pltpu.VMEM((tiles, 8, TILE), F32),
            pltpu.VMEM((tiles, 3, 8, TILE), F32),
            pltpu.VMEM((width, width), F32),
            pltpu.VMEM((24, width), F32),
            pltpu.VMEM((16, 512), F32),
            pltpu.VMEM((4, 24, width), F32),
            pltpu.VMEM((units, 16, width), BF16),
            pltpu.VMEM((32, 16, width), BF16),
            pltpu.VMEM((max(width // 16, (parts - segments[2][0]) * count), 16, width), BF16),
            pltpu.SemaphoreType.DMA((2, tiles)),
            pltpu.SemaphoreType.DMA((2, tiles)),
            pltpu.SemaphoreType.DMA((6, tiles)),
            pltpu.SemaphoreType.DMA((4, tiles)),
            pltpu.SemaphoreType.DMA((2, tiles)),
            pltpu.SemaphoreType.DMA((2, 3, tiles)),
            pltpu.SemaphoreType.DMA((count,)),
            pltpu.SemaphoreType.DMA((count,)),
            pltpu.SemaphoreType.DMA((3,)),
            pltpu.SemaphoreType.DMA((2, 3)),
        ]
        + Sum.scratch(count, parts, first, wide.shape[1:]),
        compiler_params=pltpu.CompilerParams(
            collective_id=3, has_side_effects=True, vmem_limit_bytes=VMEM_LIMIT,
            dimension_semantics=("arbitrary",),
        ),
        name="back",
    )(*fixed, wide, gsend, psend, x, cot, gx, gown, h, invf, f, o, oo, gated, ws, b, e, na, f, b, ws, e, na, h, pown, inva)


def shards(
    tokens,
    row_starts,
    attn_gain,
    query_weight,
    key_weight,
    value_weight,
    gate_weight,
    rank_down,
    rank_up,
    rank_bias,
    group_gain,
    out_weight,
    feed_gain,
    feed_gate,
    feed_up,
    feed_down,
    cotangent,
):
    rows = tokens.shape[0]
    tiles = rows // TILE
    spans = rows // SPAN
    span_ids = lax.axis_index("seq") * spans + jnp.arange(spans, dtype=jnp.int32)
    resets = jnp.any((row_starts // SPAN)[None, :] == span_ids[:, None], axis=1).astype(F32)
    keep = jnp.pad((1.0 - resets).reshape(tiles, PER, 1), ((0, 0), (0, 8 - PER), (0, 0)))
    keep = jnp.broadcast_to(keep, (tiles, 8, 128))
    weights = (
        query_weight[0], key_weight[0], value_weight[0], gate_weight[0], jnp.swapaxes(rank_down[0], 0, 1), rank_up[0]
    )
    na, cg, inva, f, b, o, u, e, inc, dec = front(tokens, cotangent, keep, attn_gain, *weights, rank_bias)
    gated, oo, ws, h, invf, gsend, gown, psend, pown, stat, wide, gx = ffn(
        tokens, keep, inc, group_gain, feed_gain, out_weight[0], jnp.swapaxes(feed_gate[0], 0, 1),
        jnp.swapaxes(feed_up[0], 0, 1), feed_down[0], f, o, u, e, cg,
    )
    fixed = (
        keep, dec, stat, group_gain, attn_gain, feed_gain, out_weight[0],
    ) + weights
    grad_tokens, layer_out, units = back(fixed, wide, gsend, psend, tokens, cotangent, gx, gown, h, invf, f, o, oo, gated, ws, b, e, na, pown, inva)
    dfg, dfu, dfd, dq, dk, dv, dg, dwo, dr, dup, dag, dffg, db, dgg = finish(
        units, feed_gate.shape[2], wide.shape[0], lax.axis_size("seq")
    )
    dfg, dfu, dr = (jnp.swapaxes(a, 0, 1) for a in (dfg, dfu, dr))
    grads = (dag, dq[None], dk[None], dv[None], dg[None], dr[None], dup[None], db, dgg, dwo[None], dffg, dfg[None], dfu[None], dfd[None])
    return (layer_out, grad_tokens) + grads


def solution(mesh):
    placed = (
        P("seq", "head"),
        P(),
        P(),
        P(None, None, "head"),
        P(None, None, "head"),
        P(None, None, "head"),
        P(None, None, "head"),
        P(),
        P(None, None, "head"),
        P(None, "head"),
        P(),
        P(None, "head", None),
        P(),
        P(None, None, "head"),
        P(None, None, "head"),
        P(None, "head", None),
        P("seq", "head"),
    )
    return jax.shard_map(
        shards,
        mesh=mesh,
        in_specs=placed,
        out_specs=(
            P("seq", "head"),
            P("seq", "head"),
            P(None, "head"),
            P(None, None, "head"),
            P(None, None, "head"),
            P(None, None, "head"),
            P(None, None, "head"),
            P(),
            P(None, None, "head"),
            P(None, "head"),
            P(),
            P(None, "head", None),
            P(None, "head"),
            P(None, None, "head"),
            P(None, None, "head"),
            P(None, "head", None),
        ),
        check_vma=False,
    )
```

```python
import functools

import jax
import jax.numpy as jnp
from jax import lax
from jax.experimental import pallas as pl
from jax.experimental.pallas import tpu as pltpu
from jax.sharding import PartitionSpec as P

MODEL_WIDTH = 1024
HK = 128
HV = 256
SPAN = 64
RANK = 16
EPS = 1e-06
GATE_NORM = 16.0
TILE = 256
PER = TILE // SPAN
BLOCK = 256
AHEAD = 3
F32 = jnp.float32
BF16 = jnp.bfloat16
MESH = pl.DeviceIdType.MESH
VMEM_LIMIT = 62 * 1024 * 1024


def dot_nn(a, b):
    return jnp.dot(a, b, preferred_element_type=F32)


def dot_nt(a, b):
    return lax.dot_general(a, b, (((1,), (1,)), ((), ())), preferred_element_type=F32)


def dot_tn(a, b):
    return lax.dot_general(a, b, (((0,), (0,)), ((), ())), preferred_element_type=F32)


def peers():
    me = lax.axis_index("head")
    mate = me + 1 - 2 * lax.rem(me, 2)
    cross = lax.rem(me + 2, 4)
    far = cross + 1 - 2 * lax.rem(cross, 2)
    return me, mate, cross, far


def greet_head():
    _, mate, cross, far = peers()
    barrier = pltpu.get_barrier_semaphore()
    for other in (mate, cross, far):
        pl.semaphore_signal(barrier, inc=1, device_id={"head": other}, device_id_type=MESH)


def greet_seq(count):
    place = lax.axis_index("seq")
    barrier = pltpu.get_barrier_semaphore()

    def one(step, carry):
        other = lax.rem(place + step, count)
        pl.semaphore_signal(barrier, inc=1, device_id={"seq": other}, device_id_type=MESH)
        return carry

    lax.fori_loop(1, count, one, 0)


def to_head(src, dst, send, recv, other):
    return pltpu.make_async_remote_copy(
        src_ref=src, dst_ref=dst, send_sem=send, recv_sem=recv,
        device_id={"head": other}, device_id_type=MESH,
    )


def to_seq(src, dst, send, recv, other):
    return pltpu.make_async_remote_copy(
        src_ref=src, dst_ref=dst, send_sem=send, recv_sem=recv,
        device_id={"seq": other}, device_id_type=MESH,
    )


def span_masks(rows, cols):
    r = lax.broadcasted_iota(jnp.int32, (rows, cols), 0)
    c = lax.broadcasted_iota(jnp.int32, (rows, cols), 1)
    same = (r >> 6) == (c >> 6)
    return same & (r >= c), same


def three(x):
    a = x.astype(BF16)
    rest = x - a.astype(F32)
    b = rest.astype(BF16)
    c = (rest - b.astype(F32)).astype(BF16)
    return jnp.concatenate([a, b, c], axis=1)


def fold(x):
    w = x.shape[1] // 3
    return x[:, :w] + x[:, w : 2 * w] + x[:, 2 * w :]


def front_kernel(
    tiles, count,
    x_ref, c_ref, keep_ref, gain_ref, wq, wk, wv, wg, wr, rup, bias_ref,
    na_o, cg_o, inv_o, f_o, b_o, o_o, u_o, e_o, in_o, d_o,
    grid_buf, wcat, tri, state, decay, sbuf, rbuf, sems, esend, erecv,
):
    i = pl.program_id(0)
    me, mate, cross, far = peers()
    place = lax.axis_index("seq")
    total = 2 * tiles

    def own_mate(m):
        return to_head(grid_buf.at[m, me], grid_buf.at[m, me], sems.at[0, m], sems.at[1, m], mate)

    def own_cross(m):
        return to_head(grid_buf.at[m, me], grid_buf.at[m, me], sems.at[2, m], sems.at[3, m], cross)

    def onward(m):
        return to_head(grid_buf.at[m, cross], grid_buf.at[m, cross], sems.at[4, m], sems.at[5, m], mate)

    @pl.when(i == 0)
    def _():
        greet_head()
        greet_seq(count)

        def own(m, carry):
            rows = pl.ds(pl.multiple_of(m * TILE, TILE), TILE)
            grid_buf[m, me] = x_ref[rows, :]
            grid_buf[m + tiles, me] = c_ref[rows, :]
            return carry

        lax.fori_loop(0, tiles, own, 0)
        pl.semaphore_wait(pltpu.get_barrier_semaphore(), 3 + count - 1)
        for m in range(AHEAD):
            own_cross(m).start()
            own_mate(m).start()
        wcat[:, 0:128] = wq[...]
        wcat[:, 128:256] = wk[...]
        wcat[:, 256:512] = wv[...]
        wcat[:, 512:768] = wg[...]
        causal, same = span_masks(TILE, TILE)
        tri[0:TILE, :] = jnp.where(causal, 1.0, 0.0).astype(BF16)
        tri[TILE : 2 * TILE, :] = jnp.where(same, 1.0, 0.0).astype(BF16)
        state[...] = jnp.zeros_like(state)
        decay[...] = jnp.ones_like(decay)

    @pl.when(i < total)
    def _():
        own_cross(i).wait_recv()
        onward(i).start()

    @pl.when(i + AHEAD < total)
    def _():
        own_cross(i + AHEAD).start()
        own_mate(i + AHEAD).start()

    @pl.when(i >= 1)
    def _():
        own_mate(i - 1).wait_recv()
        onward(i - 1).wait_recv()

    @pl.when((i >= 1) & (i <= tiles))
    def _():
        m = i - 1
        squares = jnp.zeros((TILE, 1), F32)
        for j in range(4):
            xj = grid_buf[m, j].astype(F32)
            squares = squares + jnp.sum(xj * xj, axis=1, keepdims=True)
        inv = lax.rsqrt(squares / MODEL_WIDTH + EPS)
        inv_o[...] = jnp.broadcast_to(inv, (TILE, 128))
        for j in range(4):
            cols = slice(j * BLOCK, (j + 1) * BLOCK)
            xj = grid_buf[m, j].astype(F32)
            na_o[:, cols] = (xj * inv * gain_ref[:, cols].astype(F32)).astype(BF16)
        proj = dot_nn(na_o[...], wcat[...])
        q = proj[:, 0:128]
        k = proj[:, 128:256]
        v = proj[:, 256:512].astype(BF16)
        o_o[:, 0:256] = proj[:, 512:768]
        lr = dot_nt(na_o[...], wr[...]).astype(BF16)
        z = dot_nn(lr, rup[...]) + bias_ref[...].astype(F32)
        g = (jnp.minimum(z, 0.0) - jnp.log1p(jnp.exp(-jnp.abs(z)))) / GATE_NORM
        sums = fold(dot_nn(tri[...], three(g)))
        b = sums[0:TILE]
        e = sums[TILE : 2 * TILE]
        fq = (HK ** (-0.5)) * jnp.exp(b - e)
        fk = jnp.exp(e - b)
        qf = q * fq
        kf = k * fk
        f_o[:, 0:128] = qf
        f_o[:, 128:256] = kf
        f_o[:, 256:384] = fq
        f_o[:, 384:512] = fk
        f_o[:, 512:640] = jax.nn.sigmoid(-z) / GATE_NORM
        qd = qf.astype(BF16)
        kd = kf.astype(BF16)
        causal, _ = span_masks(TILE, TILE)
        scores = jnp.where(causal, dot_nt(qd, kd), 0.0).astype(BF16)
        b_o[:, 0:256] = v
        b_o[:, 256:512] = scores
        b_o[:, 512 : 512 + RANK] = lr
        o_o[:, 256:512] = dot_nn(scores, v)
        for c in range(PER):
            rows = slice(c * SPAN, (c + 1) * SPAN)
            update = dot_tn(v[rows], kd[rows])
            u_o[c] = update
            ee = jnp.exp(e[c * SPAN : c * SPAN + 1])
            e_o[0, c : c + 1, :] = ee
            through = keep_ref[m, c : c + 1, :] * ee
            state[...] = through * state[...] + update
            decay[...] = through * decay[...]

    @pl.when(i == tiles)
    def _():
        d_o[...] = decay[...]
        sbuf[0:HV, :] = state[...].astype(BF16)
        d = decay[...]
        hi = d.astype(BF16).astype(F32)
        first = lax.broadcasted_iota(jnp.int32, (16, 128), 0) < 8
        both = jnp.where(first, jnp.concatenate([hi, hi], axis=0), jnp.concatenate([d - hi, d - hi], axis=0))
        sbuf[HV : HV + 16, :] = both.astype(BF16)

        def send(p, carry):
            to_seq(sbuf, rbuf.at[place], esend.at[p], erecv.at[place], p).start()
            return carry

        lax.fori_loop(place + 1, count, send, 0)

    @pl.when(i > tiles)
    def _():
        m = i - 1
        for j in range(4):
            cg_o[:, j * BLOCK : (j + 1) * BLOCK] = grid_buf[m, j]

    @pl.when(i == total)
    def _():
        in_o[...] = jnp.zeros_like(in_o)

        def join(p, carry):
            to_seq(sbuf, rbuf.at[p], esend.at[p], erecv.at[p], place).wait_recv()
            got = rbuf[p].astype(F32)
            d = got[HV : HV + 1] + got[HV + 8 : HV + 9]
            in_o[...] = got[0:HV] + d * in_o[...]
            return carry

        lax.fori_loop(0, place, join, 0)

        def sent(p, carry):
            to_seq(sbuf, rbuf.at[place], esend.at[p], erecv.at[place], p).wait_send()
            return carry

        lax.fori_loop(place + 1, count, sent, 0)

        def out(m, carry):
            own_cross(m).wait_send()
            own_mate(m).wait_send()
            onward(m).wait_send()
            return carry

        lax.fori_loop(0, total, out, 0)


def whole(shape):
    zeros = (0,) * len(shape)
    return pl.BlockSpec(shape, lambda i: zeros, pipeline_mode=pl.Buffered(1))


def front(x, cot, keep, gain, wq, wk, wv, wg, wr, rup, bias):
    rows = x.shape[0]
    tiles = rows // TILE
    count = lax.axis_size("seq")

    def tile(shape, lag, axis0=True):
        rest = (0,) * (len(shape) - 1)
        return pl.BlockSpec(shape, lambda i: (jnp.clip(i - lag, 0, tiles - 1),) + rest)

    ins = (x, cot, keep, gain, wq, wk, wv, wg, wr, rup, bias)
    outs = [
        ((rows, MODEL_WIDTH), BF16, tile((TILE, MODEL_WIDTH), 1)),
        ((rows, MODEL_WIDTH), BF16, tile((TILE, MODEL_WIDTH), 1 + tiles)),
        ((rows, 128), F32, tile((TILE, 128), 1)),
        ((rows, 640), F32, tile((TILE, 640), 1)),
        ((rows, 640), BF16, tile((TILE, 640), 1)),
        ((rows, 512), F32, tile((TILE, 512), 1)),
        ((rows // SPAN, HV, HK), F32, tile((PER, HV, HK), 1)),
        ((tiles, 8, 128), F32, tile((1, 8, 128), 1)),
        ((HV, HK), F32, whole((HV, HK))),
        ((8, 128), F32, whole((8, 128))),
    ]
    return pl.pallas_call(
        functools.partial(front_kernel, tiles, count),
        grid=(2 * tiles + 1,),
        out_shape=[jax.ShapeDtypeStruct(s, d) for s, d, _ in outs],
        in_specs=[whole(a.shape) for a in ins],
        out_specs=[s for _, _, s in outs],
        scratch_shapes=[
            pltpu.VMEM((2 * tiles, 4, TILE, BLOCK), BF16),
            pltpu.VMEM((MODEL_WIDTH, 768), BF16),
            pltpu.VMEM((2 * TILE, TILE), BF16),
            pltpu.VMEM((HV, HK), F32),
            pltpu.VMEM((8, 128), F32),
            pltpu.VMEM((HV + 16, HK), BF16),
            pltpu.VMEM((count, HV + 16, HK), BF16),
            pltpu.SemaphoreType.DMA((6, 2 * tiles)),
            pltpu.SemaphoreType.DMA((count,)),
            pltpu.SemaphoreType.DMA((count,)),
        ],
        compiler_params=pltpu.CompilerParams(
            collective_id=1, has_side_effects=True, vmem_limit_bytes=VMEM_LIMIT,
            dimension_semantics=("arbitrary",),
        ),
        name="front",
    )(*ins)


def tile_spec(tiles, shape, lag, back=False, col=0):
    rest = (0,) * (len(shape) - 2) + (col,)

    def index(i):
        t = jnp.clip(i - lag, 0, tiles - 1)
        return ((tiles - 1 - t) if back else t,) + rest

    return pl.BlockSpec(shape, index)


def up_to(n, step):
    return (n + step - 1) // step * step


def ffn_kernel(
    tiles,
    x_ref, keep_ref, in_ref, gg_ref, gain_ref, wout, wfg_in, wfu_in, wfd_in,
    f_ref, o_ref, u_ref, e_ref, cg_ref,
    gated_o, oo_o, ws_o, h_o, inv_o, gsend_o, gown_o, psend_o, pown_o, stat_o, wide_o, gx_o,
    state, pa, pp, pg, ma, mp, mg, sc, rc, own, hg, nf_s, acc, wfg, wfu, wfd, st_s, st_r, gxs, gxr,
    asem, psem, gsem, csem, hsem, tsem, wsem, xsem,
):
    i = pl.program_id(0)
    me, mate, cross, far = peers()
    last = tiles - 1
    hidden = wfg.shape[0]

    def pair(buf, got, sem, t, which):
        block = mate if which == 0 else far
        return to_head(buf.at[t, block], got.at[t, which], sem.at[2 * which, t], sem.at[2 * which + 1, t], mate)

    def over(t):
        return to_head(sc.at[t], rc.at[t], csem.at[0, t], csem.at[1, t], cross)

    def own_mate(t):
        return to_head(hg.at[t, me], hg.at[t, me], hsem.at[0, t], hsem.at[1, t], mate)

    def own_cross(t):
        return to_head(hg.at[t, me], hg.at[t, me], hsem.at[2, t], hsem.at[3, t], cross)

    def onward(t):
        return to_head(hg.at[t, cross], hg.at[t, cross], hsem.at[4, t], hsem.at[5, t], mate)

    some = gxs.shape[0]

    def early(t):
        return to_head(gxs.at[t], gxr.at[t], xsem.at[0, t], xsem.at[1, t], cross)

    def stats(n, other):
        return to_head(st_s, st_r.at[n], tsem.at[0, n], tsem.at[1, n], other)

    fetches = [
        pltpu.make_async_copy(src, dst, wsem.at[n])
        for n, (src, dst) in enumerate(((wfg_in, wfg), (wfu_in, wfu), (wfd_in, wfd)))
    ]

    @pl.when(i == 4)
    def _():
        for fetch in fetches:
            fetch.wait()

    @pl.when(i == 0)
    def _():
        for fetch in fetches:
            fetch.start()
        greet_head()
        state[...] = in_ref[...]
        acc[...] = jnp.zeros_like(acc)
        st_s[...] = jnp.zeros_like(st_s)
        pl.semaphore_wait(pltpu.get_barrier_semaphore(), 3)

    @pl.when((i >= 6) & (i - 6 <= last))
    def _():
        t = i - 6
        own_mate(t).wait_recv()
        onward(t).wait_recv()
        squares = jnp.zeros((TILE, 1), F32)
        for j in range(4):
            hj = hg[t, j].astype(F32)
            squares = squares + jnp.sum(hj * hj, axis=1, keepdims=True)
        inv = lax.rsqrt(squares / MODEL_WIDTH + EPS)
        inv_o[...] = jnp.broadcast_to(inv, (TILE, 128))
        for j in range(4):
            cols = slice(j * BLOCK, (j + 1) * BLOCK)
            nf_s[:, cols] = (hg[t, j].astype(F32) * inv * gain_ref[:, cols].astype(F32)).astype(BF16)
        nf = nf_s[...]
        fg = dot_nt(nf, wfg[...])
        fu = dot_nt(nf, wfu[...])
        sig = jax.nn.sigmoid(fg)
        silu = fg * sig
        act = (silu * fu).astype(BF16)
        cg = cg_ref[...]
        for j in range(4):
            pp[t, j] = dot_nn(act, wfd[:, j * BLOCK : (j + 1) * BLOCK]).astype(BF16)
        for which in range(2):
            pair(pp, mp, psem, t, which).start()
        gact = dot_nt(cg, wfd[...])
        gfg = (gact * fu * (sig * (1.0 + fg * (1.0 - sig)))).astype(BF16)
        gfu = (gact * silu).astype(BF16)
        stat = jnp.zeros((TILE, 1), F32)
        for j in range(4):
            rows = slice(j * BLOCK, (j + 1) * BLOCK)
            gj = dot_nn(gfg, wfg[:, rows]) + dot_nn(gfu, wfu[:, rows])
            stat = stat + jnp.sum(gj * nf_s[:, rows].astype(F32), axis=1, keepdims=True)
            pg[t, j] = gj.astype(BF16)
        for which in range(2):
            pair(pg, mg, gsem, t, which).start()
        st_s[pl.ds(t, 1), :] = jnp.broadcast_to(stat, (TILE, 128)).T[0:1, :]
        acc[0:hidden, :] += dot_tn(gfg, nf)
        acc[hidden : 2 * hidden, :] += dot_tn(gfu, nf)
        acc[2 * hidden : 3 * hidden, :] += dot_tn(act, cg)

    @pl.when((i >= 5) & (i - 5 <= last))
    def _():
        t = i - 5
        own_cross(t).wait_recv()
        onward(t).start()

    @pl.when((i >= 3) & (i - 3 <= last))
    def _():
        t = i - 3
        over(t).wait_recv()
        rows = pl.ds(pl.multiple_of(t * TILE, TILE), TILE)
        h = x_ref[rows, :].astype(F32) + (own[lax.rem(t, 4)] + rc[t].astype(F32))
        h_o[...] = h
        hg[t, me] = h.astype(BF16)
        own_cross(t).start()
        own_mate(t).start()

    @pl.when((i >= 1) & (i - 1 <= last))
    def _():
        t = i - 1
        pair(pa, ma, asem, t, 0).wait_recv()
        pair(pa, ma, asem, t, 1).wait_recv()
        sc[t] = (pa[t, cross].astype(F32) + ma[t, 1].astype(F32)).astype(BF16)
        over(t).start()
        own[lax.rem(t, 4)] = pa[t, me].astype(F32) + ma[t, 0].astype(F32)

    @pl.when(i <= last)
    def _():
        t = i
        for c in range(PER):
            rows = slice(c * SPAN, (c + 1) * SPAN)
            scaled = (keep_ref[t, c : c + 1, :] * e_ref[0, c : c + 1, :]) * state[...]
            low = scaled.astype(BF16)
            ws_o[c] = low
            state[...] = scaled + u_ref[c]
            oo_o[rows, :] = o_ref[rows, 256:512] + dot_nt(f_ref[rows, :].astype(BF16), low)
        o = oo_o[...]
        gz = o_ref[:, 0:256]
        inv = lax.rsqrt(jnp.mean(o * o, axis=1, keepdims=True) + EPS)
        gated = (o * inv * gg_ref[...].astype(F32) * (gz * jax.nn.sigmoid(gz))).astype(BF16)
        gated_o[...] = gated
        for j in range(4):
            pa[t, j] = dot_nn(gated, wout[:, j * BLOCK : (j + 1) * BLOCK]).astype(BF16)
        pair(pa, ma, asem, t, 1).start()
        pair(pa, ma, asem, t, 0).start()

    @pl.when((i >= 7) & (i - 7 <= last))
    def _():
        t = i - 7
        for which in range(2):
            pair(pp, mp, psem, t, which).wait_recv()
            pair(pg, mg, gsem, t, which).wait_recv()
        psend_o[...] = (pp[t, cross].astype(F32) + mp[t, 1].astype(F32)).astype(BF16)
        pown_o[...] = pp[t, me].astype(F32) + mp[t, 0].astype(F32)
        gs = (pg[t, cross].astype(F32) + mg[t, 1].astype(F32)).astype(BF16)
        gsend_o[...] = gs

        @pl.when(t < some)
        def _():
            gxs[t] = gs

        gown_o[...] = pg[t, me].astype(F32) + mg[t, 0].astype(F32)

    @pl.when(i == some + 6)
    def _():
        for t in range(some):
            early(t).start()

    @pl.when(i == last + 6)
    def _():
        for n, other in enumerate((mate, cross, far)):
            stats(n, other).start()

    @pl.when(i == last + 7)
    def _():
        used = 3 * hidden // 16

        def unit(r, carry):
            wide_o[r] = acc[pl.ds(pl.multiple_of(r * 16, 16), 16), :].astype(BF16)
            return carry

        lax.fori_loop(0, used, unit, 0)
        for n, other in enumerate((mate, cross, far)):
            stats(n, other).wait()
        for t in range(some):
            early(t).wait()
            gx_o[t * TILE : (t + 1) * TILE, :] = gxr[t]
        stat_o[...] = (st_s[...] + st_r[0]) + (st_r[1] + st_r[2])

        def out(t, carry):
            for which in range(2):
                pair(pa, ma, asem, t, which).wait_send()
                pair(pp, mp, psem, t, which).wait_send()
                pair(pg, mg, gsem, t, which).wait_send()
            over(t).wait_send()
            own_cross(t).wait_send()
            own_mate(t).wait_send()
            onward(t).wait_send()
            return carry

        lax.fori_loop(0, tiles, out, 0)


def ffn(x, keep, inc, gg, gain, wout, wfg, wfu, wfd, f, o, u, e, cg):
    rows = x.shape[0]
    tiles = rows // TILE
    hidden, width = wfg.shape
    units = 3 * hidden // 16
    some = tiles - 3
    assert 3 < tiles <= 8 and hidden % 16 == 0
    ts = functools.partial(tile_spec, tiles)
    ins = (x, keep, inc, gg, gain, wout)
    outs = [
        ((rows, BLOCK), BF16, ts((TILE, BLOCK), 0)),
        ((rows, HV), F32, ts((TILE, HV), 0)),
        ((rows // SPAN, HV, HK), BF16, ts((PER, HV, HK), 0)),
        ((rows, BLOCK), F32, ts((TILE, BLOCK), 3)),
        ((rows, 128), F32, ts((TILE, 128), 6)),
        ((rows, BLOCK), BF16, ts((TILE, BLOCK), 7)),
        ((rows, BLOCK), F32, ts((TILE, BLOCK), 7)),
        ((rows, BLOCK), BF16, ts((TILE, BLOCK), 7)),
        ((rows, BLOCK), F32, ts((TILE, BLOCK), 7)),
        ((8, TILE), F32, whole((8, TILE))),
        ((units, 16, width), BF16, whole((units, 16, width))),
        ((some * TILE, BLOCK), BF16, whole((some * TILE, BLOCK))),
    ]
    tiled = lambda n: pltpu.VMEM((tiles, n, TILE, BLOCK), BF16)
    return pl.pallas_call(
        functools.partial(ffn_kernel, tiles),
        grid=(tiles + 7,),
        out_shape=[jax.ShapeDtypeStruct(s, d) for s, d, _ in outs],
        in_specs=[whole(a.shape) for a in ins]
        + [pl.BlockSpec(memory_space=pl.ANY)] * 3
        + [
            ts((TILE, 128), 0), ts((TILE, 512), 0), ts((PER, HV, HK), 0), ts((1, 8, 128), 0),
            ts((TILE, MODEL_WIDTH), 6),
        ],
        out_specs=[s for _, _, s in outs],
        scratch_shapes=[
            pltpu.VMEM((HV, HK), F32),
            tiled(4), tiled(4), tiled(4), tiled(2), tiled(2), tiled(2),
            pltpu.VMEM((tiles, TILE, BLOCK), BF16),
            pltpu.VMEM((tiles, TILE, BLOCK), BF16),
            pltpu.VMEM((4, TILE, BLOCK), F32),
            tiled(4),
            pltpu.VMEM((TILE, MODEL_WIDTH), BF16),
            pltpu.VMEM((3 * hidden, width), F32),
            pltpu.VMEM((hidden, width), BF16),
            pltpu.VMEM((hidden, width), BF16),
            pltpu.VMEM((hidden, width), BF16),
            pltpu.VMEM((8, TILE), F32),
            pltpu.VMEM((3, 8, TILE), F32),
            pltpu.VMEM((some, TILE, BLOCK), BF16),
            pltpu.VMEM((some, TILE, BLOCK), BF16),
            pltpu.SemaphoreType.DMA((4, tiles)),
            pltpu.SemaphoreType.DMA((4, tiles)),
            pltpu.SemaphoreType.DMA((4, tiles)),
            pltpu.SemaphoreType.DMA((2, tiles)),
            pltpu.SemaphoreType.DMA((6, tiles)),
            pltpu.SemaphoreType.DMA((2, 3)),
            pltpu.SemaphoreType.DMA((3,)),
            pltpu.SemaphoreType.DMA((2, some)),
        ],
        compiler_params=pltpu.CompilerParams(
            collective_id=2, has_side_effects=True, vmem_limit_bytes=VMEM_LIMIT,
            dimension_semantics=("arbitrary",),
        ),
        name="ffn",
    )(*ins, wfg, wfu, wfd, f, o, u, e, cg)


LAGS = (2, 2, 2)
CYCLE = 5
WAIT = 2


def levels(count):
    bits = count.bit_length() - 1
    assert 1 << bits == count
    return bits


def folds(count):
    return count == 8


class Sum:
    def __init__(self, count, sources, dest, segments, scratch):
        self.count = count
        self.bits = levels(count)
        self.folds = folds(count)
        self.sources = sources
        self.dest = dest
        self.segments = segments
        self.got = scratch[: self.bits]
        self.ring, self.side_sum, self.line_sum = scratch[self.bits : self.bits + 3]
        self.sems, self.lsem = scratch[self.bits + 3 :]

    def slot(self, k):
        if not self.folds:
            return k
        odd = lax.rem(lax.rem(k, CYCLE), 2)
        return ((CYCLE + 1) // 2 - odd) * lax.div(k, CYCLE) + lax.div(lax.rem(k, CYCLE), 2)

    def where(self, k, level):
        place = lax.axis_index("seq")
        turn = 1 if self.folds else lax.div(lax.rem(k, 4), 3)
        start = 0
        for step in range(level + 1):
            stride = 1 << step
            if step < 2:
                stride = stride + turn * (3 - 2 * stride)
            bit = lax.rem(lax.div(place, stride), 2)
            if step == level:
                return bit, place + stride * (1 - 2 * bit), start
            start = start + bit * (self.count >> (step + 1))

    def own(self, k):
        bit, _, _ = self.where(k, 0)
        half = self.count >> 1
        return pltpu.make_async_copy(
            self.sources[0](k, bit * half, half), self.dest(k, bit * half, half), self.lsem.at[k]
        )

    def scatter(self, k, level, kind):
        bit, partner, start = self.where(k, level)
        half = self.count >> (level + 1)
        if level == 0:
            src = self.sources[kind](k, start + (1 - bit) * half, half)
        else:
            src = self.got[level - 1].at[self.slot(k), pl.ds((1 - bit) * half, half)]
        return to_seq(src, self.got[level].at[self.slot(k)], self.sems.at[0, level, k], self.sems.at[1, level, k], partner)

    def gather(self, k, level):
        bit, partner, start = self.where(k, level)
        half = self.count >> (level + 1)
        mine = start + bit * half
        ref = self.dest(k, mine, half)
        return to_seq(ref, ref, self.sems.at[2, level, k], self.sems.at[3, level, k], partner)

    def gathered(self, k, level):
        bit, partner, start = self.where(k, level)
        half = self.count >> (level + 1)
        ref = self.dest(k, start + (1 - bit) * half, half)
        return to_seq(ref, ref, self.sems.at[2, level, k], self.sems.at[3, level, k], partner)

    def begin(self, k, kind):
        self.scatter(k, 0, kind).start()
        if kind == 0:
            self.own(k).start()

    def add(self, k, kind, level):
        bit, _, start = self.where(k, level)
        half = self.count >> (level + 1)
        self.scatter(k, level, kind).wait_recv()
        if level == 0 and kind == 0:
            self.own(k).wait()
            mine = self.dest(k, bit * half, half)[...]
        elif level == 0:
            mine = self.sources[kind](k, bit * half, half)[...]
        else:
            mine = self.got[level - 1][self.slot(k), pl.ds(bit * half, half)]
        total = (self.got[level][self.slot(k)].astype(F32) + mine.astype(F32)).astype(BF16)
        if level + 1 < self.bits:
            self.got[level][self.slot(k)] = total
            self.scatter(k, level + 1, kind).start()
        else:
            self.dest(k, start + bit * half, half)[...] = total
            self.gather(k, level).start()

    def pass_on(self, k, kind, level):
        self.gathered(k, level).wait_recv()
        if level > 0:
            self.gather(k, level - 1).start()

    def spot(self):
        place = lax.axis_index("seq")
        side = lax.rem(place, 2)
        z = lax.div(place, 2)
        low = lax.rem(z, 2)
        end = low == lax.div(z, 2)
        return side, place + 1 - 2 * side, place + 2 * (1 - 2 * low), 2 * (3 - z) + side, end

    def half_of(self, k, which):
        half = self.count >> 1
        return self.dest(k, which * half, half)

    def fold_own(self, k):
        half = self.count >> 1
        return pltpu.make_async_copy(
            self.sources[0](k, self.spot()[0] * half, half), self.ring.at[lax.rem(k, 4)], self.lsem.at[k]
        )

    def fold_side(self, k, kind):
        side, twin, _, _, _ = self.spot()
        half = self.count >> 1
        src = self.sources[kind](k, (1 - side) * half, half)
        return to_seq(src, self.side_sum.at[self.slot(k)], self.sems.at[0, 0, k], self.sems.at[1, 0, k], twin)

    def fold_in(self, k):
        n = self.slot(k)
        return to_seq(
            self.side_sum.at[n], self.line_sum.at[n], self.sems.at[0, 1, k], self.sems.at[1, 1, k], self.spot()[2]
        )

    def fold_cross(self, k):
        side, _, _, other, _ = self.spot()
        return to_seq(
            self.line_sum.at[self.slot(k)], self.half_of(k, side), self.sems.at[0, 2, k], self.sems.at[1, 2, k], other
        )

    def fold_out(self, k):
        side, _, across, _, _ = self.spot()
        ref = self.half_of(k, side)
        return to_seq(ref, ref, self.sems.at[2, 1, k], self.sems.at[3, 1, k], across)

    def fold_back(self, k, mine):
        side, twin, _, _, _ = self.spot()
        ref = self.half_of(k, side if mine else 1 - side)
        return to_seq(ref, ref, self.sems.at[2, 0, k], self.sems.at[3, 0, k], twin)

    def fold_begin(self, k, kind):
        self.fold_side(k, kind).start()
        if kind == 0:
            self.fold_own(k).start()

    def fold_1(self, k, kind):
        side, _, _, _, end = self.spot()
        half = self.count >> 1
        n = self.slot(k)
        self.fold_side(k, kind).wait_recv()
        if kind == 0:
            self.fold_own(k).wait()
            mine = self.ring[lax.rem(k, 4)]
        else:
            mine = self.sources[kind](k, side * half, half)[...]
        self.side_sum[n] = (self.side_sum[n].astype(F32) + mine.astype(F32)).astype(BF16)

        @pl.when(end)
        def _():
            self.fold_in(k).start()

    def fold_2(self, k, kind):
        n = self.slot(k)

        @pl.when(jnp.logical_not(self.spot()[4]))
        def _():
            self.fold_in(k).wait_recv()
            self.line_sum[n] = (self.line_sum[n].astype(F32) + self.side_sum[n].astype(F32)).astype(BF16)
            self.fold_cross(k).start()

    def fold_3(self, k, kind):
        side, _, _, _, end = self.spot()

        @pl.when(jnp.logical_not(end))
        def _():
            self.fold_cross(k).wait_recv()
            ref = self.half_of(k, side)
            ref[...] = (ref[...].astype(F32) + self.line_sum[self.slot(k)].astype(F32)).astype(BF16)
            self.fold_out(k).start()
            self.fold_back(k, True).start()

    def fold_4(self, k, kind):
        end = self.spot()[4]

        @pl.when(end)
        def _():
            self.fold_out(k).wait_recv()
            self.fold_back(k, True).start()

        @pl.when(jnp.logical_not(end))
        def _():
            self.fold_back(k, False).wait_recv()

    def fold_5(self, k, kind):
        @pl.when(self.spot()[4])
        def _():
            self.fold_back(k, False).wait_recv()

    def at(self, i, stage, body, fold):
        for kind, (low, high, gap) in enumerate(self.segments):
            k = i - gap - LAGS[kind] * stage
            here = (k >= low) & (k < high)
            if not self.folds:

                @pl.when(here)
                def _(kind=kind, k=k):
                    body(k, kind)

                continue
            odd = lax.rem(lax.rem(jnp.maximum(k, 0), CYCLE), 2) == 1

            @pl.when(here & odd)
            def _(kind=kind, k=k):
                body(k, kind)

            if fold is not None:

                @pl.when(here & jnp.logical_not(odd))
                def _(kind=kind, k=k):
                    fold(k, kind)

    def step(self, i):
        stages = []
        for level in range(self.bits):
            stages.append(functools.partial(self.add, level=level))
        for level in range(self.bits - 1, -1, -1):
            stages.append(functools.partial(self.pass_on, level=level))
        folded = [self.fold_1, self.fold_2, self.fold_3, self.fold_4, self.fold_5]
        folded = folded + [None] * (len(stages) - len(folded))
        for s in range(len(stages) - 1, -1, -1):
            self.at(i, s + 1, stages[s], folded[s])
        self.at(i, 0, self.begin, self.fold_begin)

    def finish(self):
        def halving(k, kind):
            for level in range(self.bits):
                self.scatter(k, level, kind).wait_send()
                self.gather(k, level).wait_send()

        def folding(k, kind):
            end = self.spot()[4]
            self.fold_side(k, kind).wait_send()
            self.fold_back(k, True).wait_send()

            @pl.when(end)
            def _():
                self.fold_in(k).wait_send()

            @pl.when(jnp.logical_not(end))
            def _():
                self.fold_cross(k).wait_send()
                self.fold_out(k).wait_send()

        def one(kind, k, carry):
            if not self.folds:
                halving(k, kind)
                return carry
            odd = lax.rem(lax.rem(k, CYCLE), 2) == 1

            @pl.when(odd)
            def _():
                halving(k, kind)

            @pl.when(jnp.logical_not(odd))
            def _():
                folding(k, kind)

            return carry

        for kind, (low, high, _) in enumerate(self.segments):
            lax.fori_loop(low, high, functools.partial(one, kind), 0)

    @staticmethod
    def scratch(count, parts, first, unit):
        bits = levels(count)
        odd = parts
        even = 1
        half = 16
        if folds(count):
            odd = sum(1 for k in range(parts) if k % CYCLE % 2 == 1)
            even = parts - odd
            half = count // 2
        one = (1,) + unit if not folds(count) else (half,) + unit
        return [pltpu.VMEM((odd, count >> (level + 1)) + unit, BF16) for level in range(bits)] + [
            pltpu.VMEM((4 if folds(count) else 1,) + one, BF16),
            pltpu.VMEM((even,) + one, BF16),
            pltpu.VMEM((even,) + one, BF16),
            pltpu.SemaphoreType.DMA((4, bits, parts)),
            pltpu.SemaphoreType.DMA((first,)),
        ]


def plan(count, wide, tiles):
    second = tiles + 3 + WAIT
    a = wide // count
    b = a + 32 // count
    c = b + up_to(34 + wide % count, count) // count
    gap = max(0, second - a)
    late = max(gap, second + tiles - b, second + tiles + 3 - (c - 1))
    return (0, a, 0), (a, b, gap), (b, c, late)


def last_step(count, segments):
    latest = 0
    for kind, (low, high, gap) in enumerate(segments):
        for k in range(low, high):
            stages = 2 * levels(count) - (1 if folds(count) and k % CYCLE % 2 == 0 else 0)
            latest = max(latest, k + gap + stages * LAGS[kind])
    return latest


def finish_kernel(fg, fu, fd, first, second, tail, extra, gt_in, lo_in, dfg, dfu, dfd, dq, dk, dv, dg, dwo, dr, dup, dag, dffg, db, dgg, gt, lo):
    for src, dst in ((fg, dfg), (fu, dfu), (fd, dfd)):
        dst[...] = src[...].reshape(dst.shape).astype(F32)

    @pl.when(pl.program_id(0) == pl.num_programs(0) - 1)
    def _():
        tail_rows = extra.shape[0] * 16
        dfd[dfd.shape[0] - tail_rows :, :] = extra[...].reshape(tail_rows, -1).astype(F32)

    gt[...] = gt_in[...]
    lo[...] = lo_in[...]
    rows = first[...].reshape(-1, 512).astype(F32)
    dg[...] = rows[:, 0:256]
    dwo[...] = rows[:, 256:512].T
    rows = second[...].reshape(-1, 512).astype(F32)
    dq[...] = rows[:, 0:128]
    dk[...] = rows[:, 128:256]
    dv[...] = rows[:, 256:512]
    dr[...] = tail[0].astype(F32)
    last = tail[1].astype(F32)
    dup[...] = last[:, 0:128]
    dag[...] = last[0:1, 128:384]
    dffg[...] = last[1:2, 128:384]
    db[...] = last[3:4, 128:256]
    dgg[...] = last[2:3, 128:384]


def finish(units, gt, lo, hidden, wide, count):
    first = wide // count * count
    rest = wide % count
    width = units.shape[2]
    steps = 4
    per = hidden // 16 // steps
    assert per * steps * 16 == hidden and 0 < rest <= per
    rows = MODEL_WIDTH // steps
    wide_spec = lambda n: pl.BlockSpec((per, 16, width), lambda i: (i + n * steps, 0, 0))
    half_spec = lambda n: pl.BlockSpec(
        (pl.Element(rows // 16), pl.Element(16), pl.Element(512)),
        lambda i: (first + n + (i % 2) * (rows // 16), 0, (i // 2) * 512),
    )
    down = lambda r, c: ((r * steps, c), pl.BlockSpec((r, c), lambda i: (i, 0)))
    full = lambda r, c: ((r, c), pl.BlockSpec((r, c), lambda i: (0, 0)))
    outs = [
        down(per * 16, width), down(per * 16, width), down(per * 16, width),
        down(rows, 128), down(rows, 128), down(rows, 256), down(rows, 256),
        ((256, MODEL_WIDTH), pl.BlockSpec((256, rows), lambda i: (0, i))),
        full(RANK, MODEL_WIDTH), full(RANK, 128), full(1, 256), full(1, 256), full(1, 128), full(1, 256),
    ]
    same = pl.BlockSpec((gt.shape[0] // steps, gt.shape[1]), lambda i: (i, 0))
    return pl.pallas_call(
        finish_kernel,
        grid=(steps,),
        out_shape=[jax.ShapeDtypeStruct(s, F32) for s, _ in outs]
        + [jax.ShapeDtypeStruct(gt.shape, F32), jax.ShapeDtypeStruct(lo.shape, BF16)],
        in_specs=[
            wide_spec(0), wide_spec(1), wide_spec(2),
            half_spec(0), half_spec(32),
            pl.BlockSpec((pl.Element(2), pl.Element(16), pl.Element(width)), lambda i: (first + 64, 0, 0)),
            pl.BlockSpec((pl.Element(rest), pl.Element(16), pl.Element(width)), lambda i: (first + 66, 0, 0)),
            same, same,
        ],
        out_specs=[s for _, s in outs] + [same, same],
        compiler_params=pltpu.CompilerParams(
            vmem_limit_bytes=VMEM_LIMIT, dimension_semantics=("arbitrary",)
        ),
        name="finish",
    )(units, units, units, units, units, units, units, gt, lo)


def back_kernel(
    tiles, count, segments,
    keep_ref, d_ref, stat_ref, gg_ref, again, fgain, wout, wq, wk, wv, wg, wr, rup,
    wide_in, gsend, psend, x_ref, c_ref, gx, gown, h1, invf, f1, gz_ref, oo_ref, gated, ws1, b1, e1,
    na1, f2, b2, ws2, e2, na, h2, pown, inva,
    gt_o, lo_o, units_o,
    tri, rg, gh, gb, gzs, gw, gqd, gkd, gv, state, sbuf, tbuf, hbuf, xbuf, ybuf, rbuf,
    gcat, mn, sc, rc, own, st_s, st_r, both, joint, small, held, wide_o, few, lot,
    gsem, psem, hsem, nsem, csem, tsem, esend, erecv, xsem, wsem, jsem, *rest,
):
    i = pl.program_id(0)
    me, mate, cross, far = peers()
    place = lax.axis_index("seq")
    last = tiles - 1
    second = tiles + 3 + WAIT

    some = tiles - 3

    def rows_of(t):
        return pl.ds(pl.multiple_of(t * TILE, TILE), TILE)

    def own_cols(ref):
        return ref[:, pl.ds(pl.multiple_of(me * BLOCK, BLOCK), BLOCK)].astype(F32)

    def grads(t):
        return to_head(gsend.at[rows_of(t)], rg.at[t], gsem.at[0, t], gsem.at[1, t], cross)

    def feeds(t):
        return to_head(psend.at[rows_of(t)], rg.at[t], psem.at[0, t], psem.at[1, t], cross)

    def own_mate(t):
        return to_head(gb.at[t, me], gb.at[t, me], hsem.at[0, t], hsem.at[1, t], mate)

    def own_cross(t):
        return to_head(gb.at[t, me], gb.at[t, me], hsem.at[2, t], hsem.at[3, t], cross)

    def onward(t):
        return to_head(gb.at[t, cross], gb.at[t, cross], hsem.at[4, t], hsem.at[5, t], mate)

    def pair(t, which):
        block = mate if which == 0 else far
        return to_head(gb.at[t, block], mn.at[t, which], nsem.at[2 * which, t], nsem.at[2 * which + 1, t], mate)

    def over(t):
        return to_head(sc.at[t], rc.at[t], csem.at[0, t], csem.at[1, t], cross)

    def stats(t, n, other):
        return to_head(st_s.at[t], st_r.at[t, n], tsem.at[0, n, t], tsem.at[1, n, t], other)

    first = wide_in.shape[0] // count
    spare = wide_in.shape[0] - first * count
    parts = wide_o.shape[0] // count
    ready = second + tiles
    feed = ready + 4

    def early(k, start, n):
        return wide_in.at[pl.ds(k * count + start, n)]

    def middle(k, start, n):
        return few.at[pl.ds((k - segments[1][0]) * count + start, n)]

    def late(k, start, n):
        return lot.at[pl.ds((k - segments[2][0]) * count + start, n)]

    def place_of(k, start, n):
        return wide_o.at[pl.ds(k * count + start, n)]

    wide_sum = Sum(count, (early, middle, late), place_of, segments, rest)

    @pl.when(i == 0)
    def _():
        greet_head()
        greet_seq(count)
        pl.semaphore_wait(pltpu.get_barrier_semaphore(), 3 + count - 1)
        for n in range(tiles - some):
            grads(last - n).start()
        r = lax.broadcasted_iota(jnp.int32, (TILE, TILE), 0)
        c = lax.broadcasted_iota(jnp.int32, (TILE, TILE), 1)
        tri[...] = jnp.where(((r >> 6) == (c >> 6)) & (r > c), 1.0, 0.0).astype(BF16)
        state[...] = jnp.zeros_like(state)
        both[...] = jnp.zeros_like(both)
        joint[...] = jnp.zeros_like(joint)
        small[...] = jnp.zeros_like(small)

    def share(n, other):
        return to_head(joint, held.at[me], jsem.at[0, n], jsem.at[1, n], other)

    spare_copy = pltpu.make_async_copy(
        wide_in.at[pl.ds(first * count, spare)], lot.at[pl.ds(34, spare)], wsem.at[2]
    )

    def lay(dst, col):
        def copy(r, carry):
            for side in range(2):
                rows = pl.ds(pl.multiple_of(side * (MODEL_WIDTH // 2) + r * 16, 16), 16)
                dst[r, :, side * 512 : (side + 1) * 512] = both[rows, col : col + 512].astype(BF16)
            return carry

        lax.fori_loop(0, 32, copy, 0)

    @pl.when(i == second)
    def _():
        lay(few, 512)

    @pl.when(i == ready)
    def _():
        held[me] = joint[...]
        for n, other in enumerate((mate, cross, far)):
            share(n, other).start()
        lay(lot, 0)
        lot[32:] = jnp.zeros((lot.shape[0] - 32,) + lot.shape[1:], BF16)
        spare_copy.start()

    @pl.when(i == ready + 3)
    def _():
        spare_copy.wait()
        for n, other in enumerate((mate, cross, far)):
            to_head(joint, held.at[other], jsem.at[0, n], jsem.at[1, n], other).wait()
        base = 32
        sums = (held[0] + held[1]) + (held[2] + held[3])
        lot[base] = sums[0:RANK].astype(BF16)
        lot[base + 1] = jnp.zeros((16, MODEL_WIDTH), BF16)
        small[2:3, 128:384] = sums[16:17, 0:256]
        lot[base + 1, :, 0:512] = small[...].astype(BF16)

    wide_sum.step(i)

    @pl.when(i == 1)
    def _():
        def weave(r, carry):
            rows = pl.ds(pl.multiple_of(r * 16, 16), 16)
            lot[r, :, 0:128] = wq[rows, :]
            lot[r, :, 128:256] = wk[rows, :]
            lot[r, :, 256:512] = wv[rows, :]
            lot[r, :, 512:768] = wg[rows, :]
            return carry

        lax.fori_loop(0, MODEL_WIDTH // 16, weave, 0)

    @pl.when((i >= 2) & (i - 2 <= last))
    def _():
        t = last - (i - 2)
        own_cross(t).wait_recv()
        onward(t).start()

    @pl.when(i <= last)
    def _():
        t = last - i

        @pl.when(t >= some)
        def _():
            grads(t).wait_recv()

        @pl.when(t < some)
        def _():
            rg[t] = gx[...]

        gnf = gown[...] + rg[t].astype(F32)
        inv = invf[...][:, 0:1]
        hn = h1[...].astype(BF16).astype(F32) * inv
        row = stat_ref[pl.ds(t, 1), :]
        stat = jnp.broadcast_to(row, (128, TILE)).T[:, 0:1]
        grad = c_ref[...].astype(F32) + inv * (own_cols(fgain) * gnf - hn * (stat / MODEL_WIDTH))
        small[1:2, 128:384] += jnp.sum(gnf * hn, axis=0, keepdims=True)
        gh[t] = grad
        gb[t, me] = grad.astype(BF16)
        own_cross(t).start()
        own_mate(t).start()

    half = tiles // 2

    def some_feeds(low, high, at):
        @pl.when((i >= at) & (low + 2 * (i - at) < high))
        def _():
            n = low + 2 * (i - at)
            feeds(last - n).start()

            @pl.when(n + 1 < high)
            def _():
                feeds(last - n - 1).start()

    some_feeds(0, half, last + 2)
    some_feeds(half, tiles, ready)

    @pl.when((i >= 3) & (i - 3 <= last))
    def _():
        t = last - (i - 3)
        own_mate(t).wait_recv()
        onward(t).wait_recv()
        gt = jnp.zeros((TILE, BLOCK), F32)
        for j in range(4):
            cols = slice(j * BLOCK, (j + 1) * BLOCK)
            gt = gt + dot_nt(gb[t, j], wout[:, cols])
            both[cols, 768:1024] += dot_tn(gb[t, j], gated[...])
        o = oo_ref[...]
        gz = gz_ref[...]
        inv = lax.rsqrt(jnp.mean(o * o, axis=1, keepdims=True) + EPS)
        on = o * inv
        sig = jax.nn.sigmoid(gz)
        gn = gt * (gz * sig)
        joint[16:17, 0:256] += jnp.sum(gn * on, axis=0, keepdims=True)
        gain = gg_ref[...].astype(F32)
        ggz = (gt * on * gain * (sig * (1.0 + gz * (1.0 - sig)))).astype(BF16)
        gzs[t] = ggz
        both[:, 512:768] += dot_tn(na1[...], ggz)
        p = gn * gain
        go = (inv * (p - on * jnp.mean(p * on, axis=1, keepdims=True))).astype(BF16)
        qd = f1[:, 0:128].astype(BF16)
        kd = f1[:, 128:256].astype(BF16)
        v = b1[:, 0:256]
        causal, _ = span_masks(TILE, TILE)
        ga = jnp.where(causal, dot_nt(go, v), 0.0).astype(BF16)
        gqd[t] = dot_nn(ga, kd)
        gkd[t] = dot_tn(ga, qd)
        gv[t] = dot_tn(b1[:, 256:512], go)
        for c in range(PER - 1, -1, -1):
            rows = slice(c * SPAN, (c + 1) * SPAN)
            gqd[t, rows, :] += dot_nn(go[rows], ws1[c])
            fresh = dot_tn(go[rows], qd[rows])
            gw[t * PER + c] = fresh
            through = keep_ref[t, c : c + 1, :] * e1[0, c : c + 1, :]
            state[...] = through * (fresh + state[...])

    length = count // 2
    side = lax.rem(place, 2)
    line = lax.div(place, 2)
    twin = place + 1 - 2 * side
    half_rows = HV // 2
    mine = pl.ds(pl.multiple_of(side * half_rows, half_rows), half_rows)
    other = pl.ds(pl.multiple_of((1 - side) * half_rows, half_rows), half_rows)

    def to_twin():
        return to_seq(sbuf, tbuf, xsem.at[0], xsem.at[1], twin)

    def to_twin_half():
        return to_seq(xbuf, ybuf, xsem.at[2], xsem.at[3], twin)

    def to_line(p):
        return to_seq(hbuf, rbuf.at[line], esend.at[p], erecv.at[line], 2 * p + side)

    def from_line(p):
        return to_seq(hbuf, rbuf.at[p], esend.at[p], erecv.at[p], 2 * p + side)

    def two_terms(d):
        hi = d.astype(BF16).astype(F32)
        first_rows = lax.broadcasted_iota(jnp.int32, (16, HK), 0) < 8
        hi = jnp.broadcast_to(hi, (16, HK))
        return jnp.where(first_rows, hi, jnp.broadcast_to(d, (16, HK)) - hi).astype(BF16)

    def decay_of(rows):
        rows = rows.astype(F32)
        return rows[0:1] + rows[8:9]

    @pl.when(i == last + 3)
    def _():
        sbuf[0:HV, :] = state[...].astype(BF16)
        sbuf[HV : HV + 16, :] = two_terms(d_ref[0:1, :])
        to_twin().start()

    @pl.when(i == last + 4)
    def _():
        to_twin().wait_recv()
        d_mine = decay_of(sbuf[HV : HV + 16, :])
        d_twin = decay_of(tbuf[HV : HV + 16, :])
        s_mine = sbuf[mine, :].astype(F32)
        s_twin = tbuf[mine, :].astype(F32)

        @pl.when(side == 0)
        def _():
            hbuf[0:half_rows, :] = (s_mine + d_mine * s_twin).astype(BF16)

        @pl.when(side == 1)
        def _():
            hbuf[0:half_rows, :] = (s_twin + d_twin * s_mine).astype(BF16)

        hbuf[half_rows : half_rows + 16, :] = two_terms(d_mine * d_twin)

        def send(p, carry):
            to_line(p).start()
            return carry

        lax.fori_loop(0, line, send, 0)

    @pl.when(i == last + 5)
    def _():
        state[mine, :] = jnp.zeros((half_rows, HK), F32)

        def join(n, carry):
            p = length - 1 - n
            from_line(p).wait_recv()
            d = decay_of(rbuf[p, half_rows : half_rows + 16, :])
            state[mine, :] = rbuf[p, 0:half_rows, :].astype(F32) + d * state[mine, :]
            return carry

        lax.fori_loop(0, length - 1 - line, join, 0)
        xbuf[...] = state[mine, :].astype(BF16)
        to_twin_half().start()

    @pl.when(i == second)
    def _():
        def free(t, carry):
            own_cross(t).wait_send()
            own_mate(t).wait_send()
            onward(t).wait_send()
            return carry

        lax.fori_loop(0, tiles, free, 0)
        to_twin_half().wait_recv()
        state[other, :] = ybuf[...].astype(F32)

        @pl.when(side == 0)
        def _():
            state[...] = tbuf[0:HV, :].astype(F32) + decay_of(tbuf[HV : HV + 16, :]) * state[...]

    @pl.when((i >= second + 3) & (i - second - 3 <= last))
    def _():
        t = last - (i - second - 3)
        over(t).wait_recv()
        for n, other in enumerate((mate, cross, far)):
            stats(t, n, other).wait_recv()
        gna = own[lax.rem(t, 3)] + rc[t].astype(F32)
        inv = inva[...][:, 0:1]
        xn = x_ref[...].astype(F32) * inv
        row = (st_s[t] + st_r[t, 0]) + (st_r[t, 1] + st_r[t, 2])
        stat = jnp.broadcast_to(row[0:1], (128, TILE)).T[:, 0:1]
        gt_o[...] = gh[t] + inv * (own_cols(again) * gna - xn * (stat / MODEL_WIDTH))
        small[0:1, 128:384] += jnp.sum(gna * xn, axis=0, keepdims=True)

    @pl.when((i >= second + 1) & (i - second - 1 <= last))
    def _():
        t = last - (i - second - 1)
        pair(t, 0).wait_recv()
        pair(t, 1).wait_recv()
        sc[t] = (gb[t, cross].astype(F32) + mn[t, 1].astype(F32)).astype(BF16)
        over(t).start()
        own[lax.rem(t, 3)] = gb[t, me].astype(F32) + mn[t, 0].astype(F32)

    @pl.when((i >= second) & (i - second <= last))
    def _():
        t = last - (i - second)
        qf = f2[:, 0:128]
        kf = f2[:, 128:256]
        kd = kf.astype(BF16)
        pieces = [None] * PER
        for c in range(PER - 1, -1, -1):
            rows = slice(c * SPAN, (c + 1) * SPAN)
            low = state[...].astype(BF16)
            gkd[t, rows, :] += dot_nn(b2[rows, 0:256], low)
            gv[t, rows, :] += dot_nt(kd[rows], low)
            ge = gw[t * PER + c] + state[...]
            pieces[c] = jnp.broadcast_to(jnp.sum(ge * ws2[c].astype(F32), axis=0, keepdims=True), (SPAN, HK))
            state[...] = (keep_ref[t, c : c + 1, :] * e2[0, c : c + 1, :]) * ge
        gq = gqd[t]
        gk = gkd[t]
        diff = gq * qf - gk * kf
        gg = jnp.concatenate(pieces, axis=0) - fold(dot_nn(tri[...], three(diff)))
        glogit = gg * f2[:, 512:640]
        small[3:4, 128:256] += jnp.sum(glogit, axis=0, keepdims=True)
        hi = glogit.astype(BF16)
        lo = (glogit - hi.astype(F32)).astype(BF16)
        glr = dot_nt(hi, rup[...]) + dot_nt(lo, rup[...])
        lr = b2[:, 512 : 512 + RANK]
        small[:, 0:128] += dot_tn(lr, hi) + dot_tn(lr, lo)
        glr = glr.astype(BF16)
        joint[0:RANK, :] += dot_tn(glr, na[...])
        gcat[:, 0:128] = (gq * f2[:, 256:384]).astype(BF16)
        gcat[:, 128:256] = (gk * f2[:, 384:512]).astype(BF16)
        gcat[:, 256:512] = gv[t].astype(BF16)
        gcat[:, 512:768] = gzs[t]
        g = gcat[...]
        stat = jnp.zeros((TILE, 1), F32)
        for j in range(4):
            cols = slice(j * BLOCK, (j + 1) * BLOCK)
            gj = dot_nt(g, lot[16 * j : 16 * (j + 1), :, 0:768].reshape(BLOCK, 768)) + dot_nn(glr, wr[:, cols])
            stat = stat + jnp.sum(gj * na[:, cols].astype(F32), axis=1, keepdims=True)
            gb[t, j] = gj.astype(BF16)
        pair(t, 1).start()
        pair(t, 0).start()
        st_s[t] = jnp.broadcast_to(stat, (TILE, 128)).T[0:8, :]
        for n, other in enumerate((mate, cross, far)):
            stats(t, n, other).start()
        both[:, 0:512] += dot_tn(na[...], g[:, 0:512])

    @pl.when((i >= feed) & (i - feed <= last))
    def _():
        t = last - (i - feed)
        feeds(t).wait_recv()
        lo_o[...] = (h2[...] + (pown[...] + rg[t].astype(F32))).astype(BF16)

    drained = first + 2 * levels(count) * LAGS[0]
    head_units = pl.ds(0, first * count)
    tail_units = pl.ds(first * count, (parts - first) * count)
    head_copy = pltpu.make_async_copy(wide_o.at[head_units], units_o.at[head_units], wsem.at[0])
    tail_copy = pltpu.make_async_copy(wide_o.at[tail_units], units_o.at[tail_units], wsem.at[1])

    @pl.when(i == drained)
    def _():
        head_copy.start()

    @pl.when(i == pl.num_programs(0) - 1)
    def _():
        tail_copy.start()
        wide_sum.finish()
        tail_copy.wait()
        head_copy.wait()

        to_twin().wait_send()
        to_twin_half().wait_send()

        def sent(p, carry):
            to_line(p).wait_send()
            return carry

        lax.fori_loop(0, line, sent, 0)

        def out(t, carry):
            @pl.when(t >= some)
            def _():
                grads(t).wait_send()

            feeds(t).wait_send()
            pair(t, 0).wait_send()
            pair(t, 1).wait_send()
            over(t).wait_send()
            for n, other in enumerate((mate, cross, far)):
                stats(t, n, other).wait_send()
            return carry

        lax.fori_loop(0, tiles, out, 0)


def back(fixed, wide, gsend, psend, x, cot, gx, gown, h, invf, f, o, oo, gated, ws, b, e, na, pown, inva):
    rows = h.shape[0]
    tiles = rows // TILE
    count = lax.axis_size("seq")
    second = tiles + 3 + WAIT
    width = MODEL_WIDTH
    segments = plan(count, wide.shape[0], tiles)
    first = segments[0][1]
    parts = segments[2][1]
    units = parts * count
    feed = second + tiles + 4
    steps = max(feed + tiles, last_step(count, segments) + 1)
    ts = functools.partial(tile_spec, tiles, back=True)
    outs = [
        ((rows, BLOCK), F32, ts((TILE, BLOCK), second + 3)),
        ((rows, BLOCK), BF16, ts((TILE, BLOCK), feed)),
        ((units, 16, width), BF16, pl.BlockSpec(memory_space=pl.ANY)),
    ]
    tiled = lambda n: pltpu.VMEM((tiles, n, TILE, BLOCK), BF16)
    flat = lambda n, d: pltpu.VMEM((tiles, TILE, n), d)
    return pl.pallas_call(
        functools.partial(back_kernel, tiles, count, segments),
        grid=(steps,),
        out_shape=[jax.ShapeDtypeStruct(s, d) for s, d, _ in outs],
        in_specs=[whole(a.shape) for a in fixed]
        + [
            pl.BlockSpec(memory_space=pl.ANY), pl.BlockSpec(memory_space=pl.ANY), pl.BlockSpec(memory_space=pl.ANY),
            ts((TILE, BLOCK), second + 3), ts((TILE, BLOCK), 0),
            pl.BlockSpec((TILE, BLOCK), lambda i: (jnp.clip(tiles - 1 - i, 0, tiles - 4), 0)),
            ts((TILE, BLOCK), 0), ts((TILE, BLOCK), 0), ts((TILE, 128), 0),
            ts((TILE, 256), 3), ts((TILE, 256), 3), ts((TILE, 256), 3), ts((TILE, 256), 3),
            ts((PER, HV, HK), 3), ts((TILE, 640), 3), ts((1, 8, 128), 3), ts((TILE, width), 3),
            ts((TILE, 640), second), ts((TILE, 640), second), ts((PER, HV, HK), second), ts((1, 8, 128), second),
            ts((TILE, width), second), ts((TILE, BLOCK), feed), ts((TILE, BLOCK), feed),
            ts((TILE, 128), second + 3),
        ],
        out_specs=[s for _, _, s in outs],
        scratch_shapes=[
            pltpu.VMEM((TILE, TILE), BF16),
            flat(BLOCK, BF16), flat(BLOCK, F32),
            tiled(4),
            flat(BLOCK, BF16),
            pltpu.VMEM((rows // SPAN, HV, HK), F32),
            flat(HK, F32), flat(HK, F32), flat(HV, F32),
            pltpu.VMEM((HV, HK), F32),
            pltpu.VMEM((HV + 16, HK), BF16),
            pltpu.VMEM((HV + 16, HK), BF16),
            pltpu.VMEM((HV // 2 + 16, HK), BF16),
            pltpu.VMEM((HV // 2, HK), BF16),
            pltpu.VMEM((HV // 2, HK), BF16),
            pltpu.VMEM((count // 2, HV // 2 + 16, HK), BF16),
            pltpu.VMEM((TILE, 768), BF16),
            tiled(2), flat(BLOCK, BF16), flat(BLOCK, BF16),
            pltpu.VMEM((3, TILE, BLOCK), F32),
            pltpu.VMEM((tiles, 8, TILE), F32),
            pltpu.VMEM((tiles, 3, 8, TILE), F32),
            pltpu.VMEM((width, width), F32),
            pltpu.VMEM((24, width), F32),
            pltpu.VMEM((16, 512), F32),
            pltpu.VMEM((4, 24, width), F32),
            pltpu.VMEM((units, 16, width), BF16),
            pltpu.VMEM((32, 16, width), BF16),
            pltpu.VMEM((max(width // 16, (parts - segments[2][0]) * count), 16, width), BF16),
            pltpu.SemaphoreType.DMA((2, tiles)),
            pltpu.SemaphoreType.DMA((2, tiles)),
            pltpu.SemaphoreType.DMA((6, tiles)),
            pltpu.SemaphoreType.DMA((4, tiles)),
            pltpu.SemaphoreType.DMA((2, tiles)),
            pltpu.SemaphoreType.DMA((2, 3, tiles)),
            pltpu.SemaphoreType.DMA((count // 2,)),
            pltpu.SemaphoreType.DMA((count // 2,)),
            pltpu.SemaphoreType.DMA((4,)),
            pltpu.SemaphoreType.DMA((3,)),
            pltpu.SemaphoreType.DMA((2, 3)),
        ]
        + Sum.scratch(count, parts, first, wide.shape[1:]),
        compiler_params=pltpu.CompilerParams(
            collective_id=3, has_side_effects=True, vmem_limit_bytes=VMEM_LIMIT,
            dimension_semantics=("arbitrary",),
        ),
        name="back",
    )(*fixed, wide, gsend, psend, x, cot, gx, gown, h, invf, f, o, oo, gated, ws, b, e, na, f, b, ws, e, na, h, pown, inva)


def shards(
    tokens,
    row_starts,
    attn_gain,
    query_weight,
    key_weight,
    value_weight,
    gate_weight,
    rank_down,
    rank_up,
    rank_bias,
    group_gain,
    out_weight,
    feed_gain,
    feed_gate,
    feed_up,
    feed_down,
    cotangent,
):
    rows = tokens.shape[0]
    tiles = rows // TILE
    spans = rows // SPAN
    span_ids = lax.axis_index("seq") * spans + jnp.arange(spans, dtype=jnp.int32)
    resets = jnp.any((row_starts // SPAN)[None, :] == span_ids[:, None], axis=1).astype(F32)
    keep = jnp.pad((1.0 - resets).reshape(tiles, PER, 1), ((0, 0), (0, 8 - PER), (0, 0)))
    keep = jnp.broadcast_to(keep, (tiles, 8, 128))
    weights = (
        query_weight[0], key_weight[0], value_weight[0], gate_weight[0], jnp.swapaxes(rank_down[0], 0, 1), rank_up[0]
    )
    na, cg, inva, f, b, o, u, e, inc, dec = front(tokens, cotangent, keep, attn_gain, *weights, rank_bias)
    gated, oo, ws, h, invf, gsend, gown, psend, pown, stat, wide, gx = ffn(
        tokens, keep, inc, group_gain, feed_gain, out_weight[0], jnp.swapaxes(feed_gate[0], 0, 1),
        jnp.swapaxes(feed_up[0], 0, 1), feed_down[0], f, o, u, e, cg,
    )
    fixed = (
        keep, dec, stat, group_gain, attn_gain, feed_gain, out_weight[0],
    ) + weights
    grad_tokens, layer_out, units = back(fixed, wide, gsend, psend, tokens, cotangent, gx, gown, h, invf, f, o, oo, gated, ws, b, e, na, pown, inva)
    dfg, dfu, dfd, dq, dk, dv, dg, dwo, dr, dup, dag, dffg, db, dgg, grad_tokens, layer_out = finish(
        units, grad_tokens, layer_out, feed_gate.shape[2], wide.shape[0], lax.axis_size("seq")
    )
    dfg, dfu, dr = (jnp.swapaxes(a, 0, 1) for a in (dfg, dfu, dr))
    grads = (dag, dq[None], dk[None], dv[None], dg[None], dr[None], dup[None], db, dgg, dwo[None], dffg, dfg[None], dfu[None], dfd[None])
    return (layer_out, grad_tokens) + grads


def solution(mesh):
    placed = (
        P("seq", "head"),
        P(),
        P(),
        P(None, None, "head"),
        P(None, None, "head"),
        P(None, None, "head"),
        P(None, None, "head"),
        P(),
        P(None, None, "head"),
        P(None, "head"),
        P(),
        P(None, "head", None),
        P(),
        P(None, None, "head"),
        P(None, None, "head"),
        P(None, "head", None),
        P("seq", "head"),
    )
    return jax.shard_map(
        shards,
        mesh=mesh,
        in_specs=placed,
        out_specs=(
            P("seq", "head"),
            P("seq", "head"),
            P(None, "head"),
            P(None, None, "head"),
            P(None, None, "head"),
            P(None, None, "head"),
            P(None, None, "head"),
            P(),
            P(None, None, "head"),
            P(None, "head"),
            P(),
            P(None, "head", None),
            P(None, "head"),
            P(None, None, "head"),
            P(None, None, "head"),
            P(None, "head", None),
        ),
        check_vma=False,
    )
```

```python
import functools

import jax
import jax.numpy as jnp
from jax import lax
from jax.experimental import pallas as pl
from jax.experimental.pallas import tpu as pltpu
from jax.sharding import PartitionSpec as P

MODEL_WIDTH = 1024
HK = 128
HV = 256
SPAN = 64
RANK = 16
EPS = 1e-06
GATE_NORM = 16.0
TILE = 256
PER = TILE // SPAN
BLOCK = 256
AHEAD = 3
F32 = jnp.float32
BF16 = jnp.bfloat16
MESH = pl.DeviceIdType.MESH
VMEM_LIMIT = 62 * 1024 * 1024


def dot_nn(a, b):
    return jnp.dot(a, b, preferred_element_type=F32)


def dot_nt(a, b):
    return lax.dot_general(a, b, (((1,), (1,)), ((), ())), preferred_element_type=F32)


def dot_tn(a, b):
    return lax.dot_general(a, b, (((0,), (0,)), ((), ())), preferred_element_type=F32)


def peers():
    me = lax.axis_index("head")
    mate = me + 1 - 2 * lax.rem(me, 2)
    cross = lax.rem(me + 2, 4)
    far = cross + 1 - 2 * lax.rem(cross, 2)
    return me, mate, cross, far


def greet_head():
    _, mate, cross, far = peers()
    barrier = pltpu.get_barrier_semaphore()
    for other in (mate, cross, far):
        pl.semaphore_signal(barrier, inc=1, device_id={"head": other}, device_id_type=MESH)


def greet_seq(count):
    place = lax.axis_index("seq")
    barrier = pltpu.get_barrier_semaphore()

    def one(step, carry):
        other = lax.rem(place + step, count)
        pl.semaphore_signal(barrier, inc=1, device_id={"seq": other}, device_id_type=MESH)
        return carry

    lax.fori_loop(1, count, one, 0)


def to_head(src, dst, send, recv, other):
    return pltpu.make_async_remote_copy(
        src_ref=src, dst_ref=dst, send_sem=send, recv_sem=recv,
        device_id={"head": other}, device_id_type=MESH,
    )


def to_seq(src, dst, send, recv, other):
    return pltpu.make_async_remote_copy(
        src_ref=src, dst_ref=dst, send_sem=send, recv_sem=recv,
        device_id={"seq": other}, device_id_type=MESH,
    )


def span_masks(rows, cols):
    r = lax.broadcasted_iota(jnp.int32, (rows, cols), 0)
    c = lax.broadcasted_iota(jnp.int32, (rows, cols), 1)
    same = (r >> 6) == (c >> 6)
    return same & (r >= c), same


def three(x):
    a = x.astype(BF16)
    rest = x - a.astype(F32)
    b = rest.astype(BF16)
    c = (rest - b.astype(F32)).astype(BF16)
    return jnp.concatenate([a, b, c], axis=1)


def fold(x):
    w = x.shape[1] // 3
    return x[:, :w] + x[:, w : 2 * w] + x[:, 2 * w :]


def front_kernel(
    tiles, count,
    x_ref, c_ref, keep_ref, gain_ref, wq, wk, wv, wg, wr, rup, bias_ref,
    na_o, cg_o, inv_o, f_o, b_o, o_o, u_o, e_o, in_o, d_o,
    grid_buf, wcat, tri, state, decay, sbuf, rbuf, sems, esend, erecv, fsem,
):
    i = pl.program_id(0)
    me, mate, cross, far = peers()
    place = lax.axis_index("seq")
    total = 2 * tiles

    def fetch(m, ref, n):
        rows = pl.ds(pl.multiple_of(n * TILE, TILE), TILE)
        return pltpu.make_async_copy(ref.at[rows], grid_buf.at[m, me], fsem.at[m])

    def own_mate(m):
        return to_head(grid_buf.at[m, me], grid_buf.at[m, me], sems.at[0, m], sems.at[1, m], mate)

    def own_cross(m):
        return to_head(grid_buf.at[m, me], grid_buf.at[m, me], sems.at[2, m], sems.at[3, m], cross)

    def onward(m):
        return to_head(grid_buf.at[m, cross], grid_buf.at[m, cross], sems.at[4, m], sems.at[5, m], mate)

    @pl.when(i == 0)
    def _():
        def own(m, carry):
            fetch(m, x_ref, m).start()
            return carry

        def own_too(m, carry):
            fetch(m + tiles, c_ref, m).start()
            return carry

        lax.fori_loop(0, tiles, own, 0)
        lax.fori_loop(0, tiles, own_too, 0)
        greet_head()
        greet_seq(count)
        pl.semaphore_wait(pltpu.get_barrier_semaphore(), 3 + count - 1)
        for m in range(AHEAD):
            fetch(m, x_ref, m).wait()
            own_cross(m).start()
            own_mate(m).start()
        wcat[:, 0:128] = wq[...]
        wcat[:, 128:256] = wk[...]
        wcat[:, 256:512] = wv[...]
        wcat[:, 512:768] = wg[...]
        causal, same = span_masks(TILE, TILE)
        tri[0:TILE, :] = jnp.where(causal, 1.0, 0.0).astype(BF16)
        tri[TILE : 2 * TILE, :] = jnp.where(same, 1.0, 0.0).astype(BF16)
        state[...] = jnp.zeros_like(state)
        decay[...] = jnp.ones_like(decay)

    @pl.when(i < total)
    def _():
        own_cross(i).wait_recv()
        onward(i).start()

    @pl.when(i + AHEAD < total)
    def _():
        fetch(i + AHEAD, x_ref, 0).wait()
        own_cross(i + AHEAD).start()
        own_mate(i + AHEAD).start()

    @pl.when(i >= 1)
    def _():
        own_mate(i - 1).wait_recv()
        onward(i - 1).wait_recv()

    @pl.when((i >= 1) & (i <= tiles))
    def _():
        m = i - 1
        squares = jnp.zeros((TILE, 1), F32)
        for j in range(4):
            xj = grid_buf[m, j].astype(F32)
            squares = squares + jnp.sum(xj * xj, axis=1, keepdims=True)
        inv = lax.rsqrt(squares / MODEL_WIDTH + EPS)
        inv_o[...] = jnp.broadcast_to(inv, (TILE, 128))
        for j in range(4):
            cols = slice(j * BLOCK, (j + 1) * BLOCK)
            xj = grid_buf[m, j].astype(F32)
            na_o[:, cols] = (xj * inv * gain_ref[:, cols].astype(F32)).astype(BF16)
        proj = dot_nn(na_o[...], wcat[...])
        q = proj[:, 0:128]
        k = proj[:, 128:256]
        v = proj[:, 256:512].astype(BF16)
        o_o[:, 0:256] = proj[:, 512:768]
        lr = dot_nt(na_o[...], wr[...]).astype(BF16)
        z = dot_nn(lr, rup[...]) + bias_ref[...].astype(F32)
        g = (jnp.minimum(z, 0.0) - jnp.log1p(jnp.exp(-jnp.abs(z)))) / GATE_NORM
        sums = fold(dot_nn(tri[...], three(g)))
        b = sums[0:TILE]
        e = sums[TILE : 2 * TILE]
        fq = (HK ** (-0.5)) * jnp.exp(b - e)
        fk = jnp.exp(e - b)
        qf = q * fq
        kf = k * fk
        f_o[:, 0:128] = qf
        f_o[:, 128:256] = kf
        f_o[:, 256:384] = fq
        f_o[:, 384:512] = fk
        f_o[:, 512:640] = jax.nn.sigmoid(-z) / GATE_NORM
        qd = qf.astype(BF16)
        kd = kf.astype(BF16)
        causal, _ = span_masks(TILE, TILE)
        scores = jnp.where(causal, dot_nt(qd, kd), 0.0).astype(BF16)
        b_o[:, 0:256] = v
        b_o[:, 256:512] = scores
        b_o[:, 512 : 512 + RANK] = lr
        o_o[:, 256:512] = dot_nn(scores, v)
        for c in range(PER):
            rows = slice(c * SPAN, (c + 1) * SPAN)
            update = dot_tn(v[rows], kd[rows])
            u_o[c] = update
            ee = jnp.exp(e[c * SPAN : c * SPAN + 1])
            e_o[0, c : c + 1, :] = ee
            through = keep_ref[m, c : c + 1, :] * ee
            state[...] = through * state[...] + update
            decay[...] = through * decay[...]

    @pl.when(i == tiles)
    def _():
        d_o[...] = decay[...]
        sbuf[0:HV, :] = state[...].astype(BF16)
        d = decay[...]
        hi = d.astype(BF16).astype(F32)
        first = lax.broadcasted_iota(jnp.int32, (16, 128), 0) < 8
        both = jnp.where(first, jnp.concatenate([hi, hi], axis=0), jnp.concatenate([d - hi, d - hi], axis=0))
        sbuf[HV : HV + 16, :] = both.astype(BF16)

        def send(p, carry):
            to_seq(sbuf, rbuf.at[place], esend.at[p], erecv.at[place], p).start()
            return carry

        lax.fori_loop(place + 1, count, send, 0)

    @pl.when(i > tiles)
    def _():
        m = i - 1
        for j in range(4):
            cg_o[:, j * BLOCK : (j + 1) * BLOCK] = grid_buf[m, j]

    @pl.when(i == total)
    def _():
        in_o[...] = jnp.zeros_like(in_o)

        def join(p, carry):
            to_seq(sbuf, rbuf.at[p], esend.at[p], erecv.at[p], place).wait_recv()
            got = rbuf[p].astype(F32)
            d = got[HV : HV + 1] + got[HV + 8 : HV + 9]
            in_o[...] = got[0:HV] + d * in_o[...]
            return carry

        lax.fori_loop(0, place, join, 0)

        def sent(p, carry):
            to_seq(sbuf, rbuf.at[place], esend.at[p], erecv.at[place], p).wait_send()
            return carry

        lax.fori_loop(place + 1, count, sent, 0)

        def out(m, carry):
            own_cross(m).wait_send()
            own_mate(m).wait_send()
            onward(m).wait_send()
            return carry

        lax.fori_loop(0, total, out, 0)


def whole(shape):
    zeros = (0,) * len(shape)
    return pl.BlockSpec(shape, lambda i: zeros, pipeline_mode=pl.Buffered(1))


def front(x, cot, keep, gain, wq, wk, wv, wg, wr, rup, bias):
    rows = x.shape[0]
    tiles = rows // TILE
    count = lax.axis_size("seq")

    def tile(shape, lag, axis0=True):
        rest = (0,) * (len(shape) - 1)
        return pl.BlockSpec(shape, lambda i: (jnp.clip(i - lag, 0, tiles - 1),) + rest)

    ins = (x, cot, keep, gain, wq, wk, wv, wg, wr, rup, bias)
    outs = [
        ((rows, MODEL_WIDTH), BF16, tile((TILE, MODEL_WIDTH), 1)),
        ((rows, MODEL_WIDTH), BF16, tile((TILE, MODEL_WIDTH), 1 + tiles)),
        ((rows, 128), F32, tile((TILE, 128), 1)),
        ((rows, 640), F32, tile((TILE, 640), 1)),
        ((rows, 640), BF16, tile((TILE, 640), 1)),
        ((rows, 512), F32, tile((TILE, 512), 1)),
        ((rows // SPAN, HV, HK), F32, tile((PER, HV, HK), 1)),
        ((tiles, 8, 128), F32, tile((1, 8, 128), 1)),
        ((HV, HK), F32, whole((HV, HK))),
        ((8, 128), F32, whole((8, 128))),
    ]
    return pl.pallas_call(
        functools.partial(front_kernel, tiles, count),
        grid=(2 * tiles + 1,),
        out_shape=[jax.ShapeDtypeStruct(s, d) for s, d, _ in outs],
        in_specs=[pl.BlockSpec(memory_space=pl.ANY)] * 2 + [whole(a.shape) for a in ins[2:]],
        out_specs=[s for _, _, s in outs],
        scratch_shapes=[
            pltpu.VMEM((2 * tiles, 4, TILE, BLOCK), BF16),
            pltpu.VMEM((MODEL_WIDTH, 768), BF16),
            pltpu.VMEM((2 * TILE, TILE), BF16),
            pltpu.VMEM((HV, HK), F32),
            pltpu.VMEM((8, 128), F32),
            pltpu.VMEM((HV + 16, HK), BF16),
            pltpu.VMEM((count, HV + 16, HK), BF16),
            pltpu.SemaphoreType.DMA((6, 2 * tiles)),
            pltpu.SemaphoreType.DMA((count,)),
            pltpu.SemaphoreType.DMA((count,)),
            pltpu.SemaphoreType.DMA((2 * tiles,)),
        ],
        compiler_params=pltpu.CompilerParams(
            collective_id=1, has_side_effects=True, vmem_limit_bytes=VMEM_LIMIT,
            dimension_semantics=("arbitrary",),
        ),
        name="front",
    )(*ins)


def tile_spec(tiles, shape, lag, back=False, col=0):
    rest = (0,) * (len(shape) - 2) + (col,)

    def index(i):
        t = jnp.clip(i - lag, 0, tiles - 1)
        return ((tiles - 1 - t) if back else t,) + rest

    return pl.BlockSpec(shape, index)


def up_to(n, step):
    return (n + step - 1) // step * step


def ffn_kernel(
    tiles,
    x_ref, keep_ref, in_ref, gg_ref, gain_ref, wout, wfg_in, wfu_in, wfd_in,
    f_ref, o_ref, u_ref, e_ref, cg_ref,
    gated_o, oo_o, ws_o, h_o, inv_o, gsend_o, gown_o, psend_o, pown_o, stat_o, wide_o, gx_o,
    state, pa, pp, pg, ma, mp, mg, sc, rc, own, hg, nf_s, acc, wfg, wfu, wfd, st_s, st_r, gxs, gxr,
    asem, psem, gsem, csem, hsem, tsem, wsem, xsem,
):
    i = pl.program_id(0)
    me, mate, cross, far = peers()
    last = tiles - 1
    hidden = wfg.shape[0]

    def pair(buf, got, sem, t, which):
        block = mate if which == 0 else far
        return to_head(buf.at[t, block], got.at[t, which], sem.at[2 * which, t], sem.at[2 * which + 1, t], mate)

    def over(t):
        return to_head(sc.at[t], rc.at[t], csem.at[0, t], csem.at[1, t], cross)

    def own_mate(t):
        return to_head(hg.at[t, me], hg.at[t, me], hsem.at[0, t], hsem.at[1, t], mate)

    def own_cross(t):
        return to_head(hg.at[t, me], hg.at[t, me], hsem.at[2, t], hsem.at[3, t], cross)

    def onward(t):
        return to_head(hg.at[t, cross], hg.at[t, cross], hsem.at[4, t], hsem.at[5, t], mate)

    some = gxs.shape[0]

    def early(t):
        return to_head(gxs.at[t], gxr.at[t], xsem.at[0, t], xsem.at[1, t], cross)

    def stats(n, other):
        return to_head(st_s, st_r.at[n], tsem.at[0, n], tsem.at[1, n], other)

    fetches = [
        pltpu.make_async_copy(src, dst, wsem.at[n])
        for n, (src, dst) in enumerate(((wfg_in, wfg), (wfu_in, wfu), (wfd_in, wfd)))
    ]

    @pl.when(i == 4)
    def _():
        for fetch in fetches:
            fetch.wait()

    @pl.when(i == 0)
    def _():
        for fetch in fetches:
            fetch.start()
        greet_head()
        state[...] = in_ref[...]
        acc[...] = jnp.zeros_like(acc)
        st_s[...] = jnp.zeros_like(st_s)
        pl.semaphore_wait(pltpu.get_barrier_semaphore(), 3)

    @pl.when((i >= 6) & (i - 6 <= last))
    def _():
        t = i - 6
        own_mate(t).wait_recv()
        onward(t).wait_recv()
        squares = jnp.zeros((TILE, 1), F32)
        for j in range(4):
            hj = hg[t, j].astype(F32)
            squares = squares + jnp.sum(hj * hj, axis=1, keepdims=True)
        inv = lax.rsqrt(squares / MODEL_WIDTH + EPS)
        inv_o[...] = jnp.broadcast_to(inv, (TILE, 128))
        for j in range(4):
            cols = slice(j * BLOCK, (j + 1) * BLOCK)
            nf_s[:, cols] = (hg[t, j].astype(F32) * inv * gain_ref[:, cols].astype(F32)).astype(BF16)
        nf = nf_s[...]
        fg = dot_nt(nf, wfg[...])
        fu = dot_nt(nf, wfu[...])
        sig = jax.nn.sigmoid(fg)
        silu = fg * sig
        act = (silu * fu).astype(BF16)
        cg = cg_ref[...]
        for j in range(4):
            pp[t, j] = dot_nn(act, wfd[:, j * BLOCK : (j + 1) * BLOCK]).astype(BF16)
        for which in range(2):
            pair(pp, mp, psem, t, which).start()
        gact = dot_nt(cg, wfd[...])
        gfg = (gact * fu * (sig * (1.0 + fg * (1.0 - sig)))).astype(BF16)
        gfu = (gact * silu).astype(BF16)
        stat = jnp.zeros((TILE, 1), F32)
        for j in range(4):
            rows = slice(j * BLOCK, (j + 1) * BLOCK)
            gj = dot_nn(gfg, wfg[:, rows]) + dot_nn(gfu, wfu[:, rows])
            stat = stat + jnp.sum(gj * nf_s[:, rows].astype(F32), axis=1, keepdims=True)
            pg[t, j] = gj.astype(BF16)
        for which in range(2):
            pair(pg, mg, gsem, t, which).start()
        st_s[pl.ds(t, 1), :] = jnp.broadcast_to(stat, (TILE, 128)).T[0:1, :]
        acc[0:hidden, :] += dot_tn(gfg, nf)
        acc[hidden : 2 * hidden, :] += dot_tn(gfu, nf)
        acc[2 * hidden : 3 * hidden, :] += dot_tn(act, cg)

    @pl.when((i >= 5) & (i - 5 <= last))
    def _():
        t = i - 5
        own_cross(t).wait_recv()
        onward(t).start()

    @pl.when((i >= 3) & (i - 3 <= last))
    def _():
        t = i - 3
        over(t).wait_recv()
        rows = pl.ds(pl.multiple_of(t * TILE, TILE), TILE)
        h = x_ref[rows, :].astype(F32) + (own[lax.rem(t, 4)] + rc[t].astype(F32))
        h_o[...] = h
        hg[t, me] = h.astype(BF16)
        own_cross(t).start()
        own_mate(t).start()

    @pl.when((i >= 1) & (i - 1 <= last))
    def _():
        t = i - 1
        pair(pa, ma, asem, t, 0).wait_recv()
        pair(pa, ma, asem, t, 1).wait_recv()
        sc[t] = (pa[t, cross].astype(F32) + ma[t, 1].astype(F32)).astype(BF16)
        over(t).start()
        own[lax.rem(t, 4)] = pa[t, me].astype(F32) + ma[t, 0].astype(F32)

    @pl.when(i <= last)
    def _():
        t = i
        for c in range(PER):
            rows = slice(c * SPAN, (c + 1) * SPAN)
            scaled = (keep_ref[t, c : c + 1, :] * e_ref[0, c : c + 1, :]) * state[...]
            low = scaled.astype(BF16)
            ws_o[c] = low
            state[...] = scaled + u_ref[c]
            oo_o[rows, :] = o_ref[rows, 256:512] + dot_nt(f_ref[rows, :].astype(BF16), low)
        o = oo_o[...]
        gz = o_ref[:, 0:256]
        inv = lax.rsqrt(jnp.mean(o * o, axis=1, keepdims=True) + EPS)
        gated = (o * inv * gg_ref[...].astype(F32) * (gz * jax.nn.sigmoid(gz))).astype(BF16)
        gated_o[...] = gated
        for j in range(4):
            pa[t, j] = dot_nn(gated, wout[:, j * BLOCK : (j + 1) * BLOCK]).astype(BF16)
        pair(pa, ma, asem, t, 1).start()
        pair(pa, ma, asem, t, 0).start()

    @pl.when((i >= 7) & (i - 7 <= last))
    def _():
        t = i - 7
        for which in range(2):
            pair(pp, mp, psem, t, which).wait_recv()
            pair(pg, mg, gsem, t, which).wait_recv()
        psend_o[...] = (pp[t, cross].astype(F32) + mp[t, 1].astype(F32)).astype(BF16)
        pown_o[...] = pp[t, me].astype(F32) + mp[t, 0].astype(F32)
        gs = (pg[t, cross].astype(F32) + mg[t, 1].astype(F32)).astype(BF16)
        gsend_o[...] = gs

        @pl.when(t < some)
        def _():
            gxs[t] = gs

        gown_o[...] = pg[t, me].astype(F32) + mg[t, 0].astype(F32)

    @pl.when(i == some + 6)
    def _():
        for t in range(some):
            early(t).start()

    @pl.when(i == last + 6)
    def _():
        for n, other in enumerate((mate, cross, far)):
            stats(n, other).start()

    @pl.when(i == last + 7)
    def _():
        used = 3 * hidden // 16

        def unit(r, carry):
            wide_o[r] = acc[pl.ds(pl.multiple_of(r * 16, 16), 16), :].astype(BF16)
            return carry

        lax.fori_loop(0, used, unit, 0)
        for n, other in enumerate((mate, cross, far)):
            stats(n, other).wait()
        for t in range(some):
            early(t).wait()
            gx_o[t * TILE : (t + 1) * TILE, :] = gxr[t]
        stat_o[...] = (st_s[...] + st_r[0]) + (st_r[1] + st_r[2])

        def out(t, carry):
            for which in range(2):
                pair(pa, ma, asem, t, which).wait_send()
                pair(pp, mp, psem, t, which).wait_send()
                pair(pg, mg, gsem, t, which).wait_send()
            over(t).wait_send()
            own_cross(t).wait_send()
            own_mate(t).wait_send()
            onward(t).wait_send()
            return carry

        lax.fori_loop(0, tiles, out, 0)


def ffn(x, keep, inc, gg, gain, wout, wfg, wfu, wfd, f, o, u, e, cg):
    rows = x.shape[0]
    tiles = rows // TILE
    hidden, width = wfg.shape
    units = 3 * hidden // 16
    some = tiles - 3
    assert 3 < tiles <= 8 and hidden % 16 == 0
    ts = functools.partial(tile_spec, tiles)
    ins = (x, keep, inc, gg, gain, wout)
    outs = [
        ((rows, BLOCK), BF16, ts((TILE, BLOCK), 0)),
        ((rows, HV), F32, ts((TILE, HV), 0)),
        ((rows // SPAN, HV, HK), BF16, ts((PER, HV, HK), 0)),
        ((rows, BLOCK), F32, ts((TILE, BLOCK), 3)),
        ((rows, 128), F32, ts((TILE, 128), 6)),
        ((rows, BLOCK), BF16, ts((TILE, BLOCK), 7)),
        ((rows, BLOCK), F32, ts((TILE, BLOCK), 7)),
        ((rows, BLOCK), BF16, ts((TILE, BLOCK), 7)),
        ((rows, BLOCK), F32, ts((TILE, BLOCK), 7)),
        ((8, TILE), F32, whole((8, TILE))),
        ((units, 16, width), BF16, whole((units, 16, width))),
        ((some * TILE, BLOCK), BF16, whole((some * TILE, BLOCK))),
    ]
    tiled = lambda n: pltpu.VMEM((tiles, n, TILE, BLOCK), BF16)
    return pl.pallas_call(
        functools.partial(ffn_kernel, tiles),
        grid=(tiles + 7,),
        out_shape=[jax.ShapeDtypeStruct(s, d) for s, d, _ in outs],
        in_specs=[whole(a.shape) for a in ins]
        + [pl.BlockSpec(memory_space=pl.ANY)] * 3
        + [
            ts((TILE, 128), 0), ts((TILE, 512), 0), ts((PER, HV, HK), 0), ts((1, 8, 128), 0),
            ts((TILE, MODEL_WIDTH), 6),
        ],
        out_specs=[s for _, _, s in outs],
        scratch_shapes=[
            pltpu.VMEM((HV, HK), F32),
            tiled(4), tiled(4), tiled(4), tiled(2), tiled(2), tiled(2),
            pltpu.VMEM((tiles, TILE, BLOCK), BF16),
            pltpu.VMEM((tiles, TILE, BLOCK), BF16),
            pltpu.VMEM((4, TILE, BLOCK), F32),
            tiled(4),
            pltpu.VMEM((TILE, MODEL_WIDTH), BF16),
            pltpu.VMEM((3 * hidden, width), F32),
            pltpu.VMEM((hidden, width), BF16),
            pltpu.VMEM((hidden, width), BF16),
            pltpu.VMEM((hidden, width), BF16),
            pltpu.VMEM((8, TILE), F32),
            pltpu.VMEM((3, 8, TILE), F32),
            pltpu.VMEM((some, TILE, BLOCK), BF16),
            pltpu.VMEM((some, TILE, BLOCK), BF16),
            pltpu.SemaphoreType.DMA((4, tiles)),
            pltpu.SemaphoreType.DMA((4, tiles)),
            pltpu.SemaphoreType.DMA((4, tiles)),
            pltpu.SemaphoreType.DMA((2, tiles)),
            pltpu.SemaphoreType.DMA((6, tiles)),
            pltpu.SemaphoreType.DMA((2, 3)),
            pltpu.SemaphoreType.DMA((3,)),
            pltpu.SemaphoreType.DMA((2, some)),
        ],
        compiler_params=pltpu.CompilerParams(
            collective_id=2, has_side_effects=True, vmem_limit_bytes=VMEM_LIMIT,
            dimension_semantics=("arbitrary",),
        ),
        name="ffn",
    )(*ins, wfg, wfu, wfd, f, o, u, e, cg)


LAGS = (2, 2, 2)
CYCLE = 5
WAIT = 2


def levels(count):
    bits = count.bit_length() - 1
    assert 1 << bits == count
    return bits


def folds(count):
    return count == 8


class Sum:
    def __init__(self, count, sources, dest, segments, scratch):
        self.count = count
        self.bits = levels(count)
        self.folds = folds(count)
        self.sources = sources
        self.dest = dest
        self.segments = segments
        self.got = scratch[: self.bits]
        self.ring, self.side_sum, self.line_sum = scratch[self.bits : self.bits + 3]
        self.sems, self.lsem = scratch[self.bits + 3 :]

    def slot(self, k):
        if not self.folds:
            return k
        odd = lax.rem(lax.rem(k, CYCLE), 2)
        return ((CYCLE + 1) // 2 - odd) * lax.div(k, CYCLE) + lax.div(lax.rem(k, CYCLE), 2)

    def where(self, k, level):
        place = lax.axis_index("seq")
        turn = 1 if self.folds else lax.div(lax.rem(k, 4), 3)
        start = 0
        for step in range(level + 1):
            stride = 1 << step
            if step < 2:
                stride = stride + turn * (3 - 2 * stride)
            bit = lax.rem(lax.div(place, stride), 2)
            if step == level:
                return bit, place + stride * (1 - 2 * bit), start
            start = start + bit * (self.count >> (step + 1))

    def own(self, k):
        bit, _, _ = self.where(k, 0)
        half = self.count >> 1
        return pltpu.make_async_copy(
            self.sources[0](k, bit * half, half), self.dest(k, bit * half, half), self.lsem.at[k]
        )

    def scatter(self, k, level, kind):
        bit, partner, start = self.where(k, level)
        half = self.count >> (level + 1)
        if level == 0:
            src = self.sources[kind](k, start + (1 - bit) * half, half)
        else:
            src = self.got[level - 1].at[self.slot(k), pl.ds((1 - bit) * half, half)]
        return to_seq(src, self.got[level].at[self.slot(k)], self.sems.at[0, level, k], self.sems.at[1, level, k], partner)

    def gather(self, k, level):
        bit, partner, start = self.where(k, level)
        half = self.count >> (level + 1)
        mine = start + bit * half
        ref = self.dest(k, mine, half)
        return to_seq(ref, ref, self.sems.at[2, level, k], self.sems.at[3, level, k], partner)

    def gathered(self, k, level):
        bit, partner, start = self.where(k, level)
        half = self.count >> (level + 1)
        ref = self.dest(k, start + (1 - bit) * half, half)
        return to_seq(ref, ref, self.sems.at[2, level, k], self.sems.at[3, level, k], partner)

    def begin(self, k, kind):
        self.scatter(k, 0, kind).start()
        if kind == 0:
            self.own(k).start()

    def add(self, k, kind, level):
        bit, _, start = self.where(k, level)
        half = self.count >> (level + 1)
        self.scatter(k, level, kind).wait_recv()
        if level == 0 and kind == 0:
            self.own(k).wait()
            mine = self.dest(k, bit * half, half)[...]
        elif level == 0:
            mine = self.sources[kind](k, bit * half, half)[...]
        else:
            mine = self.got[level - 1][self.slot(k), pl.ds(bit * half, half)]
        total = (self.got[level][self.slot(k)].astype(F32) + mine.astype(F32)).astype(BF16)
        if level + 1 < self.bits:
            self.got[level][self.slot(k)] = total
            self.scatter(k, level + 1, kind).start()
        else:
            self.dest(k, start + bit * half, half)[...] = total
            self.gather(k, level).start()

    def pass_on(self, k, kind, level):
        self.gathered(k, level).wait_recv()
        if level > 0:
            self.gather(k, level - 1).start()

    def spot(self):
        place = lax.axis_index("seq")
        side = lax.rem(place, 2)
        z = lax.div(place, 2)
        low = lax.rem(z, 2)
        end = low == lax.div(z, 2)
        return side, place + 1 - 2 * side, place + 2 * (1 - 2 * low), 2 * (3 - z) + side, end

    def half_of(self, k, which):
        half = self.count >> 1
        return self.dest(k, which * half, half)

    def fold_own(self, k):
        half = self.count >> 1
        return pltpu.make_async_copy(
            self.sources[0](k, self.spot()[0] * half, half), self.ring.at[lax.rem(k, 4)], self.lsem.at[k]
        )

    def fold_side(self, k, kind):
        side, twin, _, _, _ = self.spot()
        half = self.count >> 1
        src = self.sources[kind](k, (1 - side) * half, half)
        return to_seq(src, self.side_sum.at[self.slot(k)], self.sems.at[0, 0, k], self.sems.at[1, 0, k], twin)

    def fold_in(self, k):
        n = self.slot(k)
        return to_seq(
            self.side_sum.at[n], self.line_sum.at[n], self.sems.at[0, 1, k], self.sems.at[1, 1, k], self.spot()[2]
        )

    def fold_cross(self, k):
        side, _, _, other, _ = self.spot()
        return to_seq(
            self.line_sum.at[self.slot(k)], self.half_of(k, side), self.sems.at[0, 2, k], self.sems.at[1, 2, k], other
        )

    def fold_out(self, k):
        side, _, across, _, _ = self.spot()
        ref = self.half_of(k, side)
        return to_seq(ref, ref, self.sems.at[2, 1, k], self.sems.at[3, 1, k], across)

    def fold_back(self, k, mine):
        side, twin, _, _, _ = self.spot()
        ref = self.half_of(k, side if mine else 1 - side)
        return to_seq(ref, ref, self.sems.at[2, 0, k], self.sems.at[3, 0, k], twin)

    def fold_begin(self, k, kind):
        self.fold_side(k, kind).start()
        if kind == 0:
            self.fold_own(k).start()

    def fold_1(self, k, kind):
        side, _, _, _, end = self.spot()
        half = self.count >> 1
        n = self.slot(k)
        self.fold_side(k, kind).wait_recv()
        if kind == 0:
            self.fold_own(k).wait()
            mine = self.ring[lax.rem(k, 4)]
        else:
            mine = self.sources[kind](k, side * half, half)[...]
        self.side_sum[n] = (self.side_sum[n].astype(F32) + mine.astype(F32)).astype(BF16)

        @pl.when(end)
        def _():
            self.fold_in(k).start()

    def fold_2(self, k, kind):
        n = self.slot(k)

        @pl.when(jnp.logical_not(self.spot()[4]))
        def _():
            self.fold_in(k).wait_recv()
            self.line_sum[n] = (self.line_sum[n].astype(F32) + self.side_sum[n].astype(F32)).astype(BF16)
            self.fold_cross(k).start()

    def fold_3(self, k, kind):
        side, _, _, _, end = self.spot()

        @pl.when(jnp.logical_not(end))
        def _():
            self.fold_cross(k).wait_recv()
            ref = self.half_of(k, side)
            ref[...] = (ref[...].astype(F32) + self.line_sum[self.slot(k)].astype(F32)).astype(BF16)
            self.fold_out(k).start()
            self.fold_back(k, True).start()

    def fold_4(self, k, kind):
        end = self.spot()[4]

        @pl.when(end)
        def _():
            self.fold_out(k).wait_recv()
            self.fold_back(k, True).start()

        @pl.when(jnp.logical_not(end))
        def _():
            self.fold_back(k, False).wait_recv()

    def fold_5(self, k, kind):
        @pl.when(self.spot()[4])
        def _():
            self.fold_back(k, False).wait_recv()

    def at(self, i, stage, body, fold):
        for kind, (low, high, gap) in enumerate(self.segments):
            k = i - gap - LAGS[kind] * stage
            here = (k >= low) & (k < high)
            if not self.folds:

                @pl.when(here)
                def _(kind=kind, k=k):
                    body(k, kind)

                continue
            odd = lax.rem(lax.rem(jnp.maximum(k, 0), CYCLE), 2) == 1

            @pl.when(here & odd)
            def _(kind=kind, k=k):
                body(k, kind)

            if fold is not None:

                @pl.when(here & jnp.logical_not(odd))
                def _(kind=kind, k=k):
                    fold(k, kind)

    def step(self, i):
        stages = []
        for level in range(self.bits):
            stages.append(functools.partial(self.add, level=level))
        for level in range(self.bits - 1, -1, -1):
            stages.append(functools.partial(self.pass_on, level=level))
        folded = [self.fold_1, self.fold_2, self.fold_3, self.fold_4, self.fold_5]
        folded = folded + [None] * (len(stages) - len(folded))
        for s in range(len(stages) - 1, -1, -1):
            self.at(i, s + 1, stages[s], folded[s])
        self.at(i, 0, self.begin, self.fold_begin)

    def finish(self):
        def halving(k, kind):
            for level in range(self.bits):
                self.scatter(k, level, kind).wait_send()
                self.gather(k, level).wait_send()

        def folding(k, kind):
            end = self.spot()[4]
            self.fold_side(k, kind).wait_send()
            self.fold_back(k, True).wait_send()

            @pl.when(end)
            def _():
                self.fold_in(k).wait_send()

            @pl.when(jnp.logical_not(end))
            def _():
                self.fold_cross(k).wait_send()
                self.fold_out(k).wait_send()

        def one(kind, k, carry):
            if not self.folds:
                halving(k, kind)
                return carry
            odd = lax.rem(lax.rem(k, CYCLE), 2) == 1

            @pl.when(odd)
            def _():
                halving(k, kind)

            @pl.when(jnp.logical_not(odd))
            def _():
                folding(k, kind)

            return carry

        for kind, (low, high, _) in enumerate(self.segments):
            lax.fori_loop(low, high, functools.partial(one, kind), 0)

    @staticmethod
    def scratch(count, parts, first, unit):
        bits = levels(count)
        odd = parts
        even = 1
        half = 16
        if folds(count):
            odd = sum(1 for k in range(parts) if k % CYCLE % 2 == 1)
            even = parts - odd
            half = count // 2
        one = (1,) + unit if not folds(count) else (half,) + unit
        return [pltpu.VMEM((odd, count >> (level + 1)) + unit, BF16) for level in range(bits)] + [
            pltpu.VMEM((4 if folds(count) else 1,) + one, BF16),
            pltpu.VMEM((even,) + one, BF16),
            pltpu.VMEM((even,) + one, BF16),
            pltpu.SemaphoreType.DMA((4, bits, parts)),
            pltpu.SemaphoreType.DMA((first,)),
        ]


def plan(count, wide, tiles):
    second = tiles + 3 + WAIT
    a = wide // count
    b = a + 32 // count
    c = b + up_to(34 + wide % count, count) // count
    gap = max(0, second - a)
    late = max(gap, second + tiles - b, second + tiles + 3 - (c - 1))
    return (0, a, 0), (a, b, gap), (b, c, late)


def last_step(count, segments):
    latest = 0
    for kind, (low, high, gap) in enumerate(segments):
        for k in range(low, high):
            stages = 2 * levels(count) - (1 if folds(count) and k % CYCLE % 2 == 0 else 0)
            latest = max(latest, k + gap + stages * LAGS[kind])
    return latest


def finish_kernel(fg, fu, fd, first, second, tail, extra, gt_in, lo_in, dfg, dfu, dfd, dq, dk, dv, dg, dwo, dr, dup, dag, dffg, db, dgg, gt, lo):
    for src, dst in ((fg, dfg), (fu, dfu), (fd, dfd)):
        dst[...] = src[...].reshape(dst.shape).astype(F32)

    @pl.when(pl.program_id(0) == pl.num_programs(0) - 1)
    def _():
        tail_rows = extra.shape[0] * 16
        dfd[dfd.shape[0] - tail_rows :, :] = extra[...].reshape(tail_rows, -1).astype(F32)

    gt[...] = gt_in[...]
    lo[...] = lo_in[...]
    rows = first[...].reshape(-1, 512).astype(F32)
    dg[...] = rows[:, 0:256]
    dwo[...] = rows[:, 256:512].T
    rows = second[...].reshape(-1, 512).astype(F32)
    dq[...] = rows[:, 0:128]
    dk[...] = rows[:, 128:256]
    dv[...] = rows[:, 256:512]
    dr[...] = tail[0].astype(F32)
    last = tail[1].astype(F32)
    dup[...] = last[:, 0:128]
    dag[...] = last[0:1, 128:384]
    dffg[...] = last[1:2, 128:384]
    db[...] = last[3:4, 128:256]
    dgg[...] = last[2:3, 128:384]


def finish(units, gt, lo, hidden, wide, count):
    first = wide // count * count
    rest = wide % count
    width = units.shape[2]
    steps = 4
    per = hidden // 16 // steps
    assert per * steps * 16 == hidden and 0 < rest <= per
    rows = MODEL_WIDTH // steps
    wide_spec = lambda n: pl.BlockSpec((per, 16, width), lambda i: (i + n * steps, 0, 0))
    half_spec = lambda n: pl.BlockSpec(
        (pl.Element(rows // 16), pl.Element(16), pl.Element(512)),
        lambda i: (first + n + (i % 2) * (rows // 16), 0, (i // 2) * 512),
    )
    down = lambda r, c: ((r * steps, c), pl.BlockSpec((r, c), lambda i: (i, 0)))
    full = lambda r, c: ((r, c), pl.BlockSpec((r, c), lambda i: (0, 0)))
    outs = [
        down(per * 16, width), down(per * 16, width), down(per * 16, width),
        down(rows, 128), down(rows, 128), down(rows, 256), down(rows, 256),
        ((256, MODEL_WIDTH), pl.BlockSpec((256, rows), lambda i: (0, i))),
        full(RANK, MODEL_WIDTH), full(RANK, 128), full(1, 256), full(1, 256), full(1, 128), full(1, 256),
    ]
    same = pl.BlockSpec((gt.shape[0] // steps, gt.shape[1]), lambda i: (i, 0))
    return pl.pallas_call(
        finish_kernel,
        grid=(steps,),
        out_shape=[jax.ShapeDtypeStruct(s, F32) for s, _ in outs]
        + [jax.ShapeDtypeStruct(gt.shape, F32), jax.ShapeDtypeStruct(lo.shape, BF16)],
        in_specs=[
            wide_spec(0), wide_spec(1), wide_spec(2),
            half_spec(0), half_spec(32),
            pl.BlockSpec((pl.Element(2), pl.Element(16), pl.Element(width)), lambda i: (first + 64, 0, 0)),
            pl.BlockSpec((pl.Element(rest), pl.Element(16), pl.Element(width)), lambda i: (first + 66, 0, 0)),
            same, same,
        ],
        out_specs=[s for _, s in outs] + [same, same],
        compiler_params=pltpu.CompilerParams(
            vmem_limit_bytes=VMEM_LIMIT, dimension_semantics=("arbitrary",)
        ),
        name="finish",
    )(units, units, units, units, units, units, units, gt, lo)


def back_kernel(
    tiles, count, segments,
    keep_ref, d_ref, stat_ref, gg_ref, again, fgain, wout, wq, wk, wv, wg, wr, rup,
    wide_in, gsend, psend, x_ref, c_ref, gx, gown, h1, invf, f1, gz_ref, oo_ref, gated, ws1, b1, e1,
    na1, f2, b2, ws2, e2, na, h2, pown, inva,
    gt_o, lo_o, units_o,
    tri, rg, gh, gb, gzs, gw, gqd, gkd, gv, state, sbuf, tbuf, hbuf, xbuf, ybuf, rbuf,
    gcat, mn, sc, rc, own, st_s, st_r, both, joint, small, held, wide_o, few, lot,
    gsem, psem, hsem, nsem, csem, tsem, esend, erecv, xsem, wsem, jsem, *rest,
):
    i = pl.program_id(0)
    me, mate, cross, far = peers()
    place = lax.axis_index("seq")
    last = tiles - 1
    second = tiles + 3 + WAIT

    some = tiles - 3

    def rows_of(t):
        return pl.ds(pl.multiple_of(t * TILE, TILE), TILE)

    def own_cols(ref):
        return ref[:, pl.ds(pl.multiple_of(me * BLOCK, BLOCK), BLOCK)].astype(F32)

    def grads(t):
        return to_head(gsend.at[rows_of(t)], rg.at[t], gsem.at[0, t], gsem.at[1, t], cross)

    def feeds(t):
        return to_head(psend.at[rows_of(t)], rg.at[t], psem.at[0, t], psem.at[1, t], cross)

    def own_mate(t):
        return to_head(gb.at[t, me], gb.at[t, me], hsem.at[0, t], hsem.at[1, t], mate)

    def own_cross(t):
        return to_head(gb.at[t, me], gb.at[t, me], hsem.at[2, t], hsem.at[3, t], cross)

    def onward(t):
        return to_head(gb.at[t, cross], gb.at[t, cross], hsem.at[4, t], hsem.at[5, t], mate)

    def pair(t, which):
        block = mate if which == 0 else far
        return to_head(gb.at[t, block], mn.at[t, which], nsem.at[2 * which, t], nsem.at[2 * which + 1, t], mate)

    def over(t):
        return to_head(sc.at[t], rc.at[t], csem.at[0, t], csem.at[1, t], cross)

    def stats(t, n, other):
        return to_head(st_s.at[t], st_r.at[t, n], tsem.at[0, n, t], tsem.at[1, n, t], other)

    first = wide_in.shape[0] // count
    spare = wide_in.shape[0] - first * count
    parts = wide_o.shape[0] // count
    ready = second + tiles
    feed = ready + 4

    def early(k, start, n):
        return wide_in.at[pl.ds(k * count + start, n)]

    def middle(k, start, n):
        return few.at[pl.ds((k - segments[1][0]) * count + start, n)]

    def late(k, start, n):
        return lot.at[pl.ds((k - segments[2][0]) * count + start, n)]

    def place_of(k, start, n):
        return wide_o.at[pl.ds(k * count + start, n)]

    wide_sum = Sum(count, (early, middle, late), place_of, segments, rest)

    @pl.when(i == 0)
    def _():
        greet_head()
        greet_seq(count)
        pl.semaphore_wait(pltpu.get_barrier_semaphore(), 3 + count - 1)
        for n in range(tiles - some):
            grads(last - n).start()
        r = lax.broadcasted_iota(jnp.int32, (TILE, TILE), 0)
        c = lax.broadcasted_iota(jnp.int32, (TILE, TILE), 1)
        tri[...] = jnp.where(((r >> 6) == (c >> 6)) & (r > c), 1.0, 0.0).astype(BF16)
        state[...] = jnp.zeros_like(state)
        both[...] = jnp.zeros_like(both)
        joint[...] = jnp.zeros_like(joint)
        small[...] = jnp.zeros_like(small)

    def share(n, other):
        return to_head(joint, held.at[me], jsem.at[0, n], jsem.at[1, n], other)

    spare_copy = pltpu.make_async_copy(
        wide_in.at[pl.ds(first * count, spare)], lot.at[pl.ds(34, spare)], wsem.at[2]
    )

    def lay(dst, col):
        def copy(r, carry):
            for side in range(2):
                rows = pl.ds(pl.multiple_of(side * (MODEL_WIDTH // 2) + r * 16, 16), 16)
                dst[r, :, side * 512 : (side + 1) * 512] = both[rows, col : col + 512].astype(BF16)
            return carry

        lax.fori_loop(0, 32, copy, 0)

    @pl.when(i == second)
    def _():
        lay(few, 512)

    @pl.when(i == ready)
    def _():
        held[me] = joint[...]
        for n, other in enumerate((mate, cross, far)):
            share(n, other).start()
        lay(lot, 0)
        lot[32:] = jnp.zeros((lot.shape[0] - 32,) + lot.shape[1:], BF16)
        spare_copy.start()

    @pl.when(i == ready + 3)
    def _():
        spare_copy.wait()
        for n, other in enumerate((mate, cross, far)):
            to_head(joint, held.at[other], jsem.at[0, n], jsem.at[1, n], other).wait()
        base = 32
        sums = (held[0] + held[1]) + (held[2] + held[3])
        lot[base] = sums[0:RANK].astype(BF16)
        lot[base + 1] = jnp.zeros((16, MODEL_WIDTH), BF16)
        small[2:3, 128:384] = sums[16:17, 0:256]
        lot[base + 1, :, 0:512] = small[...].astype(BF16)

    wide_sum.step(i)

    @pl.when(i == 1)
    def _():
        def weave(r, carry):
            rows = pl.ds(pl.multiple_of(r * 16, 16), 16)
            lot[r, :, 0:128] = wq[rows, :]
            lot[r, :, 128:256] = wk[rows, :]
            lot[r, :, 256:512] = wv[rows, :]
            lot[r, :, 512:768] = wg[rows, :]
            return carry

        lax.fori_loop(0, MODEL_WIDTH // 16, weave, 0)

    @pl.when((i >= 2) & (i - 2 <= last))
    def _():
        t = last - (i - 2)
        own_cross(t).wait_recv()
        onward(t).start()

    @pl.when(i <= last)
    def _():
        t = last - i

        @pl.when(t >= some)
        def _():
            grads(t).wait_recv()

        @pl.when(t < some)
        def _():
            rg[t] = gx[...]

        gnf = gown[...] + rg[t].astype(F32)
        inv = invf[...][:, 0:1]
        hn = h1[...].astype(BF16).astype(F32) * inv
        row = stat_ref[pl.ds(t, 1), :]
        stat = jnp.broadcast_to(row, (128, TILE)).T[:, 0:1]
        grad = c_ref[...].astype(F32) + inv * (own_cols(fgain) * gnf - hn * (stat / MODEL_WIDTH))
        small[1:2, 128:384] += jnp.sum(gnf * hn, axis=0, keepdims=True)
        gh[t] = grad
        gb[t, me] = grad.astype(BF16)
        own_cross(t).start()
        own_mate(t).start()

    half = tiles // 2

    def some_feeds(low, high, at):
        @pl.when((i >= at) & (low + 2 * (i - at) < high))
        def _():
            n = low + 2 * (i - at)
            feeds(last - n).start()

            @pl.when(n + 1 < high)
            def _():
                feeds(last - n - 1).start()

    some_feeds(0, half, last + 2)
    some_feeds(half, tiles, ready)

    @pl.when((i >= 3) & (i - 3 <= last))
    def _():
        t = last - (i - 3)
        own_mate(t).wait_recv()
        onward(t).wait_recv()
        gt = jnp.zeros((TILE, BLOCK), F32)
        for j in range(4):
            cols = slice(j * BLOCK, (j + 1) * BLOCK)
            gt = gt + dot_nt(gb[t, j], wout[:, cols])
            both[cols, 768:1024] += dot_tn(gb[t, j], gated[...])
        o = oo_ref[...]
        gz = gz_ref[...]
        inv = lax.rsqrt(jnp.mean(o * o, axis=1, keepdims=True) + EPS)
        on = o * inv
        sig = jax.nn.sigmoid(gz)
        gn = gt * (gz * sig)
        joint[16:17, 0:256] += jnp.sum(gn * on, axis=0, keepdims=True)
        gain = gg_ref[...].astype(F32)
        ggz = (gt * on * gain * (sig * (1.0 + gz * (1.0 - sig)))).astype(BF16)
        gzs[t] = ggz
        both[:, 512:768] += dot_tn(na1[...], ggz)
        p = gn * gain
        go = (inv * (p - on * jnp.mean(p * on, axis=1, keepdims=True))).astype(BF16)
        qd = f1[:, 0:128].astype(BF16)
        kd = f1[:, 128:256].astype(BF16)
        v = b1[:, 0:256]
        causal, _ = span_masks(TILE, TILE)
        ga = jnp.where(causal, dot_nt(go, v), 0.0).astype(BF16)
        gqd[t] = dot_nn(ga, kd)
        gkd[t] = dot_tn(ga, qd)
        gv[t] = dot_tn(b1[:, 256:512], go)
        for c in range(PER - 1, -1, -1):
            rows = slice(c * SPAN, (c + 1) * SPAN)
            gqd[t, rows, :] += dot_nn(go[rows], ws1[c])
            fresh = dot_tn(go[rows], qd[rows])
            gw[t * PER + c] = fresh
            through = keep_ref[t, c : c + 1, :] * e1[0, c : c + 1, :]
            state[...] = through * (fresh + state[...])

    length = count // 2
    side = lax.rem(place, 2)
    line = lax.div(place, 2)
    twin = place + 1 - 2 * side
    half_rows = HV // 2
    mine = pl.ds(pl.multiple_of(side * half_rows, half_rows), half_rows)
    other = pl.ds(pl.multiple_of((1 - side) * half_rows, half_rows), half_rows)

    def to_twin():
        return to_seq(sbuf, tbuf, xsem.at[0], xsem.at[1], twin)

    def to_twin_half():
        return to_seq(xbuf, ybuf, xsem.at[2], xsem.at[3], twin)

    def to_line(p):
        return to_seq(hbuf, rbuf.at[line], esend.at[p], erecv.at[line], 2 * p + side)

    def from_line(p):
        return to_seq(hbuf, rbuf.at[p], esend.at[p], erecv.at[p], 2 * p + side)

    def two_terms(d):
        hi = d.astype(BF16).astype(F32)
        first_rows = lax.broadcasted_iota(jnp.int32, (16, HK), 0) < 8
        hi = jnp.broadcast_to(hi, (16, HK))
        return jnp.where(first_rows, hi, jnp.broadcast_to(d, (16, HK)) - hi).astype(BF16)

    def decay_of(rows):
        rows = rows.astype(F32)
        return rows[0:1] + rows[8:9]

    @pl.when(i == last + 3)
    def _():
        sbuf[0:HV, :] = state[...].astype(BF16)
        sbuf[HV : HV + 16, :] = two_terms(d_ref[0:1, :])
        to_twin().start()

    @pl.when(i == last + 4)
    def _():
        to_twin().wait_recv()
        d_mine = decay_of(sbuf[HV : HV + 16, :])
        d_twin = decay_of(tbuf[HV : HV + 16, :])
        s_mine = sbuf[mine, :].astype(F32)
        s_twin = tbuf[mine, :].astype(F32)

        @pl.when(side == 0)
        def _():
            hbuf[0:half_rows, :] = (s_mine + d_mine * s_twin).astype(BF16)

        @pl.when(side == 1)
        def _():
            hbuf[0:half_rows, :] = (s_twin + d_twin * s_mine).astype(BF16)

        hbuf[half_rows : half_rows + 16, :] = two_terms(d_mine * d_twin)

        def send(p, carry):
            to_line(p).start()
            return carry

        lax.fori_loop(0, line, send, 0)

    @pl.when(i == last + 5)
    def _():
        state[mine, :] = jnp.zeros((half_rows, HK), F32)

        def join(n, carry):
            p = length - 1 - n
            from_line(p).wait_recv()
            d = decay_of(rbuf[p, half_rows : half_rows + 16, :])
            state[mine, :] = rbuf[p, 0:half_rows, :].astype(F32) + d * state[mine, :]
            return carry

        lax.fori_loop(0, length - 1 - line, join, 0)
        xbuf[...] = state[mine, :].astype(BF16)
        to_twin_half().start()

    @pl.when(i == second)
    def _():
        def free(t, carry):
            own_cross(t).wait_send()
            own_mate(t).wait_send()
            onward(t).wait_send()
            return carry

        lax.fori_loop(0, tiles, free, 0)
        to_twin_half().wait_recv()
        state[other, :] = ybuf[...].astype(F32)

        @pl.when(side == 0)
        def _():
            state[...] = tbuf[0:HV, :].astype(F32) + decay_of(tbuf[HV : HV + 16, :]) * state[...]

    @pl.when((i >= second + 3) & (i - second - 3 <= last))
    def _():
        t = last - (i - second - 3)
        over(t).wait_recv()
        for n, other in enumerate((mate, cross, far)):
            stats(t, n, other).wait_recv()
        gna = own[lax.rem(t, 3)] + rc[t].astype(F32)
        inv = inva[...][:, 0:1]
        xn = x_ref[...].astype(F32) * inv
        row = (st_s[t] + st_r[t, 0]) + (st_r[t, 1] + st_r[t, 2])
        stat = jnp.broadcast_to(row[0:1], (128, TILE)).T[:, 0:1]
        gt_o[...] = gh[t] + inv * (own_cols(again) * gna - xn * (stat / MODEL_WIDTH))
        small[0:1, 128:384] += jnp.sum(gna * xn, axis=0, keepdims=True)

    @pl.when((i >= second + 1) & (i - second - 1 <= last))
    def _():
        t = last - (i - second - 1)
        pair(t, 0).wait_recv()
        pair(t, 1).wait_recv()
        sc[t] = (gb[t, cross].astype(F32) + mn[t, 1].astype(F32)).astype(BF16)
        over(t).start()
        own[lax.rem(t, 3)] = gb[t, me].astype(F32) + mn[t, 0].astype(F32)

    @pl.when((i >= second) & (i - second <= last))
    def _():
        t = last - (i - second)
        qf = f2[:, 0:128]
        kf = f2[:, 128:256]
        kd = kf.astype(BF16)
        pieces = [None] * PER
        for c in range(PER - 1, -1, -1):
            rows = slice(c * SPAN, (c + 1) * SPAN)
            low = state[...].astype(BF16)
            gkd[t, rows, :] += dot_nn(b2[rows, 0:256], low)
            gv[t, rows, :] += dot_nt(kd[rows], low)
            ge = gw[t * PER + c] + state[...]
            pieces[c] = jnp.broadcast_to(jnp.sum(ge * ws2[c].astype(F32), axis=0, keepdims=True), (SPAN, HK))
            state[...] = (keep_ref[t, c : c + 1, :] * e2[0, c : c + 1, :]) * ge
        gq = gqd[t]
        gk = gkd[t]
        diff = gq * qf - gk * kf
        gg = jnp.concatenate(pieces, axis=0) - fold(dot_nn(tri[...], three(diff)))
        glogit = gg * f2[:, 512:640]
        small[3:4, 128:256] += jnp.sum(glogit, axis=0, keepdims=True)
        hi = glogit.astype(BF16)
        lo = (glogit - hi.astype(F32)).astype(BF16)
        glr = dot_nt(hi, rup[...]) + dot_nt(lo, rup[...])
        lr = b2[:, 512 : 512 + RANK]
        small[:, 0:128] += dot_tn(lr, hi) + dot_tn(lr, lo)
        glr = glr.astype(BF16)
        joint[0:RANK, :] += dot_tn(glr, na[...])
        gcat[:, 0:128] = (gq * f2[:, 256:384]).astype(BF16)
        gcat[:, 128:256] = (gk * f2[:, 384:512]).astype(BF16)
        gcat[:, 256:512] = gv[t].astype(BF16)
        gcat[:, 512:768] = gzs[t]
        g = gcat[...]
        stat = jnp.zeros((TILE, 1), F32)
        for j in range(4):
            cols = slice(j * BLOCK, (j + 1) * BLOCK)
            gj = dot_nt(g, lot[16 * j : 16 * (j + 1), :, 0:768].reshape(BLOCK, 768)) + dot_nn(glr, wr[:, cols])
            stat = stat + jnp.sum(gj * na[:, cols].astype(F32), axis=1, keepdims=True)
            gb[t, j] = gj.astype(BF16)
        pair(t, 1).start()
        pair(t, 0).start()
        st_s[t] = jnp.broadcast_to(stat, (TILE, 128)).T[0:8, :]
        for n, other in enumerate((mate, cross, far)):
            stats(t, n, other).start()
        both[:, 0:512] += dot_tn(na[...], g[:, 0:512])

    @pl.when((i >= feed) & (i - feed <= last))
    def _():
        t = last - (i - feed)
        feeds(t).wait_recv()
        lo_o[...] = (h2[...] + (pown[...] + rg[t].astype(F32))).astype(BF16)

    drained = first + 2 * levels(count) * LAGS[0]
    head_units = pl.ds(0, first * count)
    tail_units = pl.ds(first * count, (parts - first) * count)
    head_copy = pltpu.make_async_copy(wide_o.at[head_units], units_o.at[head_units], wsem.at[0])
    tail_copy = pltpu.make_async_copy(wide_o.at[tail_units], units_o.at[tail_units], wsem.at[1])

    @pl.when(i == drained)
    def _():
        head_copy.start()

    @pl.when(i == pl.num_programs(0) - 1)
    def _():
        tail_copy.start()
        wide_sum.finish()
        tail_copy.wait()
        head_copy.wait()

        to_twin().wait_send()
        to_twin_half().wait_send()

        def sent(p, carry):
            to_line(p).wait_send()
            return carry

        lax.fori_loop(0, line, sent, 0)

        def out(t, carry):
            @pl.when(t >= some)
            def _():
                grads(t).wait_send()

            feeds(t).wait_send()
            pair(t, 0).wait_send()
            pair(t, 1).wait_send()
            over(t).wait_send()
            for n, other in enumerate((mate, cross, far)):
                stats(t, n, other).wait_send()
            return carry

        lax.fori_loop(0, tiles, out, 0)


def back(fixed, wide, gsend, psend, x, cot, gx, gown, h, invf, f, o, oo, gated, ws, b, e, na, pown, inva):
    rows = h.shape[0]
    tiles = rows // TILE
    count = lax.axis_size("seq")
    second = tiles + 3 + WAIT
    width = MODEL_WIDTH
    segments = plan(count, wide.shape[0], tiles)
    first = segments[0][1]
    parts = segments[2][1]
    units = parts * count
    feed = second + tiles + 4
    steps = max(feed + tiles, last_step(count, segments) + 1)
    ts = functools.partial(tile_spec, tiles, back=True)
    outs = [
        ((rows, BLOCK), F32, ts((TILE, BLOCK), second + 3)),
        ((rows, BLOCK), BF16, ts((TILE, BLOCK), feed)),
        ((units, 16, width), BF16, pl.BlockSpec(memory_space=pl.ANY)),
    ]
    tiled = lambda n: pltpu.VMEM((tiles, n, TILE, BLOCK), BF16)
    flat = lambda n, d: pltpu.VMEM((tiles, TILE, n), d)
    return pl.pallas_call(
        functools.partial(back_kernel, tiles, count, segments),
        grid=(steps,),
        out_shape=[jax.ShapeDtypeStruct(s, d) for s, d, _ in outs],
        in_specs=[whole(a.shape) for a in fixed]
        + [
            pl.BlockSpec(memory_space=pl.ANY), pl.BlockSpec(memory_space=pl.ANY), pl.BlockSpec(memory_space=pl.ANY),
            ts((TILE, BLOCK), second + 3), ts((TILE, BLOCK), 0),
            pl.BlockSpec((TILE, BLOCK), lambda i: (jnp.clip(tiles - 1 - i, 0, tiles - 4), 0)),
            ts((TILE, BLOCK), 0), ts((TILE, BLOCK), 0), ts((TILE, 128), 0),
            ts((TILE, 256), 3), ts((TILE, 256), 3), ts((TILE, 256), 3), ts((TILE, 256), 3),
            ts((PER, HV, HK), 3), ts((TILE, 640), 3), ts((1, 8, 128), 3), ts((TILE, width), 3),
            ts((TILE, 640), second), ts((TILE, 640), second), ts((PER, HV, HK), second), ts((1, 8, 128), second),
            ts((TILE, width), second), ts((TILE, BLOCK), feed), ts((TILE, BLOCK), feed),
            ts((TILE, 128), second + 3),
        ],
        out_specs=[s for _, _, s in outs],
        scratch_shapes=[
            pltpu.VMEM((TILE, TILE), BF16),
            flat(BLOCK, BF16), flat(BLOCK, F32),
            tiled(4),
            flat(BLOCK, BF16),
            pltpu.VMEM((rows // SPAN, HV, HK), F32),
            flat(HK, F32), flat(HK, F32), flat(HV, F32),
            pltpu.VMEM((HV, HK), F32),
            pltpu.VMEM((HV + 16, HK), BF16),
            pltpu.VMEM((HV + 16, HK), BF16),
            pltpu.VMEM((HV // 2 + 16, HK), BF16),
            pltpu.VMEM((HV // 2, HK), BF16),
            pltpu.VMEM((HV // 2, HK), BF16),
            pltpu.VMEM((count // 2, HV // 2 + 16, HK), BF16),
            pltpu.VMEM((TILE, 768), BF16),
            tiled(2), flat(BLOCK, BF16), flat(BLOCK, BF16),
            pltpu.VMEM((3, TILE, BLOCK), F32),
            pltpu.VMEM((tiles, 8, TILE), F32),
            pltpu.VMEM((tiles, 3, 8, TILE), F32),
            pltpu.VMEM((width, width), F32),
            pltpu.VMEM((24, width), F32),
            pltpu.VMEM((16, 512), F32),
            pltpu.VMEM((4, 24, width), F32),
            pltpu.VMEM((units, 16, width), BF16),
            pltpu.VMEM((32, 16, width), BF16),
            pltpu.VMEM((max(width // 16, (parts - segments[2][0]) * count), 16, width), BF16),
            pltpu.SemaphoreType.DMA((2, tiles)),
            pltpu.SemaphoreType.DMA((2, tiles)),
            pltpu.SemaphoreType.DMA((6, tiles)),
            pltpu.SemaphoreType.DMA((4, tiles)),
            pltpu.SemaphoreType.DMA((2, tiles)),
            pltpu.SemaphoreType.DMA((2, 3, tiles)),
            pltpu.SemaphoreType.DMA((count // 2,)),
            pltpu.SemaphoreType.DMA((count // 2,)),
            pltpu.SemaphoreType.DMA((4,)),
            pltpu.SemaphoreType.DMA((3,)),
            pltpu.SemaphoreType.DMA((2, 3)),
        ]
        + Sum.scratch(count, parts, first, wide.shape[1:]),
        compiler_params=pltpu.CompilerParams(
            collective_id=3, has_side_effects=True, vmem_limit_bytes=VMEM_LIMIT,
            dimension_semantics=("arbitrary",),
        ),
        name="back",
    )(*fixed, wide, gsend, psend, x, cot, gx, gown, h, invf, f, o, oo, gated, ws, b, e, na, f, b, ws, e, na, h, pown, inva)


def shards(
    tokens,
    row_starts,
    attn_gain,
    query_weight,
    key_weight,
    value_weight,
    gate_weight,
    rank_down,
    rank_up,
    rank_bias,
    group_gain,
    out_weight,
    feed_gain,
    feed_gate,
    feed_up,
    feed_down,
    cotangent,
):
    rows = tokens.shape[0]
    tiles = rows // TILE
    spans = rows // SPAN
    shape = (tiles, 8, 128)
    span = lax.axis_index("seq") * spans + PER * lax.broadcasted_iota(jnp.int32, shape, 0)
    span = span + lax.broadcasted_iota(jnp.int32, shape, 1)
    hits = (row_starts // SPAN)[:, None, None, None] == span[None]
    keep = 1.0 - jnp.any(hits, axis=0).astype(F32)
    weights = (
        query_weight[0], key_weight[0], value_weight[0], gate_weight[0], jnp.swapaxes(rank_down[0], 0, 1), rank_up[0]
    )
    na, cg, inva, f, b, o, u, e, inc, dec = front(tokens, cotangent, keep, attn_gain, *weights, rank_bias)
    gated, oo, ws, h, invf, gsend, gown, psend, pown, stat, wide, gx = ffn(
        tokens, keep, inc, group_gain, feed_gain, out_weight[0], jnp.swapaxes(feed_gate[0], 0, 1),
        jnp.swapaxes(feed_up[0], 0, 1), feed_down[0], f, o, u, e, cg,
    )
    fixed = (
        keep, dec, stat, group_gain, attn_gain, feed_gain, out_weight[0],
    ) + weights
    grad_tokens, layer_out, units = back(fixed, wide, gsend, psend, tokens, cotangent, gx, gown, h, invf, f, o, oo, gated, ws, b, e, na, pown, inva)
    dfg, dfu, dfd, dq, dk, dv, dg, dwo, dr, dup, dag, dffg, db, dgg, grad_tokens, layer_out = finish(
        units, grad_tokens, layer_out, feed_gate.shape[2], wide.shape[0], lax.axis_size("seq")
    )
    dfg, dfu, dr = (jnp.swapaxes(a, 0, 1) for a in (dfg, dfu, dr))
    grads = (dag, dq[None], dk[None], dv[None], dg[None], dr[None], dup[None], db, dgg, dwo[None], dffg, dfg[None], dfu[None], dfd[None])
    return (layer_out, grad_tokens) + grads


def solution(mesh):
    placed = (
        P("seq", "head"),
        P(),
        P(),
        P(None, None, "head"),
        P(None, None, "head"),
        P(None, None, "head"),
        P(None, None, "head"),
        P(),
        P(None, None, "head"),
        P(None, "head"),
        P(),
        P(None, "head", None),
        P(),
        P(None, None, "head"),
        P(None, None, "head"),
        P(None, "head", None),
        P("seq", "head"),
    )
    return jax.shard_map(
        shards,
        mesh=mesh,
        in_specs=placed,
        out_specs=(
            P("seq", "head"),
            P("seq", "head"),
            P(None, "head"),
            P(None, None, "head"),
            P(None, None, "head"),
            P(None, None, "head"),
            P(None, None, "head"),
            P(),
            P(None, None, "head"),
            P(None, "head"),
            P(),
            P(None, "head", None),
            P(None, "head"),
            P(None, None, "head"),
            P(None, None, "head"),
            P(None, "head", None),
        ),
        check_vma=False,
    )
```
